32 devices in a mesh: group: 4 (over x, core), shard: 8 (over z, y).
Axes of the slice: x: 2, y: 2, z: 4, core: 2. Of those that a mesh axis runs over, the one named last changes fastest.
Arguments:
- data: float32 [2, 32768], P(None, ('group', 'shard')), as said below
- inv_noise: bfloat16 [32768], P(('group', 'shard')), may hold values from 0.5 to 2
- mbh_amp: float32 [128, 6, 3, 32], P('shard', None, None, 'group'), may hold values from -0.15 to 0.15
- mbh_phase: float32 [128, 6, 3, 32], P('shard', None, None, 'group'), may hold values from -1024 to 1024
- bin_amp: float32 [32, 512], P(('group', 'shard')), may hold values from 0.15 to 0.4
- bin_phase: float32 [32, 512], P(('group', 'shard')), may hold values from -3.140625 to 3.140625
- bin_slope: float32 [32, 512], P(('group', 'shard')), may hold values from -3 to 3
- bin_curve: float32 [32, 512], P(('group', 'shard')), may hold values from -0.01 to 0.01
- bin_start: int32 [32, 512], P(('group', 'shard')), may hold values from 0 to 1023, as said below
- bin_count: int32 [32], P(('group', 'shard')), may hold values from 64 to 512, as said below
Outputs:
- accept_prob: float32 [64, 16384], P(None, ('group', 'shard'))
- residual_new: float32 [64, 2, 32768], P(None, None, ('group', 'shard'))
- noise_fit: float32 [32], P(('group', 'shard'))
The draws below stay inside these ranges and needn't reach their ends.
Inputs may be any that keep to these rules, and one draw needn't show every extreme that they name: data has a scale that varies from bin to bin and shrinks from the first band to the last. Slots p < bin_count[n] of band n are live, the others are empty; each band's count is 512, 256, 128 or 64, and some band holds 512. `bin_start`: in the last band every start is at most 896, so that no waveform passes the last bin; in every other band slot 0 starts from 960 to 992, so that its waveform passes into the next band.
All inputs are finite; a program needn't handle non-finite values.
Results may differ from the reference program's by a relative error of at most 0.0025.
The reference program's roundings to bfloat16 on the way count: a program that leaves them out, or rounds other values in their place, can miss the bound.
Values may be sent and summed in bfloat16 or wider, within the bound.
No kernel may reach another device: no remote copies, remote signals or barrier semaphores. Data moves between devices by JAX's collectives and lax.ppermute only.
A program may use at most 64 MiB of HBM per device.

```python
import math
import jax
import jax.numpy as jnp
from jax import lax

BB = 1024
P_SIZE = 512
W = 64
H = 12
Q = 128
NCOEF = 8
NBANDS = 32
NBIN = 32768


def draw_data(key, part):
    key_scale, key_noise = jax.random.split(jax.random.fold_in(key, 11))
    band_of_bin = jnp.arange(NBIN, dtype=jnp.int32) // BB
    position = (2 * band_of_bin + 1).astype(jnp.float32) / NBANDS - 1.0
    trend = jnp.exp(-0.6 * position)
    scale = jnp.exp(jax.random.uniform(key_scale, (NBIN,), jnp.float32, jnp.log(0.3), jnp.log(3.0)))
    values = jax.random.normal(key_noise, (2, NBIN), jnp.float32)
    return values * (trend * scale)[None, :]


def draw_bin_start(key, part):
    key_main, key_top, key_band, key_slot, key_edge = jax.random.split(jax.random.fold_in(key, 23), 5)
    starts = jax.random.randint(key_main, (NBANDS, P_SIZE), 0, BB)
    edge_starts = jax.random.randint(key_edge, (NBANDS,), BB - Q // 2, BB - Q // 4 + 1)
    starts = starts.at[:, 0].set(edge_starts)
    last_row = jax.random.randint(key_top, (P_SIZE,), 0, BB - Q + 1)
    starts = starts.at[NBANDS - 1].set(last_row)
    chosen_band = jax.random.randint(key_band, (), 0, NBANDS - 1)
    chosen_slot = jax.random.randint(key_slot, (), 1, P_SIZE)
    return starts.at[chosen_band, chosen_slot].set(BB - 1).astype(jnp.int32)


def draw_bin_count(key, part):
    key_level, key_full = jax.random.split(jax.random.fold_in(key, 37))
    levels = jax.random.randint(key_level, (NBANDS,), 0, 4)
    counts = P_SIZE // jnp.left_shift(jnp.ones_like(levels), levels)
    chosen_band = jax.random.randint(key_full, (), 0, NBANDS)
    return counts.at[chosen_band].set(P_SIZE).astype(jnp.int32)


def shard_levels(rng, dims, shards, low, high):
    level, own = 1.0, jax.random.fold_in(rng, 6)
    for dim, parts in shards:
        draws = jnp.exp(jax.random.uniform(jax.random.fold_in(own, dim), (parts,), jnp.float32, low / len(shards), high / len(shards)))
        level = level * jnp.repeat(draws, dims[dim] // parts).reshape([-1 if axis == dim else 1 for axis in range(len(dims))])
    return level


def setup_inputs(seed: int = 0) -> dict:
    key_of = jax.random.split(jax.random.key(seed), 11)
    data = draw_data(jax.random.fold_in(key_of[10], 71), 0)
    inv_noise = jnp.clip(jnp.exp(math.log(2.0) - 1.3862944 * jax.random.uniform(key_of[1], (NBIN,), jnp.float32) ** shard_levels(key_of[1], (NBIN,), ((0, 32),), -0.2, 0.2)), 0.5, 2.0).astype(jnp.bfloat16)
    mbh_amp = jnp.clip(jax.random.uniform(key_of[2], (2 * W, H // 2, 3, NBANDS), jnp.float32, -0.15, 0.15) * shard_levels(key_of[2], (2 * W, H // 2, 3, NBANDS), ((0, 8), (3, 4)), -0.4, 0.0), -0.15, 0.15)
    mbh_phase = jnp.clip(jax.random.uniform(key_of[3], (2 * W, H // 2, 3, NBANDS), jnp.float32, -1024.0, 1024.0) * shard_levels(key_of[3], (2 * W, H // 2, 3, NBANDS), ((0, 8), (3, 4)), -0.4, 0.0), -1024.0, 1024.0)
    bin_amp = jnp.clip(jnp.exp(math.log(0.4) - 0.98082923 * jax.random.uniform(key_of[4], (NBANDS, P_SIZE), jnp.float32) ** shard_levels(key_of[4], (NBANDS, P_SIZE), ((0, 32),), -0.2, 0.2)), 0.15, 0.4)
    bin_phase = jnp.clip(jax.random.uniform(key_of[5], (NBANDS, P_SIZE), jnp.float32, -3.140625, 3.140625), -3.140625, 3.140625)
    bin_slope = jnp.clip(jax.random.uniform(key_of[6], (NBANDS, P_SIZE), jnp.float32, -3.0, 3.0) * shard_levels(key_of[6], (NBANDS, P_SIZE), ((0, 32),), -0.4, 0.0), -3.0, 3.0)
    bin_curve = jnp.clip(jax.random.uniform(key_of[7], (NBANDS, P_SIZE), jnp.float32, -0.01, 0.01) * shard_levels(key_of[7], (NBANDS, P_SIZE), ((0, 32),), -0.4, 0.0), -0.01, 0.01)
    bin_start = draw_bin_start(jax.random.fold_in(key_of[10], 71), 0)
    bin_count = draw_bin_count(jax.random.fold_in(key_of[10], 71), 0)
    return {"data": data, "inv_noise": inv_noise, "mbh_amp": mbh_amp, "mbh_phase": mbh_phase, "bin_amp": bin_amp, "bin_phase": bin_phase, "bin_slope": bin_slope, "bin_curve": bin_curve, "bin_start": bin_start, "bin_count": bin_count}


def half_templates(coef_amp, coef_phase, band_bins):
    fraction = jnp.arange(band_bins, dtype=jnp.float32) / band_bins
    amp_curve = coef_amp[:, :, 0, :, None] + coef_amp[:, :, 1, :, None] * fraction + coef_amp[:, :, 2, :, None] * fraction * fraction
    phase_curve = coef_phase[:, :, 0, :, None] + coef_phase[:, :, 1, :, None] * fraction + coef_phase[:, :, 2, :, None] * fraction * fraction
    real_part = jnp.sum(amp_curve * jnp.cos(phase_curve), axis=1)
    imag_part = jnp.sum(amp_curve * jnp.sin(phase_curve), axis=1)
    return jnp.stack([real_part, imag_part], axis=1).astype(jnp.bfloat16)

def make_wave(amplitude, phase_zero, slope, curvature, first_bin, slot_index, live_count, extent, window):
    offsets = jnp.arange(extent, dtype=jnp.int32)[None, :] - first_bin[:, None]
    inside = (offsets >= 0) & (offsets < window) & (slot_index < live_count)[:, None]
    shifted = offsets.astype(jnp.float32)
    envelope = jnp.sin(jnp.pi * (shifted + 0.5) / window) ** 2
    phase_angle = phase_zero[:, None] + slope[:, None] * shifted + curvature[:, None] * shifted * shifted
    real_part = jnp.where(inside, amplitude[:, None] * envelope * jnp.cos(phase_angle), 0.0)
    imag_part = jnp.where(inside, amplitude[:, None] * envelope * jnp.sin(phase_angle), 0.0)
    return jnp.stack([real_part, imag_part], axis=1).astype(jnp.bfloat16)

def chebyshev(position):
    terms = [jnp.ones_like(position), position]
    for degree in range(2, NCOEF):
        terms.append(2.0 * position * terms[-1] - terms[-2])
    return jnp.stack(terms[:NCOEF], axis=-1)

def cholesky_solve(gram, moment):
    lower = jnp.linalg.cholesky(gram)
    order_count = gram.shape[0]
    forward = []
    for row_index in range(order_count):
        partial_sum = moment[row_index]
        for col_index in range(row_index):
            partial_sum = partial_sum - lower[row_index, col_index] * forward[col_index]
        forward.append(partial_sum / lower[row_index, row_index])
    backward = [None] * order_count
    for row_index in reversed(range(order_count)):
        partial_sum = forward[row_index]
        for col_index in range(row_index + 1, order_count):
            partial_sum = partial_sum - lower[col_index, row_index] * backward[col_index]
        backward[row_index] = partial_sum / lower[row_index, row_index]
    return jnp.stack(backward)

def reference(data, inv_noise, mbh_amp, mbh_phase, bin_amp, bin_phase, bin_slope, bin_curve, bin_start, bin_count):

    def band_template(band_index):
        coef_amp = lax.dynamic_slice_in_dim(mbh_amp, band_index, 1, 3)
        coef_phase = lax.dynamic_slice_in_dim(mbh_phase, band_index, 1, 3)
        halves = half_templates(coef_amp, coef_phase, BB)[:, :, 0, :]
        return halves.reshape(W, 2, 2, BB).astype(jnp.float32).sum(axis=1)
    band_ids = jnp.arange(NBANDS, dtype=jnp.int32)
    template = lax.map(band_template, band_ids)
    template = template.transpose(1, 2, 0, 3).reshape(W, 2, NBIN)
    residual = data[None] - template
    weighted = (residual * inv_noise.astype(jnp.float32)[None, None, :]).astype(jnp.bfloat16)
    weighted_pad = jnp.concatenate([weighted, jnp.zeros((W, 2, Q), jnp.bfloat16)], axis=2)
    noise_pad = jnp.concatenate([inv_noise, jnp.zeros((Q,), jnp.bfloat16)], axis=0)
    slot_index = jnp.arange(P_SIZE, dtype=jnp.int32)

    def band_scores(band_index):
        offset = (band_index * BB).astype(jnp.int32)
        weighted_ext = lax.dynamic_slice_in_dim(weighted_pad, offset, BB + Q, 2)
        noise_ext = lax.dynamic_slice_in_dim(noise_pad, offset, BB + Q, 0).astype(jnp.float32)
        live_count = bin_count[band_index]
        wave = make_wave(bin_amp[band_index], bin_phase[band_index], bin_slope[band_index], bin_curve[band_index], bin_start[band_index], slot_index, live_count, BB + Q, Q)
        wave_flat = wave.reshape(P_SIZE, 2 * (BB + Q))
        correlation = jnp.dot(wave_flat.astype(jnp.float32), weighted_ext.reshape(W, 2 * (BB + Q)).T.astype(jnp.float32), preferred_element_type=jnp.float32)
        self_power = jnp.sum(wave.astype(jnp.float32) ** 2 * noise_ext[None, None, :], axis=(1, 2))
        live = slot_index < live_count
        accept = jnp.where(live[:, None], jax.nn.sigmoid(correlation - 0.5 * self_power[:, None]), 0.0)
        correction = jnp.dot(accept.astype(jnp.bfloat16).T.astype(jnp.float32), wave_flat.astype(jnp.float32), preferred_element_type=jnp.float32)
        return (accept.T, correction.reshape(W, 2, BB + Q))
    accept_all, correction_all = lax.map(band_scores, band_ids)
    accept_prob = accept_all.transpose(1, 0, 2).reshape(W, NBANDS * P_SIZE)
    own_part = correction_all[:, :, :, :BB].transpose(1, 2, 0, 3).reshape(W, 2, NBIN)
    rim_part = jnp.concatenate([correction_all[:, :, :, BB:], jnp.zeros((NBANDS, W, 2, BB - Q), jnp.float32)], axis=3)
    rim_part = jnp.concatenate([jnp.zeros((1, W, 2, BB), jnp.float32), rim_part[:-1]], axis=0)
    rim_part = rim_part.transpose(1, 2, 0, 3).reshape(W, 2, NBIN)
    residual_new = residual - own_part - rim_part
    squares = (residual_new * residual_new).reshape(W, 2, NBANDS, BB)
    log_power = jnp.log(jnp.mean(squares, axis=(0, 1, 3)) + 1e-06)
    position = (2 * band_ids + 1).astype(jnp.float32) / NBANDS - 1.0
    basis = chebyshev(position)
    gram = jnp.dot(basis.T, basis, precision=lax.Precision.HIGHEST)
    moment = jnp.dot(basis.T, log_power, precision=lax.Precision.HIGHEST)
    coef = cholesky_solve(gram, moment)
    noise_fit = jnp.dot(basis, coef, precision=lax.Precision.HIGHEST)
    return (accept_prob, residual_new, noise_fit)
```

```python
import functools
import math

import jax
import jax.numpy as jnp
import numpy as np
from jax import lax
from jax.experimental import pallas as pl
from jax.experimental.pallas import tpu as pltpu
from jax.sharding import PartitionSpec as P

Q = 128
NCOEF = 8
LANES = 128
SUB = 8
F32 = jnp.float32
BF16 = jnp.bfloat16
BOTH = ("group", "shard")

INV_TAU = np.float32(1.0 / (2.0 * math.pi))
TAU_A = np.float32(round(2.0 * math.pi * 512) / 512)
TAU_B = np.float32(round((2.0 * math.pi - float(TAU_A)) * 2**22) / 2**22)
TAU_C = np.float32(2.0 * math.pi - float(TAU_A) - float(TAU_B))
MAGIC = np.float32(1.5 * 2**23)
SIN2 = (6.283185160089475, -10.33541375785372, 5.100062754574036, -1.1960903483123309, 0.15444025802555503)
COS1 = (0.9999999534666666, -4.934792858675247, 4.058411914166824, -1.3318801612473732, 0.2196967986012024)


def nearest(x):
    return (x + MAGIC) - MAGIC


def poly(y, coefs):
    total = np.float32(coefs[-1])
    for c in coefs[-2::-1]:
        total = total * y + np.float32(c)
    return total


def cis_turns(r):
    y = r * r
    s2 = poly(y, SIN2) * r
    c1 = poly(y, COS1)
    return np.float32(1.0) - np.float32(0.5) * (s2 * s2), s2 * c1


def turns(angle):
    n = nearest(angle * INV_TAU)
    return (((angle - n * TAU_A) - n * TAU_B) - n * TAU_C) * INV_TAU


def frac(t):
    return t - nearest(t)


def col(x, lane, rows=SUB):
    return jnp.broadcast_to(x[:, lane : lane + 1], (rows, LANES))


def lane_iota(rows=SUB):
    return lax.broadcasted_iota(jnp.int32, (rows, LANES), 1)


def pack_kernel(amp_ref, phase_ref, out_ref):
    harmonics, powers, _, rows = amp_ref.shape
    width = out_ref.shape[1] // (2 * powers)
    for which, ref in enumerate((amp_ref, phase_ref)):
        for power in range(powers):
            start = (which * powers + power) * width
            parts = [ref[h, power] for h in range(harmonics)]
            if width > harmonics * rows:
                parts.append(jnp.zeros((ref.shape[2], width - harmonics * rows), F32))
            out_ref[:, start : start + width] = jnp.concatenate(parts, axis=1)


def make_template(rec_ref, compact_ref, harmonics, rows, band_bins, first_block, block_count, emit):
    peers = rec_ref.shape[0]
    width = rec_ref.shape[1] // 6
    pairs = rows // 2
    share = LANES / band_bins
    p0, p1, p2 = (rec_ref[:, (3 + k) * width : (4 + k) * width] for k in range(3))
    f0 = turns(p0)
    f1 = turns(p1 * np.float32(share))
    f2 = turns(p2 * np.float32(share * share))
    kb = first_block
    lin = (p1 + p2 * np.float32(2 * kb * share)) * np.float32(1.0 / band_bins) * INV_TAU
    quad = p2 * np.float32(1.0 / band_bins**2) * INV_TAU
    step_const = f1 + np.float32(2 * kb + 1) * f2
    step_lin = p2 * np.float32(2 * share / band_bins) * INV_TAU
    twist_cos, twist_sin = cis_turns(frac(np.float32(2.0) * f2))
    entries = [
        rec_ref[:, 0:width],
        rec_ref[:, width : 2 * width],
        rec_ref[:, 2 * width : 3 * width],
        frac(f0 + np.float32(kb) * f1 + np.float32(kb * kb) * f2),
        lin,
        quad,
    ]
    if block_count > 1:
        entries += [frac(step_const), step_lin, twist_cos, twist_sin]
    for i, entry in enumerate(entries):
        compact_ref[i] = entry

    lane = lane_iota().astype(F32)
    lane_sq = lane * lane
    u = (lane + np.float32(kb * LANES)) * np.float32(1.0 / band_bins)
    u_sq = u * u
    grow = np.float32(share * share) + np.float32(2 * share) * u

    def block(step, _):
        which, pair = step // pairs, step % pairs
        shift = (width - 2 * pair) % width
        rolled = [
            pltpu.roll(compact_ref[i, pl.ds(which * SUB, SUB), :], shift, 1)
            if pairs > 1
            else compact_ref[i, pl.ds(which * SUB, SUB), :]
            for i in range(len(entries))
        ]
        total_re = [None] * block_count
        total_im = [None] * block_count
        for s in range(2):
            re = [None] * block_count
            im = [None] * block_count
            for h in range(harmonics):
                c = [col(x, h * rows + s) for x in rolled]
                a = c[0] + c[1] * u + c[2] * u_sq
                z_re, z_im = cis_turns(frac(c[3] + c[4] * lane + c[5] * lane_sq))
                if block_count > 1:
                    da = c[1] * np.float32(share) + c[2] * grow
                    dda = c[2] * np.float32(2 * share * share)
                    w_re, w_im = cis_turns(frac(c[6] + c[7] * lane))
                for k in range(block_count):
                    x, y = a * z_re, a * z_im
                    re[k] = x if h == 0 else re[k] + x
                    im[k] = y if h == 0 else im[k] + y
                    if k + 1 < block_count:
                        z_re, z_im = z_re * w_re - z_im * w_im, z_re * w_im + z_im * w_re
                        a = a + da
                    if k + 2 < block_count:
                        w_re, w_im = w_re * c[8] - w_im * c[9], w_re * c[9] + w_im * c[8]
                        da = da + dda
            for k in range(block_count):
                half_re = re[k].astype(BF16).astype(F32)
                half_im = im[k].astype(BF16).astype(F32)
                total_re[k] = half_re if s == 0 else total_re[k] + half_re
                total_im[k] = half_im if s == 0 else total_im[k] + half_im
        emit(pl.multiple_of(pair * peers + which * SUB, SUB), total_re, total_im)
        return 0

    lax.fori_loop(0, pairs * (peers // SUB), block, 0)


def first_kernel(harmonics, rows, rec_ref, data_ref, noise_ref, resid_ref, rim_ref, compact_ref):
    band_bins = data_ref.shape[1]
    walkers = resid_ref.shape[0]

    def emit(row, re, im):
        at = pl.ds(row, SUB)
        resid_ref[at, :LANES] = data_ref[0:1, :LANES] - re[0]
        resid_ref[at, LANES:] = data_ref[1:2, :LANES] - im[0]

    make_template(rec_ref, compact_ref, harmonics, rows, band_bins, 0, 1, emit)
    noise = noise_ref[0:1, :LANES]
    noise = jnp.concatenate([noise, noise], axis=1)
    rim_ref[:walkers, :] = (resid_ref[...] * noise).astype(BF16)
    rim_ref[walkers:, :] = jnp.broadcast_to(noise, (rim_ref.shape[0] - walkers, 2 * LANES)).astype(BF16)


def rest_kernel(
    harmonics, rows, rec_ref, data_ref, noise_ref, first_ref, rim_ref, resid_ref, weighted_ref, compact_ref
):
    band_bins = data_ref.shape[1]
    blocks = band_bins // LANES
    walkers = resid_ref.shape[0]

    def emit(row, re, im):
        at = pl.ds(row, SUB)
        for k in range(1, blocks):
            here = slice(k * LANES, (k + 1) * LANES)
            there = slice(band_bins + k * LANES, band_bins + (k + 1) * LANES)
            resid_ref[at, here] = data_ref[0:1, here] - re[k - 1]
            resid_ref[at, there] = data_ref[1:2, here] - im[k - 1]

    for part in range(2):
        there = slice(part * band_bins, part * band_bins + LANES)
        resid_ref[:, there] = first_ref[:, part * LANES : (part + 1) * LANES]
        weighted_ref[:, there] = rim_ref[:walkers, part * LANES : (part + 1) * LANES]
    make_template(rec_ref, compact_ref, harmonics, rows, band_bins, 1, blocks - 1, emit)
    for part in range(2):
        there = slice(part * band_bins + LANES, (part + 1) * band_bins)
        weighted_ref[:, there] = (resid_ref[:, there] * noise_ref[0:1, LANES:]).astype(BF16)


def fit_rows(band, bands):
    width = -(-bands // LANES) * LANES
    place = lax.broadcasted_iota(jnp.int32, (NCOEF, width), 1)
    order = lax.broadcasted_iota(jnp.int32, (NCOEF, width), 0)
    x = (2 * place + 1).astype(F32) * np.float32(1.0 / bands) - np.float32(1.0)
    term, after = jnp.ones_like(x), x
    basis = jnp.zeros_like(x)
    for degree in range(NCOEF):
        basis = jnp.where(order == degree, term, basis)
        term, after = after, np.float32(2.0) * x * after - term
    basis = jnp.where(place < bands, basis, 0.0)
    row = lax.broadcasted_iota(jnp.int32, (NCOEF, LANES), 0)
    lane = lax.broadcasted_iota(jnp.int32, (NCOEF, LANES), 1)
    gram = jnp.zeros((NCOEF, LANES), F32)
    for j in range(NCOEF):
        gram = jnp.where(lane == j, jnp.sum(basis * basis[j : j + 1, :], axis=1, keepdims=True), gram)
    side = basis
    for i in range(NCOEF):
        scale = np.float32(1.0) / jnp.sqrt(gram[i : i + 1, i : i + 1])
        upper = gram[i : i + 1, :] * scale
        factor = gram[:, i : i + 1] * scale
        solved = side[i : i + 1, :] * scale
        below = row > i
        gram = jnp.where(below, gram - factor * upper, jnp.where(row == i, upper, gram))
        side = jnp.where(order > i, side - factor * solved, jnp.where(order == i, solved, side))
    for i in reversed(range(NCOEF)):
        solved = side[i : i + 1, :] / gram[i : i + 1, i : i + 1]
        side = jnp.where(order < i, side - gram[:, i : i + 1] * solved, jnp.where(order == i, solved, side))
    mine = jnp.sum(jnp.where(place == band, side, 0.0), axis=1, keepdims=True)
    return jnp.sum(basis * mine, axis=0, keepdims=True)


def wave_kernel(
    bands, count_ref, band_ref, amp_ref, phase_ref, slope_ref, curve_ref, start_ref, noise_ref,
    wave_ref, power_ref, noise_out_ref, fit_ref, cols_ref,
):
    slots = amp_ref.shape[1]
    band_bins = noise_ref.shape[1]
    blocks = band_bins // LANES
    noise_out_ref[...] = noise_ref[...].astype(F32)
    live = lax.broadcasted_iota(jnp.int32, (1, slots), 1) < count_ref[0]
    start = start_ref[...]
    stacked = jnp.concatenate(
        [
            jnp.where(live, amp_ref[...], 0.0),
            phase_ref[...],
            slope_ref[...],
            curve_ref[...],
            (start % LANES).astype(F32),
            (start // LANES).astype(F32),
            jnp.zeros((2, slots), F32),
        ],
        axis=0,
    )
    cols_ref[...] = jnp.concatenate([stacked.T, jnp.zeros((slots, LANES - SUB), F32)], axis=1)
    rows = 2 * SUB
    lane = lane_iota(rows).astype(F32)

    def block(step, _):
        at = pl.ds(pl.multiple_of(step * rows, rows), rows)
        params = cols_ref[at, :]
        amp, phase, slope, curve, low, high = (col(params, i, rows) for i in range(6))
        offset = lane - low
        wrapped = offset < 0.0
        j = jnp.where(wrapped, offset + np.float32(Q), offset)
        home = jnp.where(wrapped, high + 1.0, high)
        angle = phase + slope * j + curve * j * j
        c, s = cis_turns(turns(angle))
        y = (j + np.float32(0.5)) * np.float32(1.0 / Q) - np.float32(0.5)
        envelope = poly(y * y, COS1)
        scale = amp * (envelope * envelope)
        re = (scale * c).astype(BF16).astype(F32)
        im = (scale * s).astype(BF16).astype(F32)
        noise = jnp.zeros((rows, LANES), F32)
        for k in range(blocks):
            inside = home == np.float32(k)
            noise = jnp.where(inside, noise_out_ref[0:1, k * LANES : (k + 1) * LANES], noise)
            wave_ref[at, k * LANES : (k + 1) * LANES] = jnp.where(inside, re, 0.0).astype(BF16)
            wave_ref[at, band_bins + k * LANES : band_bins + (k + 1) * LANES] = jnp.where(inside, im, 0.0).astype(BF16)
        inside = home == np.float32(blocks)
        wave_ref[at, 2 * band_bins : 2 * band_bins + LANES] = jnp.where(inside, re, 0.0).astype(BF16)
        wave_ref[at, 2 * band_bins + LANES :] = jnp.where(inside, im, 0.0).astype(BF16)
        power_ref[at, :] = (re * re + im * im) * noise
        return 0

    lax.fori_loop(0, slots // rows, block, 0)
    fit = fit_rows(band_ref[0], bands)
    fit = jnp.broadcast_to(fit, (SUB, fit.shape[1])).T
    fit_ref[...] = jnp.broadcast_to(fit[:bands, 0:1], (bands, LANES))


def score_kernel(count_ref, weighted_ref, rim_ref, wave_ref, power_ref, accept_ref, half_ref, carry_ref):
    walkers, own = weighted_ref.shape
    slots = wave_ref.shape[0]
    over_lanes = (((1,), (1,)), ((), ()))
    corr = lax.dot_general(weighted_ref[...], wave_ref[:, :own], over_lanes, preferred_element_type=F32)
    corr += lax.dot_general(rim_ref[:walkers, :], wave_ref[:, own:], over_lanes, preferred_element_type=F32)
    rim = wave_ref[:, own:].astype(F32)
    re, im = rim[:, :LANES], rim[:, LANES:]
    noise = rim_ref[walkers : walkers + 2 * SUB, :LANES].astype(F32)[0:1]
    power = power_ref[...] + (re * re + im * im) * noise
    total = lax.dot_general(
        jnp.ones((SUB, LANES), F32), power, over_lanes, precision=lax.Precision.HIGHEST, preferred_element_type=F32
    )
    live = lax.broadcasted_iota(jnp.int32, (walkers, slots), 1) < count_ref[0]
    accept = jnp.where(live, jax.nn.sigmoid(corr - np.float32(0.5) * total[0:1, :]), 0.0)
    accept_ref[...] = accept
    half = accept.astype(BF16)
    half_ref[...] = half
    carry_ref[...] = jnp.dot(half, wave_ref[:, own:], preferred_element_type=F32).astype(BF16)


def update_kernel(half_ref, wave_ref, resid_ref, new_ref, squares_ref):
    walkers, own = resid_ref.shape
    half = half_ref[...]
    squares = jnp.zeros((walkers, LANES), F32)
    chunk = 2 * LANES
    for start in range(0, own, chunk):
        here = slice(start, start + chunk)
        new = resid_ref[:, here] - jnp.dot(half, wave_ref[:, here], preferred_element_type=F32)
        new_ref[:, here] = new
        for lane in range(0, chunk, LANES):
            if (start + lane) % (own // 2):
                squares += new[:, lane : lane + LANES] * new[:, lane : lane + LANES]
    squares_ref[...] = squares


def power_kernel(new_ref, carry_ref, squares_ref, edge_ref, log_ref):
    walkers, own = new_ref.shape
    total = squares_ref[...]
    for part in range(2):
        lanes = slice(part * LANES, (part + 1) * LANES)
        start = part * (own // 2)
        edge = new_ref[:, start : start + LANES] - carry_ref[:, lanes].astype(F32)
        edge_ref[:, lanes] = edge
        total += edge * edge
    total = jnp.sum(jnp.sum(total, axis=0, keepdims=True), axis=1, keepdims=True)
    log_power = jnp.log(total * np.float32(1.0 / (walkers * own)) + np.float32(1e-6))
    log_ref[...] = jnp.broadcast_to(log_power, log_ref.shape)


def output_kernel(peers, accept_ref, new_ref, edge_ref, prob_ref, out_ref):
    walkers, own = new_ref.shape
    pairs = walkers // peers
    half = own // 2

    def in_order(x):
        if pairs == 1:
            return x
        return jnp.swapaxes(x.reshape(pairs, peers, x.shape[1]), 0, 1).reshape(x.shape)

    prob_ref[...] = in_order(accept_ref[...])
    for part in range(2):
        out_ref[:, part, :LANES] = in_order(edge_ref[:, part * LANES : (part + 1) * LANES])
        out_ref[:, part, LANES:] = in_order(new_ref[:, part * half + LANES : (part + 1) * half])


def call(kernel, outs, args, scratch=(), smem=0, flops=0, name=None):
    vmem = pl.BlockSpec(memory_space=pltpu.VMEM)
    return pl.pallas_call(
        kernel,
        out_shape=outs,
        in_specs=[pl.BlockSpec(memory_space=pltpu.SMEM)] * smem + [vmem] * (len(args) - smem),
        out_specs=[vmem] * len(outs),
        scratch_shapes=scratch,
        compiler_params=pltpu.CompilerParams(vmem_limit_bytes=32 * 2**20),
        cost_estimate=pl.CostEstimate(flops=flops, bytes_accessed=2**20, transcendentals=0),
        name=name,
    )(*args)


def shape(dims, dtype):
    return jax.ShapeDtypeStruct(dims, dtype)


def moved(x, by):
    devices = lax.axis_size(BOTH)
    return lax.ppermute(x, BOTH, [(i, i + by) for i in range(devices) if 0 <= i + by < devices])


def local(
    data,
    inv_noise,
    mbh_amp,
    mbh_phase,
    bin_amp,
    bin_phase,
    bin_slope,
    bin_curve,
    bin_start,
    bin_count,
):
    band_bins = data.shape[1]
    slots = bin_amp.shape[1]
    rows, harmonics, powers, peers = mbh_amp.shape
    walkers = rows * peers // 2
    bands = lax.axis_size(BOTH)
    band = lax.axis_index(BOTH).astype(jnp.int32)[None]
    own = 2 * band_bins

    def padded(count):
        return -(-count // LANES) * LANES

    (packed,) = call(
        pack_kernel,
        [shape((peers, 2 * powers * padded(harmonics * rows)), F32)],
        [mbh_amp.transpose(1, 2, 3, 0), mbh_phase.transpose(1, 2, 3, 0)],
        name="pack",
    )
    received = lax.all_to_all(packed, "shard", split_axis=0, concat_axis=0, tiled=True)
    if rows % 2:
        pieces = received.reshape(peers // 2, 2, 2 * powers, -1)[..., : harmonics * rows]
        pieces = pieces.reshape(peers // 2, 2, 2 * powers, harmonics, rows).transpose(0, 2, 3, 1, 4)
        rows, peers = 2 * rows, peers // 2
        pieces = pieces.reshape(peers, 2 * powers, harmonics * rows)
        pieces = jnp.pad(pieces, ((0, 0), (0, 0), (0, padded(harmonics * rows) - harmonics * rows)))
        received = pieces.reshape(peers, -1)
    width = received.shape[1] // (2 * powers)

    wave, slot_power, noise, fit = call(
        functools.partial(wave_kernel, bands),
        [
            shape((slots, own + 2 * LANES), BF16),
            shape((slots, LANES), F32),
            shape((1, band_bins), F32),
            shape((bands, LANES), F32),
        ],
        [bin_count, band, bin_amp, bin_phase, bin_slope, bin_curve, bin_start, inv_noise[None, :]],
        scratch=[pltpu.VMEM((slots, LANES), F32)],
        smem=2,
        name="waves",
    )
    first, rim = call(
        functools.partial(first_kernel, harmonics, rows),
        [shape((walkers, 2 * LANES), F32), shape((walkers + 2 * SUB, 2 * LANES), BF16)],
        [received, data, noise],
        scratch=[pltpu.VMEM((10, peers, width), F32)],
        name="first_bins",
    )
    rim_next = moved(rim, -1)
    resid, weighted = call(
        functools.partial(rest_kernel, harmonics, rows),
        [shape((walkers, own), F32), shape((walkers, own), BF16)],
        [received, data, noise, first, rim],
        scratch=[pltpu.VMEM((10, peers, width), F32)],
        flops=10**9,
        name="other_bins",
    )
    accept, half, carry = call(
        score_kernel,
        [shape((walkers, slots), F32), shape((walkers, slots), BF16), shape((walkers, 2 * LANES), BF16)],
        [bin_count, weighted, rim_next, wave, slot_power],
        smem=1,
        name="scores",
    )
    carried = moved(carry, 1)
    updated, squares = call(
        update_kernel,
        [shape((walkers, own), F32), shape((walkers, LANES), F32)],
        [half, wave, resid],
        flops=10**9,
        name="update",
    )
    edge, log_power = call(
        power_kernel,
        [shape((walkers, 2 * LANES), F32), shape((bands, LANES), F32)],
        [updated, carried, squares],
        name="log_power",
    )
    log_powers = lax.all_to_all(log_power, BOTH, split_axis=0, concat_axis=0, tiled=True)
    accept_prob, residual_new = call(
        functools.partial(output_kernel, peers),
        [shape((walkers, slots), F32), shape((walkers, 2, band_bins), F32)],
        [accept, updated, edge],
        name="outputs",
    )
    noise_fit = jnp.sum(fit * log_powers, axis=0)[:1]
    return (accept_prob, residual_new, noise_fit)


def solution(mesh):
    in_specs = (
        P(None, BOTH),
        P(BOTH),
        P("shard", None, None, "group"),
        P("shard", None, None, "group"),
        P(BOTH, None),
        P(BOTH, None),
        P(BOTH, None),
        P(BOTH, None),
        P(BOTH, None),
        P(BOTH),
    )
    out_specs = (P(None, BOTH), P(None, None, BOTH), P(BOTH))
    return jax.shard_map(local, mesh=mesh, in_specs=in_specs, out_specs=out_specs, check_vma=False)
```

```python
import functools
import math

import jax
import jax.numpy as jnp
import numpy as np
from jax import lax
from jax.experimental import pallas as pl
from jax.experimental.pallas import tpu as pltpu
from jax.sharding import PartitionSpec as P

Q = 128
NCOEF = 8
LANES = 128
SUB = 8
F32 = jnp.float32
BF16 = jnp.bfloat16
BOTH = ("group", "shard")
UNROLL = 2

INV_TAU = np.float32(1.0 / (2.0 * math.pi))
TAU_A = np.float32(round(2.0 * math.pi * 512) / 512)
TAU_B = np.float32(round((2.0 * math.pi - float(TAU_A)) * 2**22) / 2**22)
TAU_C = np.float32(2.0 * math.pi - float(TAU_A) - float(TAU_B))
MAGIC = np.float32(1.5 * 2**23)
SIN2 = (6.283185160089475, -10.33541375785372, 5.100062754574036, -1.1960903483123309, 0.15444025802555503)
COS1 = (0.9999999534666666, -4.934792858675247, 4.058411914166824, -1.3318801612473732, 0.2196967986012024)


def nearest(x):
    return (x + MAGIC) - MAGIC


def poly(y, coefs):
    total = np.float32(coefs[-1])
    for c in coefs[-2::-1]:
        total = total * y + np.float32(c)
    return total


def cis_turns(r):
    y = r * r
    s2 = poly(y, SIN2) * r
    c1 = poly(y, COS1)
    return np.float32(1.0) - np.float32(0.5) * (s2 * s2), s2 * c1


def turns(angle):
    n = nearest(angle * INV_TAU)
    return (((angle - n * TAU_A) - n * TAU_B) - n * TAU_C) * INV_TAU


def frac(t):
    return t - nearest(t)


def col(x, lane, rows=SUB):
    return jnp.broadcast_to(x[:, lane : lane + 1], (rows, LANES))


def lane_iota(rows=SUB):
    return lax.broadcasted_iota(jnp.int32, (rows, LANES), 1)


def pack_kernel(
    place_ref, amp_hbm, phase_hbm, data_hbm, noise_hbm, bin_amp_hbm, bin_phase_hbm, bin_slope_hbm, bin_curve_hbm,
    bin_start_hbm, count_hbm, packed_ref, bins_ref, data_ref, noise_ref,
    amp_ref, phase_ref, rows_ref, start_ref, raw_noise_ref, count_ref, sems,
):
    copies = [
        pltpu.make_async_copy(source, target, sems.at[i])
        for i, (source, target) in enumerate(
            [
                (amp_hbm, amp_ref),
                (phase_hbm, phase_ref),
                (count_hbm, count_ref),
                (bin_amp_hbm, rows_ref.at[0]),
                (bin_phase_hbm, rows_ref.at[1]),
                (bin_slope_hbm, rows_ref.at[2]),
                (bin_curve_hbm, rows_ref.at[3]),
                (bin_start_hbm, start_ref),
                (data_hbm, data_ref),
                (noise_hbm, raw_noise_ref),
            ]
        )
    ]
    for copy in copies:
        copy.start()
    harmonics, powers, peers, rows = amp_ref.shape
    width = -(-harmonics * rows // LANES) * LANES
    span = 2 * powers * width
    slots = bins_ref.shape[1]
    band_bins = data_ref.shape[1]
    for copy in copies[:2]:
        copy.wait()
    for which, ref in enumerate((amp_ref, phase_ref)):
        for power in range(powers):
            start = (which * powers + power) * width
            parts = [ref[h, power] for h in range(harmonics)]
            if width > harmonics * rows:
                parts.append(jnp.zeros((peers, width - harmonics * rows), F32))
            packed = jnp.concatenate(parts, axis=1)
            packed_ref[:, 0, start : start + width] = packed
            packed_ref[:, 0, span + start : span + start + width] = jnp.concatenate([packed[-1:], packed[:-1]], axis=0)
            packed_ref[:, 0, 2 * span + start : 2 * span + start + width] = jnp.concatenate(
                [packed[1:], packed[:1]], axis=0
            )
    for copy in copies[2:]:
        copy.wait()
    live = lax.broadcasted_iota(jnp.int32, (1, slots), 1) < count_ref[0]
    start = start_ref[...]
    amp = jnp.where(live, rows_ref[0], 0.0)
    rows = [amp, rows_ref[1], rows_ref[2], rows_ref[3], start.astype(F32)]
    bins_ref[...] = jnp.concatenate([*rows, live.astype(F32), jnp.zeros((2, slots), F32)], axis=0)
    raw_noise = raw_noise_ref[...].astype(F32)
    noise = jnp.concatenate([raw_noise[i : i + 1] for i in range(raw_noise.shape[0])], axis=1)
    noise_ref[...] = noise
    place = place_ref[0]
    after = lax.rem(place + 1, peers)
    before = lax.rem(place + peers - 1, peers)
    data = data_ref[...]
    for device, lanes, slot_rows in (
        (before, slice(0, LANES), []),
        (after, slice(band_bins - LANES, band_bins), rows),
    ):
        for i, row in enumerate([data[0:1, lanes], data[1:2, lanes], noise[:, lanes], *slot_rows]):
            start = 3 * span + (i * LANES if i < 3 else 3 * LANES + (i - 3) * slots)
            packed_ref[pl.ds(device, 1), 0, start : start + row.shape[1]] = row


def cross_kernel(place_ref, rec_ref, _, out_ref):
    peers = rec_ref.shape[0]
    span = out_ref.shape[1]
    first = place_ref[0] == 0
    out_ref[:peers, :] = jnp.where(first, rec_ref[:, span : 2 * span], rec_ref[:, 2 * span : 3 * span])
    row = jnp.where(first, peers - 1, 0)
    extra = rec_ref.shape[1] - 3 * span
    for i in range(-(-extra // span)):
        lanes = min(span, extra - i * span)
        start = 3 * span + i * span
        out_ref[peers + i : peers + i + 1, :lanes] = rec_ref[pl.ds(row, 1), start : start + lanes]


def coefficients(rec, band_bins):
    width = rec.shape[1] // 6
    share = LANES / band_bins
    amps = [rec[:, k * width : (k + 1) * width] for k in range(3)]
    p0, p1, p2 = (rec[:, (3 + k) * width : (4 + k) * width] for k in range(3))
    return amps, (p1, p2), (turns(p0), turns(p1 * np.float32(share)), turns(p2 * np.float32(share * share)))


def block_entries(k, band_bins, linear, reduced):
    p1, p2 = linear
    f0, f1, f2 = reduced
    share = LANES / band_bins
    const = frac(f0 + np.float32(k) * f1 + np.float32(k * k) * f2)
    slope = (p1 + p2 * np.float32(2 * k * share)) * np.float32(1.0 / band_bins) * INV_TAU
    return [const, slope, p2 * np.float32(1.0 / band_bins**2) * INV_TAU]


def over_walkers(compact_ref, entries, rows, peers, body):
    for i, entry in enumerate(entries):
        compact_ref[i] = entry
    width = compact_ref.shape[2]
    pairs = rows // 2

    def block(step, _):
        which, pair = step // pairs, step % pairs
        shift = (width - 2 * pair) % width
        rolled = [compact_ref[i, pl.ds(which * SUB, SUB), :] for i in range(len(entries))]
        if pairs > 1:
            rolled = [pltpu.roll(x, shift, 1) for x in rolled]
        body(pl.multiple_of(pair * peers + which * SUB, SUB), lambda h, s: [col(x, h * rows + s) for x in rolled])
        return 0

    steps = pairs * (peers // SUB)
    lax.fori_loop(0, steps, block, 0, unroll=UNROLL)


def summed(halves):
    return [a.astype(BF16).astype(F32) + b.astype(BF16).astype(F32) for a, b in zip(*halves, strict=True)]


def template_kernel(harmonics, rows, rec_ref, data_ref, noise_ref, resid_ref, weighted_ref, compact_ref):
    band_bins = data_ref.shape[1]
    blocks = band_bins // LANES
    share = LANES / band_bins
    amps, linear, reduced = coefficients(rec_ref, band_bins)
    _, f1, f2 = reduced
    twist = cis_turns(frac(np.float32(2.0) * f2))
    step = [frac(f1 + f2), linear[1] * np.float32(2 * share / band_bins) * INV_TAU]
    entries = [*amps, *block_entries(0, band_bins, linear, reduced), *step, *twist]
    lane = lane_iota().astype(F32)
    lane_sq = lane * lane
    u = lane * np.float32(1.0 / band_bins)
    grow = np.float32(share * share) + np.float32(2 * share) * u

    def body(row, columns):
        halves = []
        for s in range(2):
            total = [None] * (2 * blocks)
            for h in range(harmonics):
                a0, a1, a2, const, slope, curve, step_const, step_slope, twist_re, twist_im = columns(h, s)
                z_re, z_im = cis_turns(frac((const + slope * lane) + curve * lane_sq))
                w_re, w_im = cis_turns(frac(step_const + step_slope * lane))
                a = a0 + (a1 + a2 * u) * u
                da = a1 * np.float32(share) + a2 * grow
                dda = a2 * np.float32(2 * share * share)
                for k in range(blocks):
                    terms = (a * z_re, a * z_im)
                    for i in range(2):
                        total[2 * k + i] = terms[i] if h == 0 else total[2 * k + i] + terms[i]
                    if k + 1 < blocks:
                        z_re, z_im = z_re * w_re - z_im * w_im, z_re * w_im + z_im * w_re
                        a = a + da
                    if k + 2 < blocks:
                        w_re, w_im = w_re * twist_re - w_im * twist_im, w_re * twist_im + w_im * twist_re
                        da = da + dda
            halves.append(total)
        for i, template in enumerate(summed(halves)):
            here = i // 2 * LANES
            there = i % 2 * band_bins + here
            part = data_ref[i % 2 : i % 2 + 1, here : here + LANES]
            resid_ref[pl.ds(row, SUB), there : there + LANES] = part - template

    over_walkers(compact_ref, entries, rows, rec_ref.shape[0], body)
    for part in range(2):
        lanes = slice(part * band_bins, (part + 1) * band_bins)
        weighted_ref[:, lanes] = (resid_ref[:, lanes] * noise_ref[0:1, :]).astype(BF16)


def slot_columns(bins, cols_ref):
    slots = bins.shape[1]
    cols_ref[...] = jnp.concatenate([bins.T, jnp.zeros((slots, LANES - SUB), F32)], axis=1)


def slot_wave(params, lane):
    rows = params.shape[0]
    amp, phase, slope, curve, start = (col(params, i, rows) for i in range(5))
    high = jnp.floor(start * np.float32(1.0 / LANES))
    low = start - high * np.float32(LANES)
    offset = lane - low
    wrapped = offset < 0.0
    j = jnp.where(wrapped, offset + np.float32(Q), offset)
    angle = phase + slope * j + curve * j * j
    c, s = cis_turns(turns(angle))
    y = (j + np.float32(0.5)) * np.float32(1.0 / Q) - np.float32(0.5)
    envelope = poly(y * y, COS1)
    scale = amp * (envelope * envelope)
    return scale * c, scale * s, wrapped, high


def wave_kernel(bins_ref, noise_ref, wave_ref, power_ref, cols_ref):
    slots = bins_ref.shape[1]
    band_bins = noise_ref.shape[1]
    blocks = band_bins // LANES
    slot_columns(bins_ref[...], cols_ref)
    rows = 2 * SUB
    lane = lane_iota(rows).astype(F32)

    def block(step, _):
        at = pl.ds(pl.multiple_of(step * rows, rows), rows)
        re, im, wrapped, high = slot_wave(cols_ref[at, :], lane)
        home = jnp.where(wrapped, high + 1.0, high)
        re_half, im_half = re.astype(BF16), im.astype(BF16)
        re, im = re_half.astype(F32), im_half.astype(F32)
        noise = jnp.zeros((rows, LANES), F32)
        for k in range(blocks + 1):
            inside = home == np.float32(k)
            if k < blocks:
                noise = jnp.where(inside, noise_ref[0:1, k * LANES : (k + 1) * LANES], noise)
            start = k * LANES if k < blocks else 2 * band_bins
            wave_ref[at, start : start + LANES] = jnp.where(inside, re, 0.0).astype(BF16)
            start += band_bins if k < blocks else LANES
            wave_ref[at, start : start + LANES] = jnp.where(inside, im, 0.0).astype(BF16)
        power_ref[at, :] = (re * re + im * im) * noise
        return 0

    lax.fori_loop(0, slots // rows, block, 0, unroll=4)


def fit_rows(band, bands):
    width = -(-bands // LANES) * LANES
    place = lax.broadcasted_iota(jnp.int32, (NCOEF, width), 1)
    order = lax.broadcasted_iota(jnp.int32, (NCOEF, width), 0)
    x = (2 * place + 1).astype(F32) * np.float32(1.0 / bands) - np.float32(1.0)
    term, after = jnp.ones_like(x), x
    basis = jnp.zeros_like(x)
    for degree in range(NCOEF):
        basis = jnp.where(order == degree, term, basis)
        term, after = after, np.float32(2.0) * x * after - term
    basis = jnp.where(place < bands, basis, 0.0)
    row = lax.broadcasted_iota(jnp.int32, (NCOEF, LANES), 0)
    lane = lax.broadcasted_iota(jnp.int32, (NCOEF, LANES), 1)
    gram = jnp.zeros((NCOEF, LANES), F32)
    for j in range(NCOEF):
        gram = jnp.where(lane == j, jnp.sum(basis * basis[j : j + 1, :], axis=1, keepdims=True), gram)
    side = basis
    for i in range(NCOEF):
        scale = np.float32(1.0) / jnp.sqrt(gram[i : i + 1, i : i + 1])
        upper = gram[i : i + 1, :] * scale
        factor = gram[:, i : i + 1] * scale
        solved = side[i : i + 1, :] * scale
        below = row > i
        gram = jnp.where(below, gram - factor * upper, jnp.where(row == i, upper, gram))
        side = jnp.where(order > i, side - factor * solved, jnp.where(order == i, solved, side))
    for i in reversed(range(NCOEF)):
        solved = side[i : i + 1, :] / gram[i : i + 1, i : i + 1]
        side = jnp.where(order < i, side - gram[:, i : i + 1] * solved, jnp.where(order == i, solved, side))
    mine = jnp.sum(jnp.where(place == band, side, 0.0), axis=1, keepdims=True)
    return jnp.sum(basis * mine, axis=0, keepdims=True)


OVER_LANES = (((1,), (1,)), ((), ()))


def accepted(corr, power):
    total = lax.dot_general(
        jnp.ones((SUB, LANES), F32), power, OVER_LANES, precision=lax.Precision.HIGHEST, preferred_element_type=F32
    )
    return jax.nn.sigmoid(corr - np.float32(0.5) * total[0:1, :])


def score_kernel(
    harmonics, rows, blocks, place_ref, weighted_ref, resid_ref, noise_ref, bins_ref, wave_ref, power_ref, rec_ref, extra_ref,
    cross_ref, accept_ref, new_ref, log_ref,
    cols_ref, prev_ref, prev_power_ref, beside_ref, beside_extra_ref, compact_ref, edge_ref, rim_ref,
):
    walkers, own = weighted_ref.shape
    slots = wave_ref.shape[0]
    band_bins = own // 2
    last = blocks - 1
    peers = rec_ref.shape[0]
    span = cross_ref.shape[1]
    sources = extra_ref.shape[0]
    place = place_ref[0]

    extra = extra_ref.shape[1]
    for i, (far, source) in enumerate(((0, lax.rem(place + sources - 1, sources)), (sources - 1, lax.rem(place + 1, sources)))):
        @pl.when(place == far)
        def _():
            beside_ref[i] = cross_ref[:peers, :]
            for j in range(-(-extra // span)):
                lanes = min(span, extra - j * span)
                beside_extra_ref[i : i + 1, j * span : j * span + lanes] = cross_ref[sources + j : sources + j + 1, :lanes]

        @pl.when(place != far)
        def _():
            beside_ref[i] = rec_ref[:, i * span : (i + 1) * span]
            beside_extra_ref[i : i + 1, :] = extra_ref[pl.ds(source, 1), :]

    lane = lane_iota().astype(F32)
    lane_sq = lane * lane
    entries = []
    for i, k in enumerate((last, 0)):
        amps, linear, reduced = coefficients(beside_ref[i], band_bins)
        entries += [*amps, *block_entries(k, band_bins, linear, reduced)]

    def body(row, columns):
        halves = []
        for s in range(2):
            total = None
            for h in range(harmonics):
                c = columns(h, s)
                terms = []
                for i, k in enumerate((last, 0)):
                    a0, a1, a2, const, slope, curve = c[6 * i : 6 * i + 6]
                    re, im = cis_turns(frac((const + slope * lane) + curve * lane_sq))
                    u = (lane + np.float32(k * LANES)) * np.float32(1.0 / band_bins)
                    a = a0 + (a1 + a2 * u) * u
                    terms += [a * re, a * im]
                total = terms if h == 0 else [x + y for x, y in zip(total, terms, strict=True)]
            halves.append(total)
        for i, template in enumerate(summed(halves)):
            part = beside_extra_ref[i // 2 : i // 2 + 1, i % 2 * LANES : (i % 2 + 1) * LANES]
            edge_ref[pl.ds(row, SUB), i * LANES : (i + 1) * LANES] = part - template

    over_walkers(compact_ref, entries, rows, peers, body)
    below = beside_extra_ref[0:1, 2 * LANES : 3 * LANES]
    above = beside_extra_ref[1:2, 2 * LANES : 3 * LANES]
    noise = jnp.concatenate([below, below, above, above], axis=1)
    rim_ref[...] = (edge_ref[...] * noise).astype(BF16)

    bins = [beside_extra_ref[0:1, 3 * LANES + i * slots : 3 * LANES + (i + 1) * slots] for i in range(5)]
    slot_columns(jnp.concatenate([*bins, jnp.zeros((3, slots), F32)], axis=0), cols_ref)
    group = 2 * SUB
    lane = lane_iota(group).astype(F32)
    first_noise = noise_ref[0:1, :LANES]

    def block(step, _):
        at = pl.ds(pl.multiple_of(step * group, group), group)
        re, im, wrapped, high = slot_wave(cols_ref[at, :], lane)
        passes = high == np.float32(last)
        re = jnp.where(passes, re, 0.0).astype(BF16).astype(F32)
        im = jnp.where(passes, im, 0.0).astype(BF16).astype(F32)
        prev_power_ref[at, :] = (re * re + im * im) * jnp.where(wrapped, first_noise, below)
        prev_ref[at, :LANES] = jnp.where(wrapped, 0.0, re).astype(BF16)
        prev_ref[at, LANES : 2 * LANES] = jnp.where(wrapped, 0.0, im).astype(BF16)
        prev_ref[at, 2 * LANES : 3 * LANES] = jnp.where(wrapped, re, 0.0).astype(BF16)
        prev_ref[at, 3 * LANES :] = jnp.where(wrapped, im, 0.0).astype(BF16)
        return 0

    lax.fori_loop(0, slots // group, block, 0, unroll=4)
    mine = jnp.concatenate([weighted_ref[:, :LANES], weighted_ref[:, band_bins : band_bins + LANES]], axis=1)
    tail = jnp.concatenate([rim_ref[:, : 2 * LANES], mine], axis=1)
    corr = lax.dot_general(tail, prev_ref[...], OVER_LANES, preferred_element_type=F32)
    half = accepted(corr, prev_power_ref[...]).astype(BF16)
    carried = jnp.dot(half, prev_ref[:, 2 * LANES :], preferred_element_type=F32)

    corr = lax.dot_general(weighted_ref[...], wave_ref[:, :own], OVER_LANES, preferred_element_type=F32)
    corr += lax.dot_general(rim_ref[:, 2 * LANES :], wave_ref[:, own:], OVER_LANES, preferred_element_type=F32)
    rim = wave_ref[:, own:].astype(F32)
    re, im = rim[:, :LANES], rim[:, LANES:]
    accept = accepted(corr, power_ref[...] + (re * re + im * im) * above)
    accept = jnp.where(bins_ref[5:6, :] > 0.0, accept, 0.0)
    accept_ref[...] = accept
    half = accept.astype(BF16)
    squares = jnp.zeros((walkers, LANES), F32)
    chunk = 2 * LANES
    for start in range(0, own, chunk):
        lanes = slice(start, start + chunk)
        new = resid_ref[:, lanes] - jnp.dot(half, wave_ref[:, lanes], preferred_element_type=F32)
        pieces = [new[:, i : i + LANES] for i in range(0, chunk, LANES)]
        if start % band_bins == 0:
            part = start // band_bins
            pieces[0] -= carried[:, part * LANES : (part + 1) * LANES]
        for i, piece in enumerate(pieces):
            new_ref[:, start + i * LANES : start + (i + 1) * LANES] = piece
            squares += piece * piece
    total = jnp.sum(jnp.sum(squares, axis=0, keepdims=True), axis=1, keepdims=True)
    log_power = jnp.log(total * np.float32(1.0 / (walkers * own)) + np.float32(1e-6))
    log_ref[:, 0, :] = jnp.broadcast_to(log_power, (log_ref.shape[0], log_ref.shape[2]))


def output_kernel(peers, bands, band_ref, accept_ref, new_ref, prob_ref, out_ref, fit_ref):
    walkers, own = new_ref.shape
    pairs = walkers // peers
    half = own // 2

    def in_order(x):
        if pairs == 1:
            return x
        return jnp.swapaxes(x.reshape(pairs, peers, x.shape[1]), 0, 1).reshape(x.shape)

    prob_ref[...] = in_order(accept_ref[...])
    for part in range(2):
        out_ref[:, part, :] = in_order(new_ref[:, part * half : (part + 1) * half])
    fit = fit_rows(band_ref[0], bands)
    fit = jnp.broadcast_to(fit, (SUB, fit.shape[1])).T
    fit_ref[...] = jnp.broadcast_to(fit[:bands, 0:1], (bands, LANES))


def call(kernel, outs, args, scratch=(), smem=0, flops=0, name=None, hbm=False, last_any=False):
    vmem = pl.BlockSpec(memory_space=pltpu.VMEM)
    rest = vmem
    if hbm:
        rest = pl.BlockSpec(memory_space=pl.ANY)
        args = [pltpu.with_memory_space_constraint(x, pltpu.HBM) if x.dtype != jnp.int32 or x.ndim > 1 else x for x in args]
    specs = [pl.BlockSpec(memory_space=pltpu.SMEM)] * smem + [rest] * (len(args) - smem)
    if last_any:
        specs[-1] = pl.BlockSpec(memory_space=pl.ANY)
    return pl.pallas_call(
        kernel,
        out_shape=outs,
        in_specs=specs,
        out_specs=[vmem] * len(outs),
        scratch_shapes=scratch,
        compiler_params=pltpu.CompilerParams(vmem_limit_bytes=32 * 2**20),
        cost_estimate=pl.CostEstimate(flops=flops, bytes_accessed=2**20, transcendentals=0),
        name=name,
    )(*args)


def shape(dims, dtype):
    return jax.ShapeDtypeStruct(dims, dtype)


def local(
    data,
    inv_noise,
    mbh_amp,
    mbh_phase,
    bin_amp,
    bin_phase,
    bin_slope,
    bin_curve,
    bin_start,
    bin_count,
):
    band_bins = data.shape[1]
    slots = bin_amp.shape[1]
    rows, harmonics, powers, peers = mbh_amp.shape
    sources = peers
    groups = lax.axis_size("group")
    walkers = rows * peers // 2
    bands = lax.axis_size(BOTH)
    place = lax.axis_index("shard").astype(jnp.int32)[None]
    band = lax.axis_index(BOTH).astype(jnp.int32)[None]
    own = 2 * band_bins

    def padded(count):
        return -(-count // LANES) * LANES

    width = padded(harmonics * rows)
    span = 2 * powers * width
    extra = 3 * LANES + 5 * slots
    packed, bins, data, noise = call(
        pack_kernel,
        [
            shape((peers, 1, 3 * span + extra), F32),
            shape((SUB, slots), F32),
            shape((2, band_bins), F32),
            shape((1, band_bins), F32),
        ],
        [
            place, mbh_amp.transpose(1, 2, 3, 0), mbh_phase.transpose(1, 2, 3, 0), data, inv_noise.reshape(-1, LANES),
            bin_amp, bin_phase, bin_slope, bin_curve, bin_start, bin_count,
        ],
        scratch=[
            pltpu.VMEM((harmonics, powers, peers, rows), F32),
            pltpu.VMEM((harmonics, powers, peers, rows), F32),
            pltpu.VMEM((4, 1, slots), F32),
            pltpu.VMEM((1, slots), jnp.int32),
            pltpu.VMEM((band_bins // LANES, LANES), BF16),
            pltpu.SMEM((1,), jnp.int32),
            pltpu.SemaphoreType.DMA((10,)),
        ],
        smem=1,
        hbm=True,
        name="pack",
    )
    received = lax.all_to_all(packed, "shard", split_axis=0, concat_axis=0, tiled=True)
    received = received.reshape(peers, -1)
    wave, slot_power = call(
        wave_kernel,
        [shape((slots, own + 2 * LANES), BF16), shape((slots, LANES), F32)],
        [bins, noise],
        scratch=[pltpu.VMEM((slots, LANES), F32)],
        flops=10**9,
        name="waves",
    )
    (to_cross,) = call(
        cross_kernel,
        [shape((sources + -(-extra // span // SUB) * SUB, span), F32)],
        [place, received, slot_power],
        smem=1,
        last_any=True,
        name="cross",
    )
    pairs = [(g * peers, (g + 1) * peers) for g in range(groups - 1)]
    pairs += [(g * peers + peers - 1, (g - 1) * peers + peers - 1) for g in range(1, groups)]
    crossed = lax.ppermute(to_cross, BOTH, pairs)

    extras = received[:, 3 * span :]
    if rows % 2:

        def paired(x):
            x = x.reshape(peers // 2, 2, 2 * powers, width)[..., : harmonics * rows]
            x = x.reshape(peers // 2, 2, 2 * powers, harmonics, rows).transpose(0, 2, 3, 1, 4)
            x = x.reshape(peers // 2, 2 * powers, 2 * harmonics * rows)
            x = jnp.pad(x, ((0, 0), (0, 0), (0, width - 2 * harmonics * rows)))
            return x.reshape(peers // 2, span)

        coefs, coefs_below, coefs_above = (paired(received[:, i * span : (i + 1) * span]) for i in range(3))
        coefs_beside = jnp.concatenate([coefs_below, coefs_above], axis=1)
        crossed = jnp.concatenate([paired(crossed[:peers]), jnp.zeros((peers // 2, span), F32), crossed[peers:]], axis=0)
        rows, peers = 2 * rows, peers // 2
    else:
        coefs = received[:, :span]
        coefs_beside = received[:, span : 3 * span]

    resid, weighted = call(
        functools.partial(template_kernel, harmonics, rows),
        [shape((walkers, own), F32), shape((walkers, own), BF16)],
        [coefs, data, noise],
        scratch=[pltpu.VMEM((10, peers, width), F32)],
        flops=10**9,
        name="template",
    )
    accept, updated, log_power = call(
        functools.partial(score_kernel, harmonics, rows, band_bins // LANES),
        [shape((walkers, slots), F32), shape((walkers, own), F32), shape((bands, 1, LANES), F32)],
        [place, weighted, resid, noise, bins, wave, slot_power, coefs_beside, extras, crossed],
        scratch=[
            pltpu.VMEM((slots, LANES), F32),
            pltpu.VMEM((slots, 4 * LANES), BF16),
            pltpu.VMEM((slots, LANES), F32),
            pltpu.VMEM((2, peers, span), F32),
            pltpu.VMEM((2, extra), F32),
            pltpu.VMEM((12, peers, width), F32),
            pltpu.VMEM((walkers, 4 * LANES), F32),
            pltpu.VMEM((walkers, 4 * LANES), BF16),
        ],
        smem=1,
        name="scores",
    )
    log_powers = lax.all_to_all(log_power, BOTH, split_axis=0, concat_axis=0, tiled=True)
    accept_prob, residual_new, fit = call(
        functools.partial(output_kernel, peers, bands),
        [shape((walkers, slots), F32), shape((walkers, 2, band_bins), F32), shape((bands, LANES), F32)],
        [band, accept, updated],
        smem=1,
        name="outputs",
    )
    noise_fit = jnp.sum(fit * log_powers[:, 0, :], axis=0)[:1]
    return (accept_prob, residual_new, noise_fit)


def solution(mesh):
    in_specs = (
        P(None, BOTH),
        P(BOTH),
        P("shard", None, None, "group"),
        P("shard", None, None, "group"),
        P(BOTH, None),
        P(BOTH, None),
        P(BOTH, None),
        P(BOTH, None),
        P(BOTH, None),
        P(BOTH),
    )
    out_specs = (P(None, BOTH), P(None, None, BOTH), P(BOTH))
    return jax.shard_map(local, mesh=mesh, in_specs=in_specs, out_specs=out_specs, check_vma=False)
```

```python
import functools
import math

import jax
import jax.numpy as jnp
import numpy as np
from jax import lax
from jax.experimental import pallas as pl
from jax.experimental.pallas import tpu as pltpu
from jax.sharding import PartitionSpec as P

Q = 128
NCOEF = 8
LANES = 128
SUB = 8
F32 = jnp.float32
BF16 = jnp.bfloat16
BOTH = ("group", "shard")

INV_TAU = np.float32(1.0 / (2.0 * math.pi))
TAU_A = np.float32(round(2.0 * math.pi * 512) / 512)
TAU_B = np.float32(round((2.0 * math.pi - float(TAU_A)) * 2**22) / 2**22)
TAU_C = np.float32(2.0 * math.pi - float(TAU_A) - float(TAU_B))
MAGIC = np.float32(1.5 * 2**23)
SIN2 = (6.283185160089475, -10.33541375785372, 5.100062754574036, -1.1960903483123309, 0.15444025802555503)
COS1 = (0.9999999534666666, -4.934792858675247, 4.058411914166824, -1.3318801612473732, 0.2196967986012024)


def nearest(x):
    return (x + MAGIC) - MAGIC


def padded(count):
    return -(-count // LANES) * LANES


def poly(y, coefs):
    total = np.float32(coefs[-1])
    for c in coefs[-2::-1]:
        total = total * y + np.float32(c)
    return total


def cis_turns(r):
    y = r * r
    s2 = poly(y, SIN2) * r
    c1 = poly(y, COS1)
    return np.float32(1.0) - np.float32(0.5) * (s2 * s2), s2 * c1


def turns(angle):
    n = nearest(angle * INV_TAU)
    return (((angle - n * TAU_A) - n * TAU_B) - n * TAU_C) * INV_TAU


def frac(t):
    return t - nearest(t)


def col(x, lane, rows=SUB):
    return jnp.broadcast_to(x[:, lane : lane + 1], (rows, LANES))


def lane_iota(rows=SUB):
    return lax.broadcasted_iota(jnp.int32, (rows, LANES), 1)


def pack_kernel(
    amp_hbm, phase_hbm, data_hbm, noise_hbm, bin_amp_hbm, bin_phase_hbm, bin_slope_hbm, bin_curve_hbm,
    bin_start_hbm, count_hbm, packed_ref, bins_ref, data_ref, noise_ref,
    amp_ref, phase_ref, rows_ref, start_ref, raw_noise_ref, count_ref, sems,
):
    copies = [
        pltpu.make_async_copy(source, target, sems.at[i])
        for i, (source, target) in enumerate(
            [
                (amp_hbm, amp_ref),
                (phase_hbm, phase_ref),
                (count_hbm, count_ref),
                (bin_amp_hbm, rows_ref.at[0]),
                (bin_phase_hbm, rows_ref.at[1]),
                (bin_slope_hbm, rows_ref.at[2]),
                (bin_curve_hbm, rows_ref.at[3]),
                (bin_start_hbm, start_ref),
                (data_hbm, data_ref),
                (noise_hbm, raw_noise_ref),
            ]
        )
    ]
    for copy in copies:
        copy.start()
    harmonics, powers, peers, rows = amp_ref.shape
    span = padded(2 * powers * harmonics * rows)
    slots = bins_ref.shape[1]
    band_bins = data_ref.shape[1]
    for copy in copies[2:]:
        copy.wait()
    live = lax.broadcasted_iota(jnp.int32, (1, slots), 1) < count_ref[0]
    amp = jnp.where(live, rows_ref[0], 0.0)
    slot_rows = [amp, rows_ref[1], rows_ref[2], rows_ref[3], start_ref[...].astype(F32)]
    bins_ref[...] = jnp.concatenate([*slot_rows, live.astype(F32), jnp.zeros((2, slots), F32)], axis=0)
    raw_noise = raw_noise_ref[...].astype(F32)
    noise = jnp.concatenate([raw_noise[i : i + 1] for i in range(raw_noise.shape[0])], axis=1)
    noise_ref[...] = noise
    start = 3 * span
    for lanes in (slice(0, LANES), slice(band_bins - LANES, band_bins)):
        for row in (data_ref[0:1, lanes], data_ref[1:2, lanes], noise[:, lanes]):
            packed_ref[:, 0, start : start + LANES] = jnp.broadcast_to(row, (peers, LANES))
            start += LANES
    for row in slot_rows:
        packed_ref[:, 0, start : start + slots] = jnp.broadcast_to(row, (peers, slots))
        start += slots
    for copy in copies[:2]:
        copy.wait()
    parts = [ref[h, power] for ref in (amp_ref, phase_ref) for power in range(powers) for h in range(harmonics)]
    if span > 2 * powers * harmonics * rows:
        parts.append(jnp.zeros((peers, span - 2 * powers * harmonics * rows), F32))
    packed = jnp.concatenate(parts, axis=1)
    if rows == 2 * SUB:
        lane = lax.broadcasted_iota(jnp.int32, (peers, LANES), 1)
        order = lane - lane % (2 * SUB) + lane % SUB * 2 + lane % (2 * SUB) // SUB
        blocks = [packed[:, i : i + LANES] for i in range(0, span, LANES)]
        blocks = [jnp.take_along_axis(x, order, axis=1, mode="promise_in_bounds") for x in blocks]
        packed = jnp.concatenate(blocks, axis=1)
    packed_ref[:, 0, :span] = packed
    packed_ref[:, 0, span : 2 * span] = jnp.concatenate([packed[-1:], packed[:-1]], axis=0)
    packed_ref[:, 0, 2 * span : 3 * span] = jnp.concatenate([packed[1:], packed[:1]], axis=0)


def cross_kernel(rec_ref, _, out_ref):
    peers = rec_ref.shape[0]
    span = out_ref.shape[1]
    first = lax.axis_index("shard") == 0
    out_ref[:peers, :] = jnp.where(first, rec_ref[:, span : 2 * span], rec_ref[:, 2 * span : 3 * span])
    start = 3 * span
    rim = rec_ref[0:1, start : start + 3 * LANES]
    start += 3 * LANES
    row = rec_ref[peers - 1 : peers, start:]
    row = jnp.concatenate([jnp.where(first, row[:, : 3 * LANES], rim), row[:, 3 * LANES :]], axis=1)
    for i, at in enumerate(range(0, row.shape[1], span)):
        lanes = min(span, row.shape[1] - at)
        out_ref[peers + i : peers + i + 1, :lanes] = row[:, at : at + lanes]


def coefficients(rec, width, band_bins):
    share = LANES / band_bins
    fill = jnp.zeros((rec.shape[0], LANES - width), F32)
    terms = [jnp.concatenate([rec[:, k * width : (k + 1) * width], fill], axis=1) for k in range(6)]
    amps, (p0, p1, p2) = terms[:3], terms[3:]
    return amps, (p1, p2), (turns(p0), turns(p1 * np.float32(share)), turns(p2 * np.float32(share * share)))


def phase_terms(k, band_bins, linear, reduced):
    p1, p2 = linear
    f0, f1, f2 = reduced
    share = LANES / band_bins
    const = frac(f0 + np.float32(k) * f1 + np.float32(k * k) * f2)
    slope = (p1 + p2 * np.float32(2 * k * share)) * np.float32(1.0 / band_bins) * INV_TAU
    return [const, slope, p2 * np.float32(1.0 / band_bins**2) * INV_TAU]


def amp_terms(k, band_bins, amps):
    a0, a1, a2 = amps
    at = k * LANES / band_bins
    slope = (a1 + a2 * np.float32(2 * at)) * np.float32(1.0 / band_bins)
    return [a0 + (a1 + a2 * np.float32(at)) * np.float32(at), slope, a2 * np.float32(1.0 / band_bins**2)]


def pieces(x):
    high = x.astype(BF16).astype(F32)
    rest = x - high
    middle = rest.astype(BF16).astype(F32)
    return [high, middle, (rest - middle).astype(BF16).astype(F32)]


QUAD = 16


def quad_rows(terms):
    terms = [pieces(x) for x in terms]
    rows = [*terms[0], *terms[1], *terms[2], *terms[2]]
    return rows + [jnp.zeros_like(rows[0])] * (QUAD - len(rows))


def lane_powers():
    row = lax.broadcasted_iota(jnp.int32, (QUAD, LANES), 0)
    lane = lax.broadcasted_iota(jnp.int32, (QUAD, LANES), 1)
    low = lane * lane % LANES
    table = jnp.where(row < 3, 1, jnp.where(row < 6, lane, jnp.where(row < 9, lane * lane - low, low)))
    table = jnp.where(row < 12, table, 0).astype(F32)
    zero = jnp.zeros((QUAD, LANES), F32)
    upper = jnp.concatenate([table, zero], axis=1)
    lower = jnp.concatenate([zero, table], axis=1)
    return jnp.concatenate([upper, lower], axis=0).astype(BF16)


def evaluator(pairs, stage_ref, values_ref):
    table = lane_powers()
    for pair, (first, second) in enumerate(pairs):
        for i, row in enumerate(quad_rows(first) + quad_rows(second)):
            stage_ref[pair, i] = row

    def evaluate(q):
        for pair in range(len(pairs)):
            rows = stage_ref[pair, :, q, :].T.astype(BF16)
            values_ref[pair, q * LANES : (q + 1) * LANES, :] = jnp.dot(rows, table, preferred_element_type=F32)

    return evaluate


def by_walkers(count, evaluate, block):
    evaluate(0)
    for q in range(count):
        if q + 1 < count:
            evaluate(q + 1)
        block(q)


def summed(halves):
    return [a.astype(BF16).astype(F32) + b.astype(BF16).astype(F32) for a, b in zip(*halves, strict=True)]


def template_kernel(harmonics, rec_ref, data_ref, noise_ref, resid_ref, weighted_ref, stage_ref, values_ref):
    band_bins = data_ref.shape[1]
    blocks = band_bins // LANES
    share = LANES / band_bins
    amps, linear, reduced = coefficients(rec_ref, harmonics * 2 * SUB, band_bins)
    _, f1, f2 = reduced
    zero = jnp.zeros_like(f1)
    twist_re, twist_im = cis_turns(frac(np.float32(2.0) * f2))
    step = [frac(f1 + f2), linear[1] * np.float32(2 * share / band_bins) * INV_TAU, zero]
    now, then = amp_terms(0, band_bins, amps), amp_terms(1, band_bins, amps)
    grow = [then[0] - now[0], amps[2] * np.float32(2 * share / band_bins), zero]
    evaluate = evaluator(
        [
            (phase_terms(0, band_bins, linear, reduced), now),
            (step, grow),
            ([twist_re, zero, zero], [twist_im, zero, zero]),
            ([amps[2] * np.float32(2 * share * share), zero, zero], [zero] * 3),
        ],
        stage_ref,
        values_ref,
    )

    def block(q):
        halves = []
        for s in range(2):
            total = [None] * (2 * blocks)
            for h in range(harmonics):
                at = pl.ds(q * LANES + (2 * h + s) * SUB, SUB)
                phase, a = values_ref[0, at, :LANES], values_ref[0, at, LANES:]
                w_phase, da = values_ref[1, at, :LANES], values_ref[1, at, LANES:]
                twist_re, twist_im = values_ref[2, at, :LANES], values_ref[2, at, LANES:]
                dda = values_ref[3, at, :LANES]
                z_re, z_im = cis_turns(frac(phase))
                w_re, w_im = cis_turns(frac(w_phase))
                for k in range(blocks):
                    terms = (a * z_re, a * z_im)
                    for i in range(2):
                        total[2 * k + i] = terms[i] if h == 0 else total[2 * k + i] + terms[i]
                    if k + 1 < blocks:
                        z_re, z_im = z_re * w_re - z_im * w_im, z_re * w_im + z_im * w_re
                        a = a + da
                    if k + 2 < blocks:
                        w_re, w_im = w_re * twist_re - w_im * twist_im, w_re * twist_im + w_im * twist_re
                        da = da + dda
            halves.append(total)
        row = q * SUB
        for i, template in enumerate(summed(halves)):
            here = i // 2 * LANES
            there = i % 2 * band_bins + here
            part = data_ref[i % 2 : i % 2 + 1, here : here + LANES]
            resid_ref[pl.ds(row, SUB), there : there + LANES] = part - template

    by_walkers(rec_ref.shape[0], evaluate, block)
    for part in range(2):
        lanes = slice(part * band_bins, (part + 1) * band_bins)
        weighted_ref[:, lanes] = (resid_ref[:, lanes] * noise_ref[0:1, :]).astype(BF16)


def slot_columns(bins, cols_ref):
    slots = bins.shape[1]
    cols_ref[...] = jnp.concatenate([bins.T, jnp.zeros((slots, LANES - SUB), F32)], axis=1)


def slot_wave(params, lane):
    rows = params.shape[0]
    amp, phase, slope, curve, start = (col(params, i, rows) for i in range(5))
    high = jnp.floor(start * np.float32(1.0 / LANES))
    low = start - high * np.float32(LANES)
    offset = lane - low
    wrapped = offset < 0.0
    j = jnp.where(wrapped, offset + np.float32(Q), offset)
    angle = phase + slope * j + curve * j * j
    c, s = cis_turns(turns(angle))
    y = (j + np.float32(0.5)) * np.float32(1.0 / Q) - np.float32(0.5)
    envelope = poly(y * y, COS1)
    scale = amp * (envelope * envelope)
    return scale * c, scale * s, wrapped, high


def wave_kernel(bins_ref, noise_ref, wave_ref, power_ref, cols_ref):
    slots = bins_ref.shape[1]
    band_bins = noise_ref.shape[1]
    blocks = band_bins // LANES
    slot_columns(bins_ref[...], cols_ref)
    rows = 2 * SUB
    lane = lane_iota(rows).astype(F32)

    def block(step, _):
        at = pl.ds(pl.multiple_of(step * rows, rows), rows)
        re, im, wrapped, high = slot_wave(cols_ref[at, :], lane)
        home = jnp.where(wrapped, high + 1.0, high)
        re_half, im_half = re.astype(BF16), im.astype(BF16)
        re, im = re_half.astype(F32), im_half.astype(F32)
        noise = jnp.zeros((rows, LANES), F32)
        for k in range(blocks + 1):
            inside = home == np.float32(k)
            if k < blocks:
                noise = jnp.where(inside, noise_ref[0:1, k * LANES : (k + 1) * LANES], noise)
            start = k * LANES if k < blocks else 2 * band_bins
            wave_ref[at, start : start + LANES] = jnp.where(inside, re, 0.0).astype(BF16)
            start += band_bins if k < blocks else LANES
            wave_ref[at, start : start + LANES] = jnp.where(inside, im, 0.0).astype(BF16)
        power_ref[at, :] = (re * re + im * im) * noise
        return 0

    lax.fori_loop(0, slots // rows, block, 0, unroll=4)


def fit_rows(band, bands):
    width = -(-bands // LANES) * LANES
    place = lax.broadcasted_iota(jnp.int32, (NCOEF, width), 1)
    order = lax.broadcasted_iota(jnp.int32, (NCOEF, width), 0)
    x = (2 * place + 1).astype(F32) * np.float32(1.0 / bands) - np.float32(1.0)
    term, after = jnp.ones_like(x), x
    basis = jnp.zeros_like(x)
    for degree in range(NCOEF):
        basis = jnp.where(order == degree, term, basis)
        term, after = after, np.float32(2.0) * x * after - term
    basis = jnp.where(place < bands, basis, 0.0)
    row = lax.broadcasted_iota(jnp.int32, (NCOEF, LANES), 0)
    lane = lax.broadcasted_iota(jnp.int32, (NCOEF, LANES), 1)
    gram = jnp.zeros((NCOEF, LANES), F32)
    for j in range(NCOEF):
        gram = jnp.where(lane == j, jnp.sum(basis * basis[j : j + 1, :], axis=1, keepdims=True), gram)
    side = basis
    for i in range(NCOEF):
        scale = np.float32(1.0) / jnp.sqrt(gram[i : i + 1, i : i + 1])
        upper = gram[i : i + 1, :] * scale
        factor = gram[:, i : i + 1] * scale
        solved = side[i : i + 1, :] * scale
        below = row > i
        gram = jnp.where(below, gram - factor * upper, jnp.where(row == i, upper, gram))
        side = jnp.where(order > i, side - factor * solved, jnp.where(order == i, solved, side))
    for i in reversed(range(NCOEF)):
        solved = side[i : i + 1, :] / gram[i : i + 1, i : i + 1]
        side = jnp.where(order < i, side - gram[:, i : i + 1] * solved, jnp.where(order == i, solved, side))
    mine = jnp.sum(jnp.where(place == band, side, 0.0), axis=1, keepdims=True)
    return jnp.sum(basis * mine, axis=0, keepdims=True)


OVER_LANES = (((1,), (1,)), ((), ()))


def accepted(corr, power):
    total = lax.dot_general(
        jnp.ones((SUB, LANES), F32), power, OVER_LANES, precision=lax.Precision.HIGHEST, preferred_element_type=F32
    )
    return jax.nn.sigmoid(corr - np.float32(0.5) * total[0:1, :])


def score_kernel(
    harmonics, blocks, weighted_ref, resid_ref, noise_ref, bins_ref, wave_ref, power_ref, rec_ref, extra_ref,
    cross_ref, cross_extra_ref, accept_ref, new_ref, log_ref,
    prev_ref, prev_power_ref, stage_ref, values_ref, edge_ref, rim_ref,
):
    walkers, own = weighted_ref.shape
    slots = wave_ref.shape[0]
    band_bins = own // 2
    last = blocks - 1
    span = cross_ref.shape[1]
    sources, extra = extra_ref.shape
    place = lax.axis_index("shard")
    first, final = place == 0, place == sources - 1

    below_rec = jnp.where(first, cross_ref[...], rec_ref[:, :span])
    above_rec = jnp.where(final, cross_ref[...], rec_ref[:, span:])
    source = lax.rem(place + 1, sources)
    rows = -(-3 * LANES // cross_extra_ref.shape[1])
    crossed = jnp.concatenate([cross_extra_ref[i : i + 1, :] for i in range(rows)], axis=1)
    above = jnp.where(final, crossed[:, : 3 * LANES], extra_ref[pl.ds(source, 1), : 3 * LANES])
    source = lax.rem(place + sources - 1, sources)
    below = extra_ref[pl.ds(source, 1), 3 * LANES :]
    rows = -(-below.shape[1] // cross_extra_ref.shape[1])
    crossed = jnp.concatenate([cross_extra_ref[i : i + 1, :] for i in range(rows)], axis=1)
    below = jnp.where(first, crossed[:, : below.shape[1]], below)

    bins = jnp.concatenate(
        [below[:, 3 * LANES + i * slots : 3 * LANES + (i + 1) * slots] for i in range(5)] + [jnp.zeros((3, slots), F32)],
        axis=0,
    )
    passes = (bins[4:5] > np.float32(band_bins - Q)) & (bins[0:1] != 0.0)
    flags = jnp.broadcast_to(jnp.where(passes, 1.0, 0.0), (2 * SUB, slots)).astype(BF16)
    row, column = (lax.broadcasted_iota(jnp.int32, (LANES, LANES), i) for i in range(2))
    upto = jnp.where(row <= column, 1.0, 0.0).astype(BF16)
    ranks = []
    for start in range(0, slots, LANES):
        rank = jnp.dot(flags[:, start : start + LANES], upto, preferred_element_type=F32)[0:1]
        ranks.append(rank + ranks[-1][:, LANES - 1 :] if ranks else rank)
    passing = jnp.max(ranks[-1]).astype(jnp.int32)
    rank = jnp.where(passes, jnp.concatenate(ranks, axis=1), 0.0)
    bin_pieces = [x.astype(BF16) for x in pieces(bins)]

    pairs = []
    for k, rec in ((last, below_rec), (0, above_rec)):
        amps, linear, reduced = coefficients(rec, harmonics * 2 * SUB, band_bins)
        pairs.append((phase_terms(k, band_bins, linear, reduced), amp_terms(k, band_bins, amps)))
    evaluate = evaluator(pairs, stage_ref, values_ref)

    def edge_block(q):
        halves = []
        for s in range(2):
            total = None
            for h in range(harmonics):
                at = pl.ds(q * LANES + (2 * h + s) * SUB, SUB)
                terms = []
                for i in range(2):
                    a = values_ref[i, at, LANES:]
                    terms += [a * x for x in cis_turns(frac(values_ref[i, at, :LANES]))]
                total = terms if h == 0 else [x + y for x, y in zip(total, terms, strict=True)]
            halves.append(total)
        for i, template in enumerate(summed(halves)):
            part = (below, above)[i // 2][:, i % 2 * LANES : (i % 2 + 1) * LANES]
            edge_ref[q * SUB : (q + 1) * SUB, i * LANES : (i + 1) * LANES] = part - template

    by_walkers(walkers // SUB, evaluate, edge_block)
    below_noise, above_noise = below[:, 2 * LANES : 3 * LANES], above[:, 2 * LANES : 3 * LANES]
    noise = jnp.concatenate([below_noise, below_noise, above_noise, above_noise], axis=1)
    rim_ref[...] = (edge_ref[...] * noise).astype(BF16)

    mine = jnp.concatenate([weighted_ref[:, :LANES], weighted_ref[:, band_bins : band_bins + LANES]], axis=1)
    tail = jnp.concatenate([rim_ref[:, : 2 * LANES], mine], axis=1)
    group = 2 * SUB
    lane = lane_iota(group).astype(F32)
    first_noise = noise_ref[0:1, :LANES]
    chunk = prev_ref.shape[0]

    def spill(index):
        place = lax.broadcasted_iota(jnp.int32, (chunk, slots), 0) + (index * chunk + 1)
        chosen = jnp.where(rank == place.astype(F32), 1.0, 0.0).astype(BF16)
        cols = [lax.dot_general(chosen, x, OVER_LANES, preferred_element_type=F32) for x in bin_pieces]
        cols = cols[0] + cols[1] + cols[2]
        for start in range(0, chunk, group):
            at = slice(start, start + group)
            re, im, wrapped, _ = slot_wave(cols[at, :], lane)
            re, im = re.astype(BF16).astype(F32), im.astype(BF16).astype(F32)
            prev_power_ref[at, :] = (re * re + im * im) * jnp.where(wrapped, first_noise, below_noise)
            prev_ref[at, :LANES] = jnp.where(wrapped, 0.0, re).astype(BF16)
            prev_ref[at, LANES : 2 * LANES] = jnp.where(wrapped, 0.0, im).astype(BF16)
            prev_ref[at, 2 * LANES : 3 * LANES] = jnp.where(wrapped, re, 0.0).astype(BF16)
            prev_ref[at, 3 * LANES :] = jnp.where(wrapped, im, 0.0).astype(BF16)
        corr = lax.dot_general(tail, prev_ref[...], OVER_LANES, preferred_element_type=F32)
        half = accepted(corr, prev_power_ref[...]).astype(BF16)
        return jnp.dot(half, prev_ref[:, 2 * LANES :], preferred_element_type=F32)

    carried = spill(0)
    corr = lax.dot_general(weighted_ref[...], wave_ref[:, :own], OVER_LANES, preferred_element_type=F32)
    corr += lax.dot_general(rim_ref[:, 2 * LANES :], wave_ref[:, own:], OVER_LANES, preferred_element_type=F32)
    rim = wave_ref[:, own:].astype(F32)
    re, im = rim[:, :LANES], rim[:, LANES:]
    accept = accepted(corr, power_ref[...] + (re * re + im * im) * above_noise)
    accept = jnp.where(bins_ref[5:6, :] > 0.0, accept, 0.0)
    accept_ref[...] = accept
    half = accept.astype(BF16)
    carried = lax.fori_loop(1, (passing + chunk - 1) // chunk, lambda i, total: total + spill(i), carried)
    squares = jnp.zeros((walkers, LANES), F32)
    width = 2 * LANES
    for start in range(0, own, width):
        lanes = slice(start, start + width)
        new = resid_ref[:, lanes] - jnp.dot(half, wave_ref[:, lanes], preferred_element_type=F32)
        parts = [new[:, i : i + LANES] for i in range(0, width, LANES)]
        if start % band_bins == 0:
            part = start // band_bins
            parts[0] -= carried[:, part * LANES : (part + 1) * LANES]
        for i, piece in enumerate(parts):
            new_ref[:, start + i * LANES : start + (i + 1) * LANES] = piece
            squares += piece * piece
    total = jnp.sum(jnp.sum(squares, axis=0, keepdims=True), axis=1, keepdims=True)
    log_power = jnp.log(total * np.float32(1.0 / (walkers * own)) + np.float32(1e-6))
    log_ref[:, 0, :] = jnp.broadcast_to(log_power, (log_ref.shape[0], log_ref.shape[2]))


def output_kernel(bands, accept_ref, new_ref, prob_ref, out_ref, fit_ref):
    _, own = new_ref.shape
    half = own // 2
    prob_ref[...] = accept_ref[...]
    for part in range(2):
        out_ref[:, part, :] = new_ref[:, part * half : (part + 1) * half]
    fit = fit_rows(lax.axis_index(BOTH), bands)
    fit = jnp.broadcast_to(fit, (SUB, fit.shape[1])).T
    fit_ref[...] = jnp.broadcast_to(fit[:bands, 0:1], (bands, LANES))


def call(kernel, outs, args, scratch=(), smem=0, flops=0, name=None, hbm=False, last_any=False, alias=None):
    vmem = pl.BlockSpec(memory_space=pltpu.VMEM)
    rest = vmem
    if hbm:
        rest = pl.BlockSpec(memory_space=pl.ANY)
        args = [pltpu.with_memory_space_constraint(x, pltpu.HBM) if x.dtype != jnp.int32 or x.ndim > 1 else x for x in args]
    specs = [pl.BlockSpec(memory_space=pltpu.SMEM)] * smem + [rest] * (len(args) - smem)
    if last_any:
        specs[-1] = pl.BlockSpec(memory_space=pl.ANY)
    return pl.pallas_call(
        kernel,
        out_shape=outs,
        in_specs=specs,
        out_specs=[vmem] * len(outs),
        scratch_shapes=scratch,
        compiler_params=pltpu.CompilerParams(vmem_limit_bytes=16 * 2**20),
        cost_estimate=pl.CostEstimate(flops=flops, bytes_accessed=2**20, transcendentals=0),
        name=name,
        input_output_aliases=alias or {},
    )(*args)


def shape(dims, dtype):
    return jax.ShapeDtypeStruct(dims, dtype)


def local(
    data,
    inv_noise,
    mbh_amp,
    mbh_phase,
    bin_amp,
    bin_phase,
    bin_slope,
    bin_curve,
    bin_start,
    bin_count,
):
    band_bins = data.shape[1]
    slots = bin_amp.shape[1]
    rows, harmonics, powers, peers = mbh_amp.shape
    groups = lax.axis_size("group")
    walkers = rows * peers // 2
    bands = lax.axis_size(BOTH)
    own = 2 * band_bins

    span = padded(2 * powers * harmonics * rows)
    extra = 6 * LANES + 5 * slots
    cross_rows = -(-(extra - 3 * LANES) // span // SUB) * SUB
    packed, bins, data, noise = call(
        pack_kernel,
        [
            shape((peers, 1, 3 * span + extra), F32),
            shape((SUB, slots), F32),
            shape((2, band_bins), F32),
            shape((1, band_bins), F32),
        ],
        [
            mbh_amp.transpose(1, 2, 3, 0), mbh_phase.transpose(1, 2, 3, 0), data, inv_noise.reshape(-1, LANES),
            bin_amp, bin_phase, bin_slope, bin_curve, bin_start, bin_count,
        ],
        scratch=[
            pltpu.VMEM((harmonics, powers, peers, rows), F32),
            pltpu.VMEM((harmonics, powers, peers, rows), F32),
            pltpu.VMEM((4, 1, slots), F32),
            pltpu.VMEM((1, slots), jnp.int32),
            pltpu.VMEM((band_bins // LANES, LANES), BF16),
            pltpu.SMEM((1,), jnp.int32),
            pltpu.SemaphoreType.DMA((10,)),
        ],
        hbm=True,
        name="pack",
    )
    received = lax.all_to_all(packed, "shard", split_axis=0, concat_axis=0, tiled=True)
    received = received.reshape(peers, -1)
    wave, slot_power = call(
        wave_kernel,
        [shape((slots, own + 2 * LANES), BF16), shape((slots, LANES), F32)],
        [bins, noise],
        scratch=[pltpu.VMEM((slots, LANES), F32)],
        flops=10**9,
        name="waves",
    )
    (to_cross,) = call(
        cross_kernel,
        [shape((peers + cross_rows, span), F32)],
        [received, slot_power],
        last_any=True,
        name="cross",
    )
    pairs = [(g * peers, (g + 1) * peers) for g in range(groups - 1)]
    pairs += [(g * peers + peers - 1, (g - 1) * peers + peers - 1) for g in range(1, groups)]
    crossed = lax.ppermute(to_cross, BOTH, pairs)

    extras = received[:, 3 * span :]
    parts = [received[:, i * span : (i + 1) * span] for i in range(3)] + [crossed[:peers]]
    crossed_extra = crossed[peers:]
    if rows != 2 * SUB:

        def by_eight(x):
            x = x[:, : 2 * powers * harmonics * rows].reshape(peers, 2 * powers, harmonics, rows)
            x = x.transpose(1, 2, 0, 3).reshape(2 * powers, harmonics, walkers // SUB, SUB, 2)
            x = x.transpose(2, 0, 1, 4, 3).reshape(walkers // SUB, 2 * powers * harmonics * 2 * SUB)
            return jnp.pad(x, ((0, 0), (0, padded(x.shape[1]) - x.shape[1])))

        parts = [by_eight(x) for x in parts]

    resid, weighted = call(
        functools.partial(template_kernel, harmonics),
        [shape((walkers, own), F32), shape((walkers, own), BF16)],
        [parts[0], data, noise],
        scratch=[
            pltpu.VMEM((4, 2 * QUAD, walkers // SUB, LANES), F32),
            pltpu.VMEM((4, walkers // SUB * LANES, 2 * LANES), F32),
        ],
        flops=10**9,
        name="template",
    )
    accept, updated, log_power = call(
        functools.partial(score_kernel, harmonics, band_bins // LANES),
        [shape((walkers, slots), F32), shape((walkers, own), F32), shape((bands, 1, LANES), F32)],
        [
            weighted, resid, noise, bins, wave, slot_power, jnp.concatenate(parts[1:3], axis=1), extras,
            parts[3], crossed_extra,
        ],
        scratch=[
            pltpu.VMEM((min(slots, LANES), 4 * LANES), BF16),
            pltpu.VMEM((min(slots, LANES), LANES), F32),
            pltpu.VMEM((2, 2 * QUAD, walkers // SUB, LANES), F32),
            pltpu.VMEM((2, walkers // SUB * LANES, 2 * LANES), F32),
            pltpu.VMEM((walkers, 4 * LANES), F32),
            pltpu.VMEM((walkers, 4 * LANES), BF16),
        ],
        name="scores",
    )
    log_powers = lax.all_to_all(log_power, BOTH, split_axis=0, concat_axis=0, tiled=True)
    accept_prob, residual_new, fit = call(
        functools.partial(output_kernel, bands),
        [shape((walkers, slots), F32), shape((walkers, 2, band_bins), F32), shape((bands, LANES), F32)],
        [accept, updated],
        name="outputs",
    )
    noise_fit = jnp.sum(fit * log_powers[:, 0, :], axis=0)[:1]
    return (accept_prob, residual_new, noise_fit)


def solution(mesh):
    in_specs = (
        P(None, BOTH),
        P(BOTH),
        P("shard", None, None, "group"),
        P("shard", None, None, "group"),
        P(BOTH, None),
        P(BOTH, None),
        P(BOTH, None),
        P(BOTH, None),
        P(BOTH, None),
        P(BOTH),
    )
    out_specs = (P(None, BOTH), P(None, None, BOTH), P(BOTH))
    return jax.shard_map(local, mesh=mesh, in_specs=in_specs, out_specs=out_specs, check_vma=False)
```

```python
import functools
import math

import jax
import jax.numpy as jnp
import numpy as np
from jax import lax
from jax.experimental import pallas as pl
from jax.experimental.pallas import tpu as pltpu
from jax.sharding import PartitionSpec as P

Q = 128
NCOEF = 8
LANES = 128
SUB = 8
F32 = jnp.float32
BF16 = jnp.bfloat16
BOTH = ("group", "shard")
OVER_LANES = (((1,), (1,)), ((), ()))

INV_TAU = np.float32(1.0 / (2.0 * math.pi))
TAU_A = np.float32(round(2.0 * math.pi * 512) / 512)
TAU_B = np.float32(round((2.0 * math.pi - float(TAU_A)) * 2**22) / 2**22)
TAU_C = np.float32(2.0 * math.pi - float(TAU_A) - float(TAU_B))
MAGIC = np.float32(1.5 * 2**23)
SIN2 = (6.283185160089475, -10.33541375785372, 5.100062754574036, -1.1960903483123309, 0.15444025802555503)
COS1 = (0.9999999534666666, -4.934792858675247, 4.058411914166824, -1.3318801612473732, 0.2196967986012024)


def nearest(x):
    return (x + MAGIC) - MAGIC


def padded(count):
    return -(-count // LANES) * LANES


def poly(y, coefs):
    total = np.float32(coefs[-1])
    for c in coefs[-2::-1]:
        total = total * y + np.float32(c)
    return total


def cis_turns(r):
    y = r * r
    s2 = poly(y, SIN2) * r
    c1 = poly(y, COS1)
    return np.float32(1.0) - np.float32(0.5) * (s2 * s2), s2 * c1


def turns(angle):
    n = nearest(angle * INV_TAU)
    return (((angle - n * TAU_A) - n * TAU_B) - n * TAU_C) * INV_TAU


def frac(t):
    return t - nearest(t)


def col(x, lane, rows=SUB):
    return jnp.broadcast_to(x[:, lane : lane + 1], (rows, LANES))


def lane_iota(rows=SUB):
    return lax.broadcasted_iota(jnp.int32, (rows, LANES), 1)


def pack_kernel(
    amp_hbm, phase_hbm, data_hbm, noise_hbm, bin_amp_hbm, bin_phase_hbm, bin_slope_hbm, bin_curve_hbm,
    bin_start_hbm, count_hbm, packed_ref, bins_ref, data_ref, noise_ref,
    amp_ref, phase_ref, rows_ref, start_ref, raw_noise_ref, count_ref, sems,
):
    copies = [
        pltpu.make_async_copy(source, target, sems.at[i])
        for i, (source, target) in enumerate(
            [
                (amp_hbm, amp_ref),
                (phase_hbm, phase_ref),
                (count_hbm, count_ref),
                (bin_amp_hbm, rows_ref.at[0]),
                (bin_phase_hbm, rows_ref.at[1]),
                (bin_slope_hbm, rows_ref.at[2]),
                (bin_curve_hbm, rows_ref.at[3]),
                (bin_start_hbm, start_ref),
                (data_hbm, data_ref),
                (noise_hbm, raw_noise_ref),
            ]
        )
    ]
    for copy in copies:
        copy.start()
    harmonics, powers, peers, rows = amp_ref.shape
    span = padded(2 * powers * harmonics * rows)
    slots = bins_ref.shape[1]
    band_bins = data_ref.shape[1]
    for copy in copies[2:]:
        copy.wait()
    live = lax.broadcasted_iota(jnp.int32, (1, slots), 1) < count_ref[0]
    amp = jnp.where(live, rows_ref[0], 0.0)
    slot_rows = [amp, rows_ref[1], rows_ref[2], rows_ref[3], start_ref[...].astype(F32)]
    bins_ref[...] = jnp.concatenate([*slot_rows, live.astype(F32), jnp.zeros((2, slots), F32)], axis=0)
    raw_noise = raw_noise_ref[...].astype(F32)
    noise = jnp.concatenate([raw_noise[i : i + 1] for i in range(raw_noise.shape[0])], axis=1)
    noise_ref[...] = noise
    start = 3 * span
    for lanes in (slice(0, LANES), slice(band_bins - LANES, band_bins)):
        for row in (data_ref[0:1, lanes], data_ref[1:2, lanes], noise[:, lanes]):
            packed_ref[:, 0, start : start + LANES] = jnp.broadcast_to(row, (peers, LANES))
            start += LANES
    for row in slot_rows:
        packed_ref[:, 0, start : start + slots] = jnp.broadcast_to(row, (peers, slots))
        start += slots
    for copy in copies[:2]:
        copy.wait()
    parts = [ref[h, power] for ref in (amp_ref, phase_ref) for power in range(powers) for h in range(harmonics)]
    if span > 2 * powers * harmonics * rows:
        parts.append(jnp.zeros((peers, span - 2 * powers * harmonics * rows), F32))
    packed = jnp.concatenate(parts, axis=1)
    if rows == 2 * SUB:
        lane = lax.broadcasted_iota(jnp.int32, (peers, LANES), 1)
        order = lane - lane % (2 * SUB) + lane % SUB * 2 + lane % (2 * SUB) // SUB
        blocks = [packed[:, i : i + LANES] for i in range(0, span, LANES)]
        blocks = [jnp.take_along_axis(x, order, axis=1, mode="promise_in_bounds") for x in blocks]
        packed = jnp.concatenate(blocks, axis=1)
    packed_ref[:, 0, :span] = packed
    packed_ref[:, 0, span : 2 * span] = jnp.concatenate([packed[-1:], packed[:-1]], axis=0)
    packed_ref[:, 0, 2 * span : 3 * span] = jnp.concatenate([packed[1:], packed[:1]], axis=0)


def cross_kernel(rec_ref, _, out_ref):
    peers = rec_ref.shape[0]
    span = out_ref.shape[1]
    first = lax.axis_index("shard") == 0
    out_ref[:peers, :] = jnp.where(first, rec_ref[:, span : 2 * span], rec_ref[:, 2 * span : 3 * span])
    start = 3 * span
    rim = rec_ref[0:1, start : start + 3 * LANES]
    start += 3 * LANES
    row = rec_ref[peers - 1 : peers, start:]
    row = jnp.concatenate([jnp.where(first, row[:, : 3 * LANES], rim), row[:, 3 * LANES :]], axis=1)
    for i, at in enumerate(range(0, row.shape[1], span)):
        lanes = min(span, row.shape[1] - at)
        out_ref[peers + i : peers + i + 1, :lanes] = row[:, at : at + lanes]


def coefficients(rec, width, band_bins):
    share = LANES / band_bins
    fill = jnp.zeros((rec.shape[0], LANES - width), F32)
    terms = [jnp.concatenate([rec[:, k * width : (k + 1) * width], fill], axis=1) for k in range(6)]
    amps, (p0, p1, p2) = terms[:3], terms[3:]
    return amps, (p1, p2), (turns(p0), turns(p1 * np.float32(share)), turns(p2 * np.float32(share * share)))


def phase_terms(k, band_bins, linear, reduced):
    p1, p2 = linear
    f0, f1, f2 = reduced
    share = LANES / band_bins
    const = frac(f0 + np.float32(k) * f1 + np.float32(k * k) * f2)
    slope = (p1 + p2 * np.float32(2 * k * share)) * np.float32(1.0 / band_bins) * INV_TAU
    return [const, slope, p2 * np.float32(1.0 / band_bins**2) * INV_TAU]


def amp_terms(k, band_bins, amps):
    a0, a1, a2 = amps
    at = k * LANES / band_bins
    slope = (a1 + a2 * np.float32(2 * at)) * np.float32(1.0 / band_bins)
    return [a0 + (a1 + a2 * np.float32(at)) * np.float32(at), slope, a2 * np.float32(1.0 / band_bins**2)]


def pieces(x):
    high = x.astype(BF16).astype(F32)
    rest = x - high
    middle = rest.astype(BF16).astype(F32)
    return [high, middle, (rest - middle).astype(BF16).astype(F32)]


QUAD = 16


def quad_rows(terms):
    terms = [pieces(x) for x in terms]
    rows = [*terms[0], *terms[1], *terms[2], *terms[2]]
    return rows + [jnp.zeros_like(rows[0])] * (QUAD - len(rows))


def lane_powers():
    row = lax.broadcasted_iota(jnp.int32, (QUAD, LANES), 0)
    lane = lax.broadcasted_iota(jnp.int32, (QUAD, LANES), 1)
    low = lane * lane % LANES
    table = jnp.where(row < 3, 1, jnp.where(row < 6, lane, jnp.where(row < 9, lane * lane - low, low)))
    table = jnp.where(row < 12, table, 0).astype(F32)
    zero = jnp.zeros((QUAD, LANES), F32)
    upper = jnp.concatenate([table, zero], axis=1)
    lower = jnp.concatenate([zero, table], axis=1)
    return jnp.concatenate([upper, lower], axis=0).astype(BF16)


def evaluator(pairs, stage_ref, values_ref):
    table = lane_powers()
    for pair, (first, second) in enumerate(pairs):
        for i, row in enumerate(quad_rows(first) + quad_rows(second)):
            stage_ref[pair, i] = row

    def evaluate(q):
        for pair in range(len(pairs)):
            rows = stage_ref[pair, :, q, :].T.astype(BF16)
            values_ref[pair, q * LANES : (q + 1) * LANES, :] = jnp.dot(rows, table, preferred_element_type=F32)

    return evaluate


def by_walkers(count, evaluate, block):
    evaluate(0)
    for q in range(count):
        if q + 1 < count:
            evaluate(q + 1)
        block(q)


def summed(halves):
    return [a.astype(BF16).astype(F32) + b.astype(BF16).astype(F32) for a, b in zip(*halves, strict=True)]


def template_kernel(harmonics, rec_ref, data_ref, noise_ref, resid_ref, weighted_ref, stage_ref, values_ref):
    band_bins = data_ref.shape[1]
    blocks = band_bins // LANES
    share = LANES / band_bins
    amps, linear, reduced = coefficients(rec_ref, harmonics * 2 * SUB, band_bins)
    _, f1, f2 = reduced
    zero = jnp.zeros_like(f1)
    twist_re, twist_im = cis_turns(frac(np.float32(2.0) * f2))
    step = [frac(f1 + f2), linear[1] * np.float32(2 * share / band_bins) * INV_TAU, zero]
    now, then = amp_terms(0, band_bins, amps), amp_terms(1, band_bins, amps)
    grow = [then[0] - now[0], amps[2] * np.float32(2 * share / band_bins), zero]
    evaluate = evaluator(
        [
            (phase_terms(0, band_bins, linear, reduced), now),
            (step, grow),
            ([twist_re, zero, zero], [twist_im, zero, zero]),
            ([amps[2] * np.float32(2 * share * share), zero, zero], [zero] * 3),
        ],
        stage_ref,
        values_ref,
    )

    def block(q):
        halves = []
        for s in range(2):
            total = [None] * (2 * blocks)
            for h in range(harmonics):
                at = pl.ds(q * LANES + (2 * h + s) * SUB, SUB)
                phase, a = values_ref[0, at, :LANES], values_ref[0, at, LANES:]
                w_phase, da = values_ref[1, at, :LANES], values_ref[1, at, LANES:]
                twist_re, twist_im = values_ref[2, at, :LANES], values_ref[2, at, LANES:]
                dda = values_ref[3, at, :LANES]
                z_re, z_im = cis_turns(frac(phase))
                w_re, w_im = cis_turns(frac(w_phase))
                for k in range(blocks):
                    terms = (a * z_re, a * z_im)
                    for i in range(2):
                        total[2 * k + i] = terms[i] if h == 0 else total[2 * k + i] + terms[i]
                    if k + 1 < blocks:
                        z_re, z_im = z_re * w_re - z_im * w_im, z_re * w_im + z_im * w_re
                        a = a + da
                    if k + 2 < blocks:
                        w_re, w_im = w_re * twist_re - w_im * twist_im, w_re * twist_im + w_im * twist_re
                        da = da + dda
            halves.append(total)
        row = q * SUB
        for i, template in enumerate(summed(halves)):
            here = i // 2 * LANES
            there = i % 2 * band_bins + here
            part = data_ref[i % 2 : i % 2 + 1, here : here + LANES]
            resid_ref[pl.ds(row, SUB), there : there + LANES] = part - template

    by_walkers(rec_ref.shape[0], evaluate, block)
    for part in range(2):
        lanes = slice(part * band_bins, (part + 1) * band_bins)
        weighted_ref[:, lanes] = (resid_ref[:, lanes] * noise_ref[0:1, :]).astype(BF16)


def slot_columns(bins, cols_ref):
    slots = bins.shape[1]
    cols_ref[...] = jnp.concatenate([bins.T, jnp.zeros((slots, LANES - SUB), F32)], axis=1)


def slot_wave(params, lane):
    rows = params.shape[0]
    amp, phase, slope, curve, start = (col(params, i, rows) for i in range(5))
    high = jnp.floor(start * np.float32(1.0 / LANES))
    low = start - high * np.float32(LANES)
    offset = lane - low
    wrapped = offset < 0.0
    j = jnp.where(wrapped, offset + np.float32(Q), offset)
    angle = phase + slope * j + curve * j * j
    c, s = cis_turns(turns(angle))
    y = (j + np.float32(0.5)) * np.float32(1.0 / Q) - np.float32(0.5)
    envelope = poly(y * y, COS1)
    scale = amp * (envelope * envelope)
    return scale * c, scale * s, wrapped, high


def wave_kernel(bins_ref, noise_ref, wave_ref, total_ref, rim_ref, cols_ref, power_ref):
    slots = bins_ref.shape[1]
    band_bins = noise_ref.shape[1]
    blocks = band_bins // LANES
    slot_columns(bins_ref[...], cols_ref)
    rows = 2 * SUB
    lane = lane_iota(rows).astype(F32)

    def block(step, _):
        at = pl.ds(pl.multiple_of(step * rows, rows), rows)
        re, im, wrapped, high = slot_wave(cols_ref[at, :], lane)
        home = jnp.where(wrapped, high + 1.0, high)
        re_half, im_half = re.astype(BF16), im.astype(BF16)
        re, im = re_half.astype(F32), im_half.astype(F32)
        noise = jnp.zeros((rows, LANES), F32)
        for k in range(blocks + 1):
            inside = home == np.float32(k)
            if k < blocks:
                noise = jnp.where(inside, noise_ref[0:1, k * LANES : (k + 1) * LANES], noise)
            start = k * LANES if k < blocks else 2 * band_bins
            wave_ref[at, start : start + LANES] = jnp.where(inside, re, 0.0).astype(BF16)
            start += band_bins if k < blocks else LANES
            wave_ref[at, start : start + LANES] = jnp.where(inside, im, 0.0).astype(BF16)
        squares = re * re + im * im
        power_ref[at, :] = squares * noise
        for i, piece in enumerate(pieces(jnp.where(home == np.float32(blocks), squares, 0.0))):
            rim_ref[at, i * LANES : (i + 1) * LANES] = piece.astype(BF16)
        return 0

    lax.fori_loop(0, slots // rows, block, 0, unroll=4)
    total_ref[...] = row_sums(power_ref[...])


def fit_rows(band, bands):
    width = -(-bands // LANES) * LANES
    place = lax.broadcasted_iota(jnp.int32, (NCOEF, width), 1)
    order = lax.broadcasted_iota(jnp.int32, (NCOEF, width), 0)
    x = (2 * place + 1).astype(F32) * np.float32(1.0 / bands) - np.float32(1.0)
    term, after = jnp.ones_like(x), x
    basis = jnp.zeros_like(x)
    for degree in range(NCOEF):
        basis = jnp.where(order == degree, term, basis)
        term, after = after, np.float32(2.0) * x * after - term
    basis = jnp.where(place < bands, basis, 0.0)
    row = lax.broadcasted_iota(jnp.int32, (NCOEF, LANES), 0)
    lane = lax.broadcasted_iota(jnp.int32, (NCOEF, LANES), 1)
    gram = jnp.zeros((NCOEF, LANES), F32)
    for j in range(NCOEF):
        gram = jnp.where(lane == j, jnp.sum(basis * basis[j : j + 1, :], axis=1, keepdims=True), gram)
    side = basis
    for i in range(NCOEF):
        scale = np.float32(1.0) / jnp.sqrt(gram[i : i + 1, i : i + 1])
        upper = gram[i : i + 1, :] * scale
        factor = gram[:, i : i + 1] * scale
        solved = side[i : i + 1, :] * scale
        below = row > i
        gram = jnp.where(below, gram - factor * upper, jnp.where(row == i, upper, gram))
        side = jnp.where(order > i, side - factor * solved, jnp.where(order == i, solved, side))
    for i in reversed(range(NCOEF)):
        solved = side[i : i + 1, :] / gram[i : i + 1, i : i + 1]
        side = jnp.where(order < i, side - gram[:, i : i + 1] * solved, jnp.where(order == i, solved, side))
    mine = jnp.sum(jnp.where(place == band, side, 0.0), axis=1, keepdims=True)
    return jnp.sum(basis * mine, axis=0, keepdims=True)


def row_sums(x):
    ones = jnp.ones((SUB, LANES), F32)
    return lax.dot_general(ones, x, OVER_LANES, precision=lax.Precision.HIGHEST, preferred_element_type=F32)


def accepted(corr, total):
    return jax.nn.sigmoid(corr - np.float32(0.5) * total)


def score_kernel(
    harmonics, blocks, weighted_ref, resid_ref, noise_ref, bins_ref, wave_ref, total_ref, rim_squares_ref, rec_ref, extra_ref,
    cross_ref, cross_extra_ref, accept_ref, new_ref, log_ref,
    prev_ref, prev_power_ref, stage_ref, values_ref, edge_ref, rim_ref,
):
    walkers, own = weighted_ref.shape
    slots = wave_ref.shape[0]
    band_bins = own // 2
    last = blocks - 1
    span = cross_ref.shape[1]
    sources, extra = extra_ref.shape
    place = lax.axis_index("shard")
    first, final = place == 0, place == sources - 1

    below_rec = jnp.where(first, cross_ref[...], rec_ref[:, :span])
    above_rec = jnp.where(final, cross_ref[...], rec_ref[:, span:])
    source = lax.rem(place + 1, sources)
    rows = -(-3 * LANES // cross_extra_ref.shape[1])
    crossed = jnp.concatenate([cross_extra_ref[i : i + 1, :] for i in range(rows)], axis=1)
    above = jnp.where(final, crossed[:, : 3 * LANES], extra_ref[pl.ds(source, 1), : 3 * LANES])
    source = lax.rem(place + sources - 1, sources)
    below = extra_ref[pl.ds(source, 1), 3 * LANES :]
    rows = -(-below.shape[1] // cross_extra_ref.shape[1])
    crossed = jnp.concatenate([cross_extra_ref[i : i + 1, :] for i in range(rows)], axis=1)
    below = jnp.where(first, crossed[:, : below.shape[1]], below)

    bins = jnp.concatenate(
        [below[:, 3 * LANES + i * slots : 3 * LANES + (i + 1) * slots] for i in range(5)] + [jnp.zeros((3, slots), F32)],
        axis=0,
    )
    passes = (bins[4:5] > np.float32(band_bins - Q)) & (bins[0:1] != 0.0)
    flags = jnp.broadcast_to(jnp.where(passes, 1.0, 0.0), (2 * SUB, slots)).astype(BF16)
    row, column = (lax.broadcasted_iota(jnp.int32, (LANES, LANES), i) for i in range(2))
    upto = jnp.where(row <= column, 1.0, 0.0).astype(BF16)
    ranks = []
    for start in range(0, slots, LANES):
        rank = jnp.dot(flags[:, start : start + LANES], upto, preferred_element_type=F32)[0:1]
        ranks.append(rank + ranks[-1][:, LANES - 1 :] if ranks else rank)
    passing = jnp.max(ranks[-1]).astype(jnp.int32)
    rank = jnp.where(passes, jnp.concatenate(ranks, axis=1), 0.0)
    bin_pieces = [x.astype(BF16) for x in pieces(bins)]

    pairs = []
    for k, rec in ((last, below_rec), (0, above_rec)):
        amps, linear, reduced = coefficients(rec, harmonics * 2 * SUB, band_bins)
        pairs.append((phase_terms(k, band_bins, linear, reduced), amp_terms(k, band_bins, amps)))
    evaluate = evaluator(pairs, stage_ref, values_ref)

    step = own // (walkers // SUB)
    corr = [jnp.zeros((walkers, slots), F32)]

    def edge_block(q):
        lanes = slice(q * step, (q + 1) * step)
        corr[0] += lax.dot_general(weighted_ref[:, lanes], wave_ref[:, lanes], OVER_LANES, preferred_element_type=F32)
        halves = []
        for s in range(2):
            total = None
            for h in range(harmonics):
                at = pl.ds(q * LANES + (2 * h + s) * SUB, SUB)
                terms = []
                for i in range(2):
                    a = values_ref[i, at, LANES:]
                    terms += [a * x for x in cis_turns(frac(values_ref[i, at, :LANES]))]
                total = terms if h == 0 else [x + y for x, y in zip(total, terms, strict=True)]
            halves.append(total)
        for i, template in enumerate(summed(halves)):
            part = (below, above)[i // 2][:, i % 2 * LANES : (i % 2 + 1) * LANES]
            edge_ref[q * SUB : (q + 1) * SUB, i * LANES : (i + 1) * LANES] = part - template

    by_walkers(walkers // SUB, evaluate, edge_block)
    below_noise, above_noise = below[:, 2 * LANES : 3 * LANES], above[:, 2 * LANES : 3 * LANES]
    noise = jnp.concatenate([below_noise, below_noise, above_noise, above_noise], axis=1)
    rim_ref[...] = (edge_ref[...] * noise).astype(BF16)

    corr = corr[0] + lax.dot_general(rim_ref[:, 2 * LANES :], wave_ref[:, own:], OVER_LANES, preferred_element_type=F32)
    noise = jnp.broadcast_to(jnp.concatenate([above_noise] * 3, axis=1), (2 * SUB, 3 * LANES)).astype(BF16)
    total = lax.dot_general(noise, rim_squares_ref[...], OVER_LANES, preferred_element_type=F32)
    accept = accepted(corr, total_ref[0:1, :] + total[0:1, :])
    accept = jnp.where(bins_ref[5:6, :] > 0.0, accept, 0.0)
    accept_ref[...] = accept
    half = accept.astype(BF16)

    mine = jnp.concatenate([weighted_ref[:, :LANES], weighted_ref[:, band_bins : band_bins + LANES]], axis=1)
    tail = jnp.concatenate([rim_ref[:, : 2 * LANES], mine], axis=1)
    group = 2 * SUB
    lane = lane_iota(group).astype(F32)
    first_noise = noise_ref[0:1, :LANES]
    chunk = prev_ref.shape[0]

    def chosen_slots(index):
        place = lax.broadcasted_iota(jnp.int32, (chunk, slots), 0) + (index * chunk + 1)
        chosen = jnp.where(rank == place.astype(F32), 1.0, 0.0).astype(BF16)
        cols = [lax.dot_general(chosen, x, OVER_LANES, preferred_element_type=F32) for x in bin_pieces]
        return cols[0] + cols[1] + cols[2]

    def fill(cols, start):
        at = slice(start, start + group)
        re, im, wrapped, _ = slot_wave(cols[at, :], lane)
        re, im = re.astype(BF16).astype(F32), im.astype(BF16).astype(F32)
        prev_power_ref[at, :] = (re * re + im * im) * jnp.where(wrapped, first_noise, below_noise)
        prev_ref[at, :LANES] = jnp.where(wrapped, 0.0, re).astype(BF16)
        prev_ref[at, LANES : 2 * LANES] = jnp.where(wrapped, 0.0, im).astype(BF16)
        prev_ref[at, 2 * LANES : 3 * LANES] = jnp.where(wrapped, re, 0.0).astype(BF16)
        prev_ref[at, 3 * LANES :] = jnp.where(wrapped, im, 0.0).astype(BF16)

    def spilled():
        corr = lax.dot_general(tail, prev_ref[...], OVER_LANES, preferred_element_type=F32)
        half = accepted(corr, row_sums(prev_power_ref[...])[0:1, :]).astype(BF16)
        return jnp.dot(half, prev_ref[:, 2 * LANES :], preferred_element_type=F32)

    def spill(index, carried):
        cols = chosen_slots(index)
        for start in range(0, chunk, group):
            fill(cols, start)
        return carried + spilled()

    squares = [jnp.zeros((walkers, LANES), F32)]
    width = 2 * LANES

    def update(start, carried=None):
        lanes = slice(start, start + width)
        new = resid_ref[:, lanes] - jnp.dot(half, wave_ref[:, lanes], preferred_element_type=F32)
        parts = [new[:, i : i + LANES] for i in range(0, width, LANES)]
        if carried is not None:
            part = start // band_bins
            parts[0] -= carried[:, part * LANES : (part + 1) * LANES]
        for i, piece in enumerate(parts):
            new_ref[:, start + i * LANES : start + (i + 1) * LANES] = piece
            squares[0] += piece * piece

    cols = chosen_slots(0)
    fills = list(range(0, chunk, group))
    starts = [start for start in range(0, own, width) if start % band_bins]
    for i in range(max(len(fills), len(starts))):
        if i < len(starts):
            update(starts[i])
        if i < len(fills):
            fill(cols, fills[i])
    carried = lax.fori_loop(1, (passing + chunk - 1) // chunk, spill, spilled())
    update(0, carried)
    update(band_bins, carried)
    squares = squares[0]
    total = jnp.sum(jnp.sum(squares, axis=0, keepdims=True), axis=1, keepdims=True)
    log_power = jnp.log(total * np.float32(1.0 / (walkers * own)) + np.float32(1e-6))
    log_ref[:, 0, :] = jnp.broadcast_to(log_power, (log_ref.shape[0], log_ref.shape[2]))


def output_kernel(bands, accept_ref, new_ref, prob_ref, out_ref, fit_ref):
    _, own = new_ref.shape
    half = own // 2
    prob_ref[...] = accept_ref[...]
    for part in range(2):
        out_ref[:, part, :] = new_ref[:, part * half : (part + 1) * half]
    fit = fit_rows(lax.axis_index(BOTH), bands)
    fit = jnp.broadcast_to(fit, (SUB, fit.shape[1])).T
    fit_ref[...] = jnp.broadcast_to(fit[:bands, 0:1], (bands, LANES))


def call(kernel, outs, args, scratch=(), smem=0, flops=0, name=None, hbm=False, last_any=False, alias=None):
    vmem = pl.BlockSpec(memory_space=pltpu.VMEM)
    rest = vmem
    if hbm:
        rest = pl.BlockSpec(memory_space=pl.ANY)
        args = [pltpu.with_memory_space_constraint(x, pltpu.HBM) if x.dtype != jnp.int32 or x.ndim > 1 else x for x in args]
    specs = [pl.BlockSpec(memory_space=pltpu.SMEM)] * smem + [rest] * (len(args) - smem)
    if last_any:
        specs[-1] = pl.BlockSpec(memory_space=pl.ANY)
    return pl.pallas_call(
        kernel,
        out_shape=outs,
        in_specs=specs,
        out_specs=[vmem] * len(outs),
        scratch_shapes=scratch,
        compiler_params=pltpu.CompilerParams(vmem_limit_bytes=16 * 2**20),
        cost_estimate=pl.CostEstimate(flops=flops, bytes_accessed=2**20, transcendentals=0),
        name=name,
        input_output_aliases=alias or {},
    )(*args)


def shape(dims, dtype):
    return jax.ShapeDtypeStruct(dims, dtype)


def local(
    data,
    inv_noise,
    mbh_amp,
    mbh_phase,
    bin_amp,
    bin_phase,
    bin_slope,
    bin_curve,
    bin_start,
    bin_count,
):
    band_bins = data.shape[1]
    slots = bin_amp.shape[1]
    rows, harmonics, powers, peers = mbh_amp.shape
    groups = lax.axis_size("group")
    walkers = rows * peers // 2
    bands = lax.axis_size(BOTH)
    own = 2 * band_bins

    span = padded(2 * powers * harmonics * rows)
    extra = 6 * LANES + 5 * slots
    cross_rows = -(-(extra - 3 * LANES) // span // SUB) * SUB
    packed, bins, data, noise = call(
        pack_kernel,
        [
            shape((peers, 1, 3 * span + extra), F32),
            shape((SUB, slots), F32),
            shape((2, band_bins), F32),
            shape((1, band_bins), F32),
        ],
        [
            mbh_amp.transpose(1, 2, 3, 0), mbh_phase.transpose(1, 2, 3, 0), data, inv_noise.reshape(-1, LANES),
            bin_amp, bin_phase, bin_slope, bin_curve, bin_start, bin_count,
        ],
        scratch=[
            pltpu.VMEM((harmonics, powers, peers, rows), F32),
            pltpu.VMEM((harmonics, powers, peers, rows), F32),
            pltpu.VMEM((4, 1, slots), F32),
            pltpu.VMEM((1, slots), jnp.int32),
            pltpu.VMEM((band_bins // LANES, LANES), BF16),
            pltpu.SMEM((1,), jnp.int32),
            pltpu.SemaphoreType.DMA((10,)),
        ],
        hbm=True,
        name="pack",
    )
    received = lax.all_to_all(packed, "shard", split_axis=0, concat_axis=0, tiled=True)
    received = received.reshape(peers, -1)
    wave, slot_power, rim_squares = call(
        wave_kernel,
        [shape((slots, own + 2 * LANES), BF16), shape((SUB, slots), F32), shape((slots, 3 * LANES), BF16)],
        [bins, noise],
        scratch=[pltpu.VMEM((slots, LANES), F32), pltpu.VMEM((slots, LANES), F32)],
        flops=10**9,
        name="waves",
    )
    (to_cross,) = call(
        cross_kernel,
        [shape((peers + cross_rows, span), F32)],
        [received, slot_power],
        last_any=True,
        name="cross",
    )
    pairs = [(g * peers, (g + 1) * peers) for g in range(groups - 1)]
    pairs += [(g * peers + peers - 1, (g - 1) * peers + peers - 1) for g in range(1, groups)]
    crossed = lax.ppermute(to_cross, BOTH, pairs)

    extras = received[:, 3 * span :]
    parts = [received[:, i * span : (i + 1) * span] for i in range(3)] + [crossed[:peers]]
    crossed_extra = crossed[peers:]
    if rows != 2 * SUB:

        def by_eight(x):
            x = x[:, : 2 * powers * harmonics * rows].reshape(peers, 2 * powers, harmonics, rows)
            x = x.transpose(1, 2, 0, 3).reshape(2 * powers, harmonics, walkers // SUB, SUB, 2)
            x = x.transpose(2, 0, 1, 4, 3).reshape(walkers // SUB, 2 * powers * harmonics * 2 * SUB)
            return jnp.pad(x, ((0, 0), (0, padded(x.shape[1]) - x.shape[1])))

        parts = [by_eight(x) for x in parts]

    resid, weighted = call(
        functools.partial(template_kernel, harmonics),
        [shape((walkers, own), F32), shape((walkers, own), BF16)],
        [parts[0], data, noise],
        scratch=[
            pltpu.VMEM((4, 2 * QUAD, walkers // SUB, LANES), F32),
            pltpu.VMEM((4, walkers // SUB * LANES, 2 * LANES), F32),
        ],
        flops=10**9,
        name="template",
    )
    accept, updated, log_power = call(
        functools.partial(score_kernel, harmonics, band_bins // LANES),
        [shape((walkers, slots), F32), shape((walkers, own), F32), shape((bands, 1, LANES), F32)],
        [
            weighted, resid, noise, bins, wave, slot_power, rim_squares, jnp.concatenate(parts[1:3], axis=1), extras,
            parts[3], crossed_extra,
        ],
        scratch=[
            pltpu.VMEM((min(slots, LANES), 4 * LANES), BF16),
            pltpu.VMEM((min(slots, LANES), LANES), F32),
            pltpu.VMEM((2, 2 * QUAD, walkers // SUB, LANES), F32),
            pltpu.VMEM((2, walkers // SUB * LANES, 2 * LANES), F32),
            pltpu.VMEM((walkers, 4 * LANES), F32),
            pltpu.VMEM((walkers, 4 * LANES), BF16),
        ],
        name="scores",
    )
    log_powers = lax.all_to_all(log_power, BOTH, split_axis=0, concat_axis=0, tiled=True)
    accept_prob, residual_new, fit = call(
        functools.partial(output_kernel, bands),
        [shape((walkers, slots), F32), shape((walkers, 2, band_bins), F32), shape((bands, LANES), F32)],
        [accept, updated],
        name="outputs",
    )
    noise_fit = jnp.sum(fit * log_powers[:, 0, :], axis=0)[:1]
    return (accept_prob, residual_new, noise_fit)


def solution(mesh):
    in_specs = (
        P(None, BOTH),
        P(BOTH),
        P("shard", None, None, "group"),
        P("shard", None, None, "group"),
        P(BOTH, None),
        P(BOTH, None),
        P(BOTH, None),
        P(BOTH, None),
        P(BOTH, None),
        P(BOTH),
    )
    out_specs = (P(None, BOTH), P(None, None, BOTH), P(BOTH))
    return jax.shard_map(local, mesh=mesh, in_specs=in_specs, out_specs=out_specs, check_vma=False)
```

```python
import functools
import math

import jax
import jax.numpy as jnp
import numpy as np
from jax import lax
from jax.experimental import pallas as pl
from jax.experimental.pallas import tpu as pltpu
from jax.sharding import PartitionSpec as P

Q = 128
NCOEF = 8
LANES = 128
SUB = 8
F32 = jnp.float32
BF16 = jnp.bfloat16
BOTH = ("group", "shard")
OVER_LANES = (((1,), (1,)), ((), ()))

INV_TAU = np.float32(1.0 / (2.0 * math.pi))
TAU_A = np.float32(round(2.0 * math.pi * 512) / 512)
TAU_B = np.float32(round((2.0 * math.pi - float(TAU_A)) * 2**22) / 2**22)
TAU_C = np.float32(2.0 * math.pi - float(TAU_A) - float(TAU_B))
MAGIC = np.float32(1.5 * 2**23)
SIN2 = (6.283185160089475, -10.33541375785372, 5.100062754574036, -1.1960903483123309, 0.15444025802555503)
COS1 = (0.9999999534666666, -4.934792858675247, 4.058411914166824, -1.3318801612473732, 0.2196967986012024)


def nearest(x):
    return (x + MAGIC) - MAGIC


def padded(count):
    return -(-count // LANES) * LANES


def poly(y, coefs):
    total = np.float32(coefs[-1])
    for c in coefs[-2::-1]:
        total = total * y + np.float32(c)
    return total


def cis_turns(r):
    y = r * r
    s2 = poly(y, SIN2) * r
    c1 = poly(y, COS1)
    return np.float32(1.0) - np.float32(0.5) * (s2 * s2), s2 * c1


def turns(angle):
    n = nearest(angle * INV_TAU)
    return (((angle - n * TAU_A) - n * TAU_B) - n * TAU_C) * INV_TAU


def frac(t):
    return t - nearest(t)


def col(x, lane, rows=SUB):
    return jnp.broadcast_to(x[:, lane : lane + 1], (rows, LANES))


def lane_iota(rows=SUB):
    return lax.broadcasted_iota(jnp.int32, (rows, LANES), 1)


def pack_kernel(
    amp_hbm, phase_hbm, data_hbm, noise_hbm, bin_amp_hbm, bin_phase_hbm, bin_slope_hbm, bin_curve_hbm,
    bin_start_hbm, count_hbm, packed_ref, bins_ref, data_ref, noise_ref, own_ref,
    amp_ref, phase_ref, rows_ref, start_ref, raw_noise_ref, count_ref, sems,
):
    copies = [
        pltpu.make_async_copy(source, target, sems.at[i])
        for i, (source, target) in enumerate(
            [
                (amp_hbm, amp_ref),
                (phase_hbm, phase_ref),
                (count_hbm, count_ref),
                (bin_amp_hbm, rows_ref.at[0]),
                (bin_phase_hbm, rows_ref.at[1]),
                (bin_slope_hbm, rows_ref.at[2]),
                (bin_curve_hbm, rows_ref.at[3]),
                (bin_start_hbm, start_ref),
                (data_hbm, data_ref),
                (noise_hbm, raw_noise_ref),
            ]
        )
    ]
    for copy in copies:
        copy.start()
    harmonics, powers, peers, rows = amp_ref.shape
    span = padded(2 * powers * harmonics * rows)
    slots = bins_ref.shape[1]
    band_bins = data_ref.shape[1]
    for copy in copies[2:]:
        copy.wait()
    live = lax.broadcasted_iota(jnp.int32, (1, slots), 1) < count_ref[0]
    amp = jnp.where(live, rows_ref[0], 0.0)
    slot_rows = [amp, rows_ref[1], rows_ref[2], rows_ref[3], start_ref[...].astype(F32)]
    bins_ref[...] = jnp.concatenate([*slot_rows, live.astype(F32), jnp.zeros((2, slots), F32)], axis=0)
    raw_noise = raw_noise_ref[...].astype(F32)
    noise = jnp.concatenate([raw_noise[i : i + 1] for i in range(raw_noise.shape[0])], axis=1)
    noise_ref[...] = noise
    start = 3 * span
    before = lax.rem(lax.axis_index("shard") + peers - 1, peers)
    for i, row in enumerate((data_ref[0:1, :], data_ref[1:2, :], noise)):
        packed_ref[:, 0, start : start + LANES] = jnp.broadcast_to(row[:, band_bins - LANES :], (peers, LANES))
        packed_ref[pl.ds(before, 1), 0, start : start + LANES] = row[:, :LANES]
        start += LANES
    for row in slot_rows:
        packed_ref[:, 0, start : start + slots] = jnp.broadcast_to(row, (peers, slots))
        start += slots
    for copy in copies[:2]:
        copy.wait()
    parts = [ref[h, power] for ref in (amp_ref, phase_ref) for power in range(powers) for h in range(harmonics)]
    if span > 2 * powers * harmonics * rows:
        parts.append(jnp.zeros((peers, span - 2 * powers * harmonics * rows), F32))
    packed = jnp.concatenate(parts, axis=1)
    if rows == 2 * SUB:
        lane = lax.broadcasted_iota(jnp.int32, (peers, LANES), 1)
        order = lane - lane % (2 * SUB) + lane % SUB * 2 + lane % (2 * SUB) // SUB
        blocks = [packed[:, i : i + LANES] for i in range(0, span, LANES)]
        blocks = [jnp.take_along_axis(x, order, axis=1, mode="promise_in_bounds") for x in blocks]
        packed = jnp.concatenate(blocks, axis=1)
    own_ref[...] = packed
    packed_ref[:, 0, :span] = packed
    packed_ref[:, 0, span : 2 * span] = jnp.concatenate([packed[-1:], packed[:-1]], axis=0)
    packed_ref[:, 0, 2 * span : 3 * span] = jnp.concatenate([packed[1:], packed[:1]], axis=0)


def cross_kernel(rec_ref, *refs):
    out_ref = refs[-1]
    peers = rec_ref.shape[0]
    span = out_ref.shape[1]
    first = lax.axis_index("shard") == 0
    out_ref[:peers, :] = jnp.where(first, rec_ref[:, span : 2 * span], rec_ref[:, 2 * span : 3 * span])
    row = rec_ref[peers - 1 : peers, 3 * span :]
    rim = rec_ref[0:1, 3 * span : 3 * span + 3 * LANES]
    row = jnp.concatenate([jnp.where(first, row[:, : 3 * LANES], rim), row[:, 3 * LANES :]], axis=1)
    for i, at in enumerate(range(0, row.shape[1], span)):
        lanes = min(span, row.shape[1] - at)
        out_ref[peers + i : peers + i + 1, :lanes] = row[:, at : at + lanes]


def coefficients(rec, width, band_bins):
    share = LANES / band_bins
    fill = jnp.zeros((rec.shape[0], LANES - width), F32)
    terms = [jnp.concatenate([rec[:, k * width : (k + 1) * width], fill], axis=1) for k in range(6)]
    amps, (p0, p1, p2) = terms[:3], terms[3:]
    return amps, (p1, p2), (turns(p0), turns(p1 * np.float32(share)), turns(p2 * np.float32(share * share)))


def phase_terms(k, band_bins, linear, reduced):
    p1, p2 = linear
    f0, f1, f2 = reduced
    share = LANES / band_bins
    const = frac(f0 + np.float32(k) * f1 + np.float32(k * k) * f2)
    slope = (p1 + p2 * np.float32(2 * k * share)) * np.float32(1.0 / band_bins) * INV_TAU
    return [const, slope, p2 * np.float32(1.0 / band_bins**2) * INV_TAU]


def amp_terms(k, band_bins, amps):
    a0, a1, a2 = amps
    at = k * LANES / band_bins
    slope = (a1 + a2 * np.float32(2 * at)) * np.float32(1.0 / band_bins)
    return [a0 + (a1 + a2 * np.float32(at)) * np.float32(at), slope, a2 * np.float32(1.0 / band_bins**2)]


def pieces(x):
    high = x.astype(BF16).astype(F32)
    rest = x - high
    middle = rest.astype(BF16).astype(F32)
    return [high, middle, (rest - middle).astype(BF16).astype(F32)]


def piece_rows(terms):
    rows = []
    for kind, term in zip(((0,), (1,), (2, 3)), terms):
        parts = pieces(term)
        rows += [(part, power) for power in kind for part in parts]
    return rows


def evaluator(quantities, stage_ref, values_ref):
    lane = lax.broadcasted_iota(jnp.int32, (1, LANES), 1)
    low = lane * lane % LANES
    powers = [x.astype(F32) for x in (jnp.ones_like(lane), lane, lane * lane - low, low)]
    count = stage_ref.shape[0]
    table, spans = [], []
    for terms in quantities:
        start = len(table)
        for part, power in piece_rows(terms):
            stage_ref[len(table)] = part
            table.append(powers[power])
        spans.append((start, len(table)))
    for i in range(len(table), count):
        stage_ref[i] = jnp.zeros(stage_ref.shape[1:], F32)
        table.append(jnp.zeros((1, LANES), F32))
    table = jnp.concatenate(table, axis=0)
    row = lax.broadcasted_iota(jnp.int32, (count, LANES), 0)
    blocks = [jnp.where((row >= start) & (row < stop), table, 0.0) for start, stop in spans]
    table = jnp.concatenate(blocks, axis=1).astype(BF16)

    def evaluate(q):
        rows = stage_ref[:, q, :].T.astype(BF16)
        values_ref[q * LANES : (q + 1) * LANES, :] = jnp.dot(rows, table, preferred_element_type=F32)

    return evaluate


def stage_rows(count):
    return -(-count // (2 * SUB)) * 2 * SUB


def by_walkers(count, evaluate, block):
    evaluate(0)
    for q in range(count):
        if q + 1 < count:
            evaluate(q + 1)
        block(q)


def summed(halves):
    return [a.astype(BF16).astype(F32) + b.astype(BF16).astype(F32) for a, b in zip(*halves, strict=True)]


def template_blocks(harmonics, rec, rows, data_ref, stage_ref, values_ref, emit):
    band_bins = data_ref.shape[1]
    blocks = band_bins // LANES
    share = LANES / band_bins
    amps, linear, reduced = coefficients(rec, harmonics * 2 * SUB, band_bins)
    _, f1, f2 = reduced
    twist_re, twist_im = cis_turns(frac(np.float32(2.0) * f2))
    now, then = amp_terms(0, band_bins, amps), amp_terms(1, band_bins, amps)
    evaluate = evaluator(
        [
            phase_terms(0, band_bins, linear, reduced),
            now,
            [frac(f1 + f2), linear[1] * np.float32(2 * share / band_bins) * INV_TAU],
            [then[0] - now[0], amps[2] * np.float32(2 * share / band_bins)],
            [twist_re],
            [twist_im],
            [amps[2] * np.float32(2 * share * share)],
        ],
        stage_ref,
        values_ref,
    )

    def block(q):
        halves = []
        for s in range(2):
            total = [None] * (2 * blocks)
            for h in range(harmonics):
                at = pl.ds(q * LANES + (2 * h + s) * SUB, SUB)
                values = [values_ref[at, i * LANES : (i + 1) * LANES] for i in range(7)]
                phase, a, w_phase, da, twist_re, twist_im, dda = values
                z_re, z_im = cis_turns(frac(phase))
                w_re, w_im = cis_turns(frac(w_phase))
                for k in range(blocks):
                    terms = (a * z_re, a * z_im)
                    for i in range(2):
                        total[2 * k + i] = terms[i] if h == 0 else total[2 * k + i] + terms[i]
                    if k + 1 < blocks:
                        z_re, z_im = z_re * w_re - z_im * w_im, z_re * w_im + z_im * w_re
                        a = a + da
                    if k + 2 < blocks:
                        w_re, w_im = w_re * twist_re - w_im * twist_im, w_re * twist_im + w_im * twist_re
                        da = da + dda
            halves.append(total)
        for i, template in enumerate(summed(halves)):
            here = i // 2 * LANES
            there = i % 2 * band_bins + here
            emit(q, slice(there, there + LANES), data_ref[i % 2 : i % 2 + 1, here : here + LANES] - template)

    by_walkers(rows, evaluate, block)


def own_kernel(harmonics, rec_ref, data_ref, resid_ref, stage_ref, values_ref):
    def emit(_, lanes, residual):
        resid_ref[:, lanes] = residual

    rec = rec_ref[pl.ds(lax.axis_index("shard"), 1), :]
    template_blocks(harmonics, rec, 1, data_ref, stage_ref, values_ref, emit)


def template_kernel(harmonics, own_done, *refs):
    if own_done:
        rec_ref, data_ref, noise_ref, own_ref, resid_ref, weighted_ref, stage_ref, values_ref = refs
    else:
        rec_ref, data_ref, noise_ref, resid_ref, weighted_ref, stage_ref, values_ref = refs
    band_bins = data_ref.shape[1]
    count = rec_ref.shape[0]
    rec = rec_ref[...]
    skip = 0
    if own_done:
        place = lax.axis_index("shard")
        rec = pltpu.roll(rec, lax.rem(2 * count - 1 - place, count), 0)
        resid_ref[pl.ds(pl.multiple_of(place * SUB, SUB), SUB), :] = own_ref[...]
        skip = 1

    def emit(q, lanes, residual):
        row = q * SUB
        if own_done:
            row = pl.multiple_of(lax.rem(place + 1 + q, count) * SUB, SUB)
        resid_ref[pl.ds(row, SUB), lanes] = residual

    template_blocks(harmonics, rec, count - skip, data_ref, stage_ref, values_ref, emit)
    for part in range(2):
        lanes = slice(part * band_bins, (part + 1) * band_bins)
        weighted_ref[:, lanes] = (resid_ref[:, lanes] * noise_ref[0:1, :]).astype(BF16)


def slot_columns(bins, cols_ref):
    slots = bins.shape[1]
    cols_ref[...] = jnp.concatenate([bins.T, jnp.zeros((slots, LANES - SUB), F32)], axis=1)


def slot_wave(params, lane):
    rows = params.shape[0]
    amp, phase, slope, curve, start = (col(params, i, rows) for i in range(5))
    high = jnp.floor(start * np.float32(1.0 / LANES))
    low = start - high * np.float32(LANES)
    offset = lane - low
    wrapped = offset < 0.0
    j = jnp.where(wrapped, offset + np.float32(Q), offset)
    angle = phase + slope * j + curve * j * j
    c, s = cis_turns(turns(angle))
    y = (j + np.float32(0.5)) * np.float32(1.0 / Q) - np.float32(0.5)
    envelope = poly(y * y, COS1)
    scale = amp * (envelope * envelope)
    return scale * c, scale * s, wrapped, high


def wave_kernel(bins_ref, noise_ref, wave_ref, total_ref, rim_ref, cols_ref, power_ref):
    slots = bins_ref.shape[1]
    band_bins = noise_ref.shape[1]
    blocks = band_bins // LANES
    slot_columns(bins_ref[...], cols_ref)
    rows = 2 * SUB
    lane = lane_iota(rows).astype(F32)

    def block(step, _):
        at = pl.ds(pl.multiple_of(step * rows, rows), rows)
        re, im, wrapped, high = slot_wave(cols_ref[at, :], lane)
        home = jnp.where(wrapped, high + 1.0, high)
        re_half, im_half = re.astype(BF16), im.astype(BF16)
        re, im = re_half.astype(F32), im_half.astype(F32)
        noise = jnp.zeros((rows, LANES), F32)
        for k in range(blocks + 1):
            inside = home == np.float32(k)
            if k < blocks:
                noise = jnp.where(inside, noise_ref[0:1, k * LANES : (k + 1) * LANES], noise)
            start = k * LANES if k < blocks else 2 * band_bins
            wave_ref[at, start : start + LANES] = jnp.where(inside, re, 0.0).astype(BF16)
            start += band_bins if k < blocks else LANES
            wave_ref[at, start : start + LANES] = jnp.where(inside, im, 0.0).astype(BF16)
        squares = re * re + im * im
        power_ref[at, :] = squares * noise
        for i, piece in enumerate(pieces(jnp.where(home == np.float32(blocks), squares, 0.0))):
            rim_ref[at, i * LANES : (i + 1) * LANES] = piece.astype(BF16)
        return 0

    lax.fori_loop(0, slots // rows, block, 0, unroll=4)
    total_ref[...] = row_sums(power_ref[...])


def fit_rows(band, bands):
    width = -(-bands // LANES) * LANES
    place = lax.broadcasted_iota(jnp.int32, (NCOEF, width), 1)
    order = lax.broadcasted_iota(jnp.int32, (NCOEF, width), 0)
    x = (2 * place + 1).astype(F32) * np.float32(1.0 / bands) - np.float32(1.0)
    term, after = jnp.ones_like(x), x
    basis = jnp.zeros_like(x)
    for degree in range(NCOEF):
        basis = jnp.where(order == degree, term, basis)
        term, after = after, np.float32(2.0) * x * after - term
    basis = jnp.where(place < bands, basis, 0.0)
    row = lax.broadcasted_iota(jnp.int32, (NCOEF, LANES), 0)
    lane = lax.broadcasted_iota(jnp.int32, (NCOEF, LANES), 1)
    gram = jnp.zeros((NCOEF, LANES), F32)
    for j in range(NCOEF):
        gram = jnp.where(lane == j, jnp.sum(basis * basis[j : j + 1, :], axis=1, keepdims=True), gram)
    side = basis
    for i in range(NCOEF):
        scale = np.float32(1.0) / jnp.sqrt(gram[i : i + 1, i : i + 1])
        upper = gram[i : i + 1, :] * scale
        factor = gram[:, i : i + 1] * scale
        solved = side[i : i + 1, :] * scale
        below = row > i
        gram = jnp.where(below, gram - factor * upper, jnp.where(row == i, upper, gram))
        side = jnp.where(order > i, side - factor * solved, jnp.where(order == i, solved, side))
    for i in reversed(range(NCOEF)):
        solved = side[i : i + 1, :] / gram[i : i + 1, i : i + 1]
        side = jnp.where(order < i, side - gram[:, i : i + 1] * solved, jnp.where(order == i, solved, side))
    mine = jnp.sum(jnp.where(place == band, side, 0.0), axis=1, keepdims=True)
    return jnp.sum(basis * mine, axis=0, keepdims=True)


def row_sums(x):
    ones = jnp.ones((SUB, LANES), F32)
    return lax.dot_general(ones, x, OVER_LANES, precision=lax.Precision.HIGHEST, preferred_element_type=F32)


def accepted(corr, total):
    return jax.nn.sigmoid(corr - np.float32(0.5) * total)


def score_kernel(
    harmonics, blocks, weighted_ref, resid_ref, noise_ref, bins_ref, wave_ref, total_ref, rim_squares_ref, rec_ref, extra_ref,
    cross_ref, cross_extra_ref, accept_ref, new_ref, log_ref,
    prev_ref, prev_power_ref, stage_ref, values_ref, edge_ref, rim_ref,
):
    walkers, own = weighted_ref.shape
    slots = wave_ref.shape[0]
    band_bins = own // 2
    last = blocks - 1
    span = cross_ref.shape[1]
    sources, extra = extra_ref.shape
    place = lax.axis_index("shard")
    first, final = place == 0, place == sources - 1

    below_rec = jnp.where(first, cross_ref[...], rec_ref[:, :span])
    above_rec = jnp.where(final, cross_ref[...], rec_ref[:, span:])
    source = lax.rem(place + 1, sources)
    rows = -(-3 * LANES // cross_extra_ref.shape[1])
    crossed = jnp.concatenate([cross_extra_ref[i : i + 1, :] for i in range(rows)], axis=1)
    above = jnp.where(final, crossed[:, : 3 * LANES], extra_ref[pl.ds(source, 1), : 3 * LANES])
    source = lax.rem(place + sources - 1, sources)
    below = extra_ref[pl.ds(source, 1), :]
    rows = -(-below.shape[1] // cross_extra_ref.shape[1])
    crossed = jnp.concatenate([cross_extra_ref[i : i + 1, :] for i in range(rows)], axis=1)
    below = jnp.where(first, crossed[:, : below.shape[1]], below)

    bins = jnp.concatenate(
        [below[:, 3 * LANES + i * slots : 3 * LANES + (i + 1) * slots] for i in range(5)] + [jnp.zeros((3, slots), F32)],
        axis=0,
    )
    passes = (bins[4:5] > np.float32(band_bins - Q)) & (bins[0:1] != 0.0)
    flags = jnp.broadcast_to(jnp.where(passes, 1.0, 0.0), (2 * SUB, slots)).astype(BF16)
    row, column = (lax.broadcasted_iota(jnp.int32, (LANES, LANES), i) for i in range(2))
    upto = jnp.where(row <= column, 1.0, 0.0).astype(BF16)
    ranks = []
    for start in range(0, slots, LANES):
        rank = jnp.dot(flags[:, start : start + LANES], upto, preferred_element_type=F32)[0:1]
        ranks.append(rank + ranks[-1][:, LANES - 1 :] if ranks else rank)
    passing = jnp.max(ranks[-1]).astype(jnp.int32)
    rank = jnp.where(passes, jnp.concatenate(ranks, axis=1), 0.0)
    bin_pieces = [x.astype(BF16) for x in pieces(bins)]

    below_noise, above_noise = below[:, 2 * LANES : 3 * LANES], above[:, 2 * LANES : 3 * LANES]
    group = 2 * SUB
    lane = lane_iota(group).astype(F32)
    first_noise = noise_ref[0:1, :LANES]
    chunk = prev_ref.shape[0]
    tail = []

    def chosen_slots(index):
        place = lax.broadcasted_iota(jnp.int32, (chunk, slots), 0) + (index * chunk + 1)
        chosen = jnp.where(rank == place.astype(F32), 1.0, 0.0).astype(BF16)
        cols = [lax.dot_general(chosen, x, OVER_LANES, preferred_element_type=F32) for x in bin_pieces]
        return cols[0] + cols[1] + cols[2]

    def fill(cols, start):
        at = slice(start, start + group)
        re, im, wrapped, _ = slot_wave(cols[at, :], lane)
        re, im = re.astype(BF16).astype(F32), im.astype(BF16).astype(F32)
        power = (re * re + im * im) * jnp.where(wrapped, first_noise, below_noise)
        for i, piece in enumerate(pieces(power)):
            prev_power_ref[at, i * LANES : (i + 1) * LANES] = piece.astype(BF16)
        prev_ref[at, :LANES] = jnp.where(wrapped, 0.0, re).astype(BF16)
        prev_ref[at, LANES : 2 * LANES] = jnp.where(wrapped, 0.0, im).astype(BF16)
        prev_ref[at, 2 * LANES : 3 * LANES] = jnp.where(wrapped, re, 0.0).astype(BF16)
        prev_ref[at, 3 * LANES :] = jnp.where(wrapped, im, 0.0).astype(BF16)

    def spilled():
        corr = lax.dot_general(tail[0], prev_ref[...], OVER_LANES, preferred_element_type=F32)
        ones = jnp.ones((2 * SUB, prev_power_ref.shape[1]), BF16)
        total = lax.dot_general(ones, prev_power_ref[...], OVER_LANES, preferred_element_type=F32)
        half = accepted(corr, total[0:1, :]).astype(BF16)
        return jnp.dot(half, prev_ref[:, 2 * LANES :], preferred_element_type=F32)

    def spill(index, carried):
        cols = chosen_slots(index)
        for start in range(0, chunk, group):
            fill(cols, start)
        return carried + spilled()

    quantities = []
    for k, rec in ((last, below_rec), (0, above_rec)):
        amps, linear, reduced = coefficients(rec, harmonics * 2 * SUB, band_bins)
        quantities += [phase_terms(k, band_bins, linear, reduced), amp_terms(k, band_bins, amps)]
    evaluate = evaluator(quantities, stage_ref, values_ref)

    step = own // (walkers // SUB)
    corr = [jnp.zeros((walkers, slots), F32)]

    cols = chosen_slots(0)
    fills = list(range(0, chunk, group))

    def edge_block(q):
        lanes = slice(q * step, (q + 1) * step)
        corr[0] += lax.dot_general(weighted_ref[:, lanes], wave_ref[:, lanes], OVER_LANES, preferred_element_type=F32)
        halves = []
        for s in range(2):
            total = None
            for h in range(harmonics):
                at = pl.ds(q * LANES + (2 * h + s) * SUB, SUB)
                terms = []
                for i in range(2):
                    phase, a = (values_ref[at, (2 * i + j) * LANES : (2 * i + j + 1) * LANES] for j in range(2))
                    terms += [a * x for x in cis_turns(frac(phase))]
                total = terms if h == 0 else [x + y for x, y in zip(total, terms, strict=True)]
            halves.append(total)
        for i, template in enumerate(summed(halves)):
            part = (below, above)[i // 2][:, i % 2 * LANES : (i % 2 + 1) * LANES]
            edge_ref[q * SUB : (q + 1) * SUB, i * LANES : (i + 1) * LANES] = part - template
        for start in fills[q :: walkers // SUB]:
            fill(cols, start)

    by_walkers(walkers // SUB, evaluate, edge_block)
    noise = jnp.concatenate([below_noise, below_noise, above_noise, above_noise], axis=1)
    rim_ref[...] = (edge_ref[...] * noise).astype(BF16)
    mine = jnp.concatenate([weighted_ref[:, :LANES], weighted_ref[:, band_bins : band_bins + LANES]], axis=1)
    tail.append(jnp.concatenate([rim_ref[:, : 2 * LANES], mine], axis=1))

    corr = corr[0] + lax.dot_general(rim_ref[:, 2 * LANES :], wave_ref[:, own:], OVER_LANES, preferred_element_type=F32)
    noise = jnp.broadcast_to(jnp.concatenate([above_noise] * 3, axis=1), (2 * SUB, 3 * LANES)).astype(BF16)
    total = lax.dot_general(noise, rim_squares_ref[...], OVER_LANES, preferred_element_type=F32)
    accept = accepted(corr, total_ref[0:1, :] + total[0:1, :])
    accept = jnp.where(bins_ref[5:6, :] > 0.0, accept, 0.0)
    accept_ref[...] = accept
    half = accept.astype(BF16)

    squares = [jnp.zeros((walkers, LANES), F32)]
    width = 2 * LANES

    def update(start, carried=None):
        lanes = slice(start, start + width)
        new = resid_ref[:, lanes] - jnp.dot(half, wave_ref[:, lanes], preferred_element_type=F32)
        parts = [new[:, i : i + LANES] for i in range(0, width, LANES)]
        if carried is not None:
            part = start // band_bins
            parts[0] -= carried[:, part * LANES : (part + 1) * LANES]
        for i, piece in enumerate(parts):
            new_ref[:, start + i * LANES : start + (i + 1) * LANES] = piece
            squares[0] += piece * piece

    carried = spilled()
    for start in range(0, own, width):
        if start % band_bins:
            update(start)
    carried = lax.fori_loop(1, (passing + chunk - 1) // chunk, spill, carried)
    update(0, carried)
    update(band_bins, carried)
    squares = squares[0]
    total = jnp.sum(jnp.sum(squares, axis=0, keepdims=True), axis=1, keepdims=True)
    log_power = jnp.log(total * np.float32(1.0 / (walkers * own)) + np.float32(1e-6))
    log_ref[:, 0, :] = jnp.broadcast_to(log_power, (log_ref.shape[0], log_ref.shape[2]))


def output_kernel(bands, accept_ref, new_ref, prob_ref, out_ref, fit_ref):
    _, own = new_ref.shape
    half = own // 2
    prob_ref[...] = accept_ref[...]
    for part in range(2):
        out_ref[:, part, :] = new_ref[:, part * half : (part + 1) * half]
    fit = fit_rows(lax.axis_index(BOTH), bands)
    fit = jnp.broadcast_to(fit, (SUB, fit.shape[1])).T
    fit_ref[...] = jnp.broadcast_to(fit[:bands, 0:1], (bands, LANES))


def call(kernel, outs, args, scratch=(), smem=0, flops=0, name=None, hbm=False, unread=0, alias=None):
    vmem = pl.BlockSpec(memory_space=pltpu.VMEM)
    rest = vmem
    if hbm:
        rest = pl.BlockSpec(memory_space=pl.ANY)
        args = [pltpu.with_memory_space_constraint(x, pltpu.HBM) if x.dtype != jnp.int32 or x.ndim > 1 else x for x in args]
    specs = [pl.BlockSpec(memory_space=pltpu.SMEM)] * smem + [rest] * (len(args) - smem)
    if unread:
        specs[-unread:] = [pl.BlockSpec(memory_space=pl.ANY)] * unread
    return pl.pallas_call(
        kernel,
        out_shape=outs,
        in_specs=specs,
        out_specs=[vmem] * len(outs),
        scratch_shapes=scratch,
        compiler_params=pltpu.CompilerParams(vmem_limit_bytes=16 * 2**20),
        cost_estimate=pl.CostEstimate(flops=flops, bytes_accessed=2**20, transcendentals=0),
        name=name,
        input_output_aliases=alias or {},
    )(*args)


def shape(dims, dtype):
    return jax.ShapeDtypeStruct(dims, dtype)


def local(
    data,
    inv_noise,
    mbh_amp,
    mbh_phase,
    bin_amp,
    bin_phase,
    bin_slope,
    bin_curve,
    bin_start,
    bin_count,
):
    band_bins = data.shape[1]
    slots = bin_amp.shape[1]
    rows, harmonics, powers, peers = mbh_amp.shape
    groups = lax.axis_size("group")
    walkers = rows * peers // 2
    bands = lax.axis_size(BOTH)
    own = 2 * band_bins

    span = padded(2 * powers * harmonics * rows)
    extra = 3 * LANES + 5 * slots
    cross_rows = -(-extra // span // SUB) * SUB
    packed, bins, data, noise, own_rows = call(
        pack_kernel,
        [
            shape((peers, 1, 3 * span + extra), F32),
            shape((SUB, slots), F32),
            shape((2, band_bins), F32),
            shape((1, band_bins), F32),
            shape((peers, span), F32),
        ],
        [
            mbh_amp.transpose(1, 2, 3, 0), mbh_phase.transpose(1, 2, 3, 0), data, inv_noise.reshape(-1, LANES),
            bin_amp, bin_phase, bin_slope, bin_curve, bin_start, bin_count,
        ],
        scratch=[
            pltpu.VMEM((harmonics, powers, peers, rows), F32),
            pltpu.VMEM((harmonics, powers, peers, rows), F32),
            pltpu.VMEM((4, 1, slots), F32),
            pltpu.VMEM((1, slots), jnp.int32),
            pltpu.VMEM((band_bins // LANES, LANES), BF16),
            pltpu.SMEM((1,), jnp.int32),
            pltpu.SemaphoreType.DMA((10,)),
        ],
        hbm=True,
        name="pack",
    )
    received = lax.all_to_all(packed, "shard", split_axis=0, concat_axis=0, tiled=True)
    received = received.reshape(peers, -1)
    wave, slot_power, rim_squares = call(
        wave_kernel,
        [shape((slots, own + 2 * LANES), BF16), shape((SUB, slots), F32), shape((slots, 3 * LANES), BF16)],
        [bins, noise],
        scratch=[pltpu.VMEM((slots, LANES), F32), pltpu.VMEM((slots, LANES), F32)],
        flops=10**9,
        name="waves",
    )
    direct = rows == 2 * SUB
    before = [slot_power]
    scratch = [pltpu.VMEM((stage_rows(45), walkers // SUB, LANES), F32), pltpu.VMEM((walkers // SUB * LANES, 7 * LANES), F32)]
    if direct:
        (own_resid,) = call(
            functools.partial(own_kernel, harmonics),
            [shape((SUB, own), F32)],
            [own_rows, data],
            scratch=[pltpu.VMEM((stage_rows(45), 1, LANES), F32), pltpu.VMEM((LANES, 7 * LANES), F32)],
            flops=10**9,
            name="own_template",
        )
        before.append(own_resid)
    (to_cross,) = call(
        cross_kernel,
        [shape((peers + cross_rows, span), F32)],
        [received, *before],
        unread=len(before),
        name="cross",
    )
    pairs = [(g * peers, (g + 1) * peers) for g in range(groups - 1)]
    pairs += [(g * peers + peers - 1, (g - 1) * peers + peers - 1) for g in range(1, groups)]
    crossed = lax.ppermute(to_cross, BOTH, pairs)

    extras = received[:, 3 * span :]
    parts = [received[:, i * span : (i + 1) * span] for i in range(3)] + [crossed[:peers]]
    crossed_extra = crossed[peers:]
    if not direct:

        def by_eight(x):
            x = x[:, : 2 * powers * harmonics * rows].reshape(peers, 2 * powers, harmonics, rows)
            x = x.transpose(1, 2, 0, 3).reshape(2 * powers, harmonics, walkers // SUB, SUB, 2)
            x = x.transpose(2, 0, 1, 4, 3).reshape(walkers // SUB, 2 * powers * harmonics * 2 * SUB)
            return jnp.pad(x, ((0, 0), (0, padded(x.shape[1]) - x.shape[1])))

        parts = [by_eight(x) for x in parts]

    resid, weighted = call(
        functools.partial(template_kernel, harmonics, direct),
        [shape((walkers, own), F32), shape((walkers, own), BF16)],
        [parts[0], data, noise, *before[1:]],
        scratch=scratch,
        flops=10**9,
        name="template",
    )
    accept, updated, log_power = call(
        functools.partial(score_kernel, harmonics, band_bins // LANES),
        [shape((walkers, slots), F32), shape((walkers, own), F32), shape((bands, 1, LANES), F32)],
        [
            weighted, resid, noise, bins, wave, slot_power, rim_squares, jnp.concatenate(parts[1:3], axis=1), extras,
            parts[3], crossed_extra,
        ],
        scratch=[
            pltpu.VMEM((min(slots, LANES), 4 * LANES), BF16),
            pltpu.VMEM((min(slots, LANES), 3 * LANES), BF16),
            pltpu.VMEM((stage_rows(48), walkers // SUB, LANES), F32),
            pltpu.VMEM((walkers // SUB * LANES, 4 * LANES), F32),
            pltpu.VMEM((walkers, 4 * LANES), F32),
            pltpu.VMEM((walkers, 4 * LANES), BF16),
        ],
        name="scores",
    )
    log_powers = lax.all_to_all(log_power, BOTH, split_axis=0, concat_axis=0, tiled=True)
    accept_prob, residual_new, fit = call(
        functools.partial(output_kernel, bands),
        [shape((walkers, slots), F32), shape((walkers, 2, band_bins), F32), shape((bands, LANES), F32)],
        [accept, updated],
        name="outputs",
    )
    noise_fit = jnp.sum(fit * log_powers[:, 0, :], axis=0)[:1]
    return (accept_prob, residual_new, noise_fit)


def solution(mesh):
    in_specs = (
        P(None, BOTH),
        P(BOTH),
        P("shard", None, None, "group"),
        P("shard", None, None, "group"),
        P(BOTH, None),
        P(BOTH, None),
        P(BOTH, None),
        P(BOTH, None),
        P(BOTH, None),
        P(BOTH),
    )
    out_specs = (P(None, BOTH), P(None, None, BOTH), P(BOTH))
    return jax.shard_map(local, mesh=mesh, in_specs=in_specs, out_specs=out_specs, check_vma=False)
```

```python
import functools
import math

import jax
import jax.numpy as jnp
import numpy as np
from jax import lax
from jax.experimental import pallas as pl
from jax.experimental.pallas import tpu as pltpu
from jax.sharding import PartitionSpec as P

Q = 128
NCOEF = 8
LANES = 128
SUB = 8
F32 = jnp.float32
BF16 = jnp.bfloat16
BOTH = ("group", "shard")
OVER_LANES = (((1,), (1,)), ((), ()))

INV_TAU = np.float32(1.0 / (2.0 * math.pi))
TAU_A = np.float32(round(2.0 * math.pi * 512) / 512)
TAU_B = np.float32(round((2.0 * math.pi - float(TAU_A)) * 2**22) / 2**22)
TAU_C = np.float32(2.0 * math.pi - float(TAU_A) - float(TAU_B))
SIN2 = (6.283185160089475, -10.33541375785372, 5.100062754574036, -1.1960903483123309, 0.15444025802555503)
COS1 = (0.9999999534666666, -4.934792858675247, 4.058411914166824, -1.3318801612473732, 0.2196967986012024)
SIN_ROOT2 = tuple(c / math.sqrt(2.0) for c in SIN2)
COS_ROOT2 = tuple(c * math.sqrt(2.0) for c in COS1)


def nearest(x):
    return jnp.round(x)


def padded(count):
    return -(-count // LANES) * LANES


def poly(y, coefs):
    total = np.float32(coefs[-1])
    for c in coefs[-2::-1]:
        total = total * y + np.float32(c)
    return total


def cis_turns(r):
    y = r * r
    s2 = poly(y, SIN_ROOT2) * r
    c1 = poly(y, COS_ROOT2)
    return np.float32(1.0) - s2 * s2, s2 * c1


def turns(angle):
    n = nearest(angle * INV_TAU)
    return (((angle - n * TAU_A) - n * TAU_B) - n * TAU_C) * INV_TAU


def frac(t):
    return t - nearest(t)


def col(x, lane, rows=SUB):
    return jnp.broadcast_to(x[:, lane : lane + 1], (rows, LANES))


def lane_iota(rows=SUB):
    return lax.broadcasted_iota(jnp.int32, (rows, LANES), 1)


def pack_kernel(
    amp_hbm, phase_hbm, data_hbm, noise_hbm, bin_amp_hbm, bin_phase_hbm, bin_slope_hbm, bin_curve_hbm,
    bin_start_hbm, count_hbm, packed_ref, bins_ref, data_ref, noise_ref, own_ref,
    amp_ref, phase_ref, rows_ref, start_ref, raw_noise_ref, count_ref, sems,
):
    copies = [
        pltpu.make_async_copy(source, target, sems.at[i])
        for i, (source, target) in enumerate(
            [
                (amp_hbm, amp_ref),
                (phase_hbm, phase_ref),
                (count_hbm, count_ref),
                (bin_amp_hbm, rows_ref.at[0]),
                (bin_phase_hbm, rows_ref.at[1]),
                (bin_slope_hbm, rows_ref.at[2]),
                (bin_curve_hbm, rows_ref.at[3]),
                (bin_start_hbm, start_ref),
                (data_hbm, data_ref),
                (noise_hbm, raw_noise_ref),
            ]
        )
    ]
    for copy in copies:
        copy.start()
    harmonics, powers, peers, rows = amp_ref.shape
    span = padded(2 * powers * harmonics * rows)
    slots = bins_ref.shape[1]
    band_bins = data_ref.shape[1]
    for copy in copies[2:]:
        copy.wait()
    live = lax.broadcasted_iota(jnp.int32, (1, slots), 1) < count_ref[0]
    amp = jnp.where(live, rows_ref[0], 0.0)
    slot_rows = [amp, rows_ref[1], rows_ref[2], rows_ref[3], start_ref[...].astype(F32)]
    bins_ref[...] = jnp.concatenate([*slot_rows, live.astype(F32), jnp.zeros((2, slots), F32)], axis=0)
    raw_noise = raw_noise_ref[...].astype(F32)
    noise = jnp.concatenate([raw_noise[i : i + 1] for i in range(raw_noise.shape[0])], axis=1)
    noise_ref[...] = noise
    start = 3 * span
    before = lax.rem(lax.axis_index("shard") + peers - 1, peers)
    for i, row in enumerate((data_ref[0:1, :], data_ref[1:2, :], noise)):
        packed_ref[:, 0, start : start + LANES] = jnp.broadcast_to(row[:, band_bins - LANES :], (peers, LANES))
        packed_ref[pl.ds(before, 1), 0, start : start + LANES] = row[:, :LANES]
        start += LANES
    for row in slot_rows:
        packed_ref[:, 0, start : start + slots] = jnp.broadcast_to(row, (peers, slots))
        start += slots
    for copy in copies[:2]:
        copy.wait()
    parts = [ref[h, power] for ref in (amp_ref, phase_ref) for power in range(powers) for h in range(harmonics)]
    if span > 2 * powers * harmonics * rows:
        parts.append(jnp.zeros((peers, span - 2 * powers * harmonics * rows), F32))
    packed = jnp.concatenate(parts, axis=1)
    if rows == 2 * SUB:
        lane = lax.broadcasted_iota(jnp.int32, (peers, LANES), 1)
        order = lane - lane % (2 * SUB) + lane % SUB * 2 + lane % (2 * SUB) // SUB
        blocks = [packed[:, i : i + LANES] for i in range(0, span, LANES)]
        blocks = [jnp.take_along_axis(x, order, axis=1, mode="promise_in_bounds") for x in blocks]
        packed = jnp.concatenate(blocks, axis=1)
    own_ref[...] = packed
    packed_ref[:, 0, :span] = packed
    packed_ref[:, 0, span : 2 * span] = jnp.concatenate([packed[-1:], packed[:-1]], axis=0)
    packed_ref[:, 0, 2 * span : 3 * span] = jnp.concatenate([packed[1:], packed[:1]], axis=0)


def cross_kernel(rec_ref, *refs):
    out_ref = refs[-1]
    peers = rec_ref.shape[0]
    span = out_ref.shape[1]
    first = lax.axis_index("shard") == 0
    out_ref[:peers, :] = jnp.where(first, rec_ref[:, span : 2 * span], rec_ref[:, 2 * span : 3 * span])
    row = rec_ref[peers - 1 : peers, 3 * span :]
    rim = rec_ref[0:1, 3 * span : 3 * span + 3 * LANES]
    row = jnp.concatenate([jnp.where(first, row[:, : 3 * LANES], rim), row[:, 3 * LANES :]], axis=1)
    for i, at in enumerate(range(0, row.shape[1], span)):
        lanes = min(span, row.shape[1] - at)
        out_ref[peers + i : peers + i + 1, :lanes] = row[:, at : at + lanes]


def coefficients(rec, width, band_bins):
    share = LANES / band_bins
    fill = jnp.zeros((rec.shape[0], LANES - width), F32)
    terms = [jnp.concatenate([rec[:, k * width : (k + 1) * width], fill], axis=1) for k in range(6)]
    amps, (p0, p1, p2) = terms[:3], terms[3:]
    return amps, (p1, p2), (turns(p0), turns(p1 * np.float32(share)), turns(p2 * np.float32(share * share)))


def phase_terms(k, band_bins, linear, reduced):
    p1, p2 = linear
    f0, f1, f2 = reduced
    share = LANES / band_bins
    const = frac(f0 + np.float32(k) * f1 + np.float32(k * k) * f2)
    slope = (p1 + p2 * np.float32(2 * k * share)) * np.float32(1.0 / band_bins) * INV_TAU
    return [const, slope, p2 * np.float32(1.0 / band_bins**2) * INV_TAU]


def amp_terms(k, band_bins, amps):
    a0, a1, a2 = amps
    at = k * LANES / band_bins
    slope = (a1 + a2 * np.float32(2 * at)) * np.float32(1.0 / band_bins)
    return [a0 + (a1 + a2 * np.float32(at)) * np.float32(at), slope, a2 * np.float32(1.0 / band_bins**2)]


def pieces(x):
    high = x.astype(BF16).astype(F32)
    rest = x - high
    middle = rest.astype(BF16).astype(F32)
    return [high, middle, (rest - middle).astype(BF16).astype(F32)]


def piece_rows(terms):
    rows = []
    for kind, term in zip(((0,), (1,), (2, 3)), terms):
        parts = pieces(term)
        rows += [(part, power) for power in kind for part in parts]
    return rows


def evaluator(quantities, stage_ref, values_ref):
    lane = lax.broadcasted_iota(jnp.int32, (1, LANES), 1)
    low = lane * lane % LANES
    powers = [x.astype(F32) for x in (jnp.ones_like(lane), lane, lane * lane - low, low)]
    count = stage_ref.shape[0]
    table, spans = [], []
    for terms in quantities:
        start = len(table)
        for part, power in piece_rows(terms):
            stage_ref[len(table)] = part
            table.append(powers[power])
        spans.append((start, len(table)))
    for i in range(len(table), count):
        stage_ref[i] = jnp.zeros(stage_ref.shape[1:], F32)
        table.append(jnp.zeros((1, LANES), F32))
    table = jnp.concatenate(table, axis=0)
    row = lax.broadcasted_iota(jnp.int32, (count, LANES), 0)
    blocks = [jnp.where((row >= start) & (row < stop), table, 0.0) for start, stop in spans]
    table = jnp.concatenate(blocks, axis=1).astype(BF16)

    def evaluate(q):
        rows = stage_ref[:, q, :].T.astype(BF16)
        values_ref[q * LANES : (q + 1) * LANES, :] = jnp.dot(rows, table, preferred_element_type=F32)

    return evaluate


def stage_rows(count):
    return -(-count // (2 * SUB)) * 2 * SUB


def by_walkers(count, evaluate, block):
    evaluate(0)
    for q in range(count):
        if q + 1 < count:
            evaluate(q + 1)
        block(q)


def summed(halves):
    return [a.astype(BF16).astype(F32) + b.astype(BF16).astype(F32) for a, b in zip(*halves, strict=True)]


def template_blocks(harmonics, rec, rows, data_ref, stage_ref, values_ref, emit):
    band_bins = data_ref.shape[1]
    blocks = band_bins // LANES
    share = LANES / band_bins
    amps, linear, reduced = coefficients(rec, harmonics * 2 * SUB, band_bins)
    _, f1, f2 = reduced
    twist_re, twist_im = cis_turns(frac(np.float32(2.0) * f2))
    now, then = amp_terms(0, band_bins, amps), amp_terms(1, band_bins, amps)
    evaluate = evaluator(
        [
            phase_terms(0, band_bins, linear, reduced),
            now,
            [frac(f1 + f2), linear[1] * np.float32(2 * share / band_bins) * INV_TAU],
            [then[0] - now[0], amps[2] * np.float32(2 * share / band_bins)],
            [twist_re],
            [twist_im],
            [amps[2] * np.float32(2 * share * share)],
        ],
        stage_ref,
        values_ref,
    )

    def block(q):
        halves = []
        for s in range(2):
            total = [None] * (2 * blocks)
            for h in range(harmonics):
                at = pl.ds(q * LANES + (2 * h + s) * SUB, SUB)
                values = [values_ref[at, i * LANES : (i + 1) * LANES] for i in range(7)]
                phase, a, w_phase, da, twist_re, twist_im, dda = values
                z_re, z_im = cis_turns(frac(phase))
                w_re, w_im = cis_turns(frac(w_phase))
                for k in range(blocks):
                    terms = (a * z_re, a * z_im)
                    for i in range(2):
                        total[2 * k + i] = terms[i] if h == 0 else total[2 * k + i] + terms[i]
                    if k + 1 < blocks:
                        z_re, z_im = z_re * w_re - z_im * w_im, z_re * w_im + z_im * w_re
                        a = a + da
                    if k + 2 < blocks:
                        w_re, w_im = w_re * twist_re - w_im * twist_im, w_re * twist_im + w_im * twist_re
                        da = da + dda
            halves.append(total)
        for i, template in enumerate(summed(halves)):
            here = i // 2 * LANES
            there = i % 2 * band_bins + here
            emit(q, slice(there, there + LANES), data_ref[i % 2 : i % 2 + 1, here : here + LANES] - template)

    by_walkers(rows, evaluate, block)


def own_kernel(harmonics, rec_ref, data_ref, resid_ref, stage_ref, values_ref):
    def emit(_, lanes, residual):
        resid_ref[:, lanes] = residual

    rec = rec_ref[pl.ds(lax.axis_index("shard"), 1), :]
    template_blocks(harmonics, rec, 1, data_ref, stage_ref, values_ref, emit)


def template_kernel(harmonics, own_done, *refs):
    if own_done:
        rec_ref, data_ref, noise_ref, own_ref, resid_ref, weighted_ref, stage_ref, values_ref = refs
    else:
        rec_ref, data_ref, noise_ref, resid_ref, weighted_ref, stage_ref, values_ref = refs
    band_bins = data_ref.shape[1]
    count = rec_ref.shape[0]
    rec = rec_ref[...]
    skip = 0
    if own_done:
        place = lax.axis_index("shard")
        rec = pltpu.roll(rec, lax.rem(2 * count - 1 - place, count), 0)
        resid_ref[pl.ds(pl.multiple_of(place * SUB, SUB), SUB), :] = own_ref[...]
        skip = 1

    def emit(q, lanes, residual):
        row = q * SUB
        if own_done:
            row = pl.multiple_of(lax.rem(place + 1 + q, count) * SUB, SUB)
        resid_ref[pl.ds(row, SUB), lanes] = residual

    template_blocks(harmonics, rec, count - skip, data_ref, stage_ref, values_ref, emit)
    for part in range(2):
        lanes = slice(part * band_bins, (part + 1) * band_bins)
        weighted_ref[:, lanes] = (resid_ref[:, lanes] * noise_ref[0:1, :]).astype(BF16)


def slot_columns(bins, cols_ref):
    slots = bins.shape[1]
    cols_ref[...] = jnp.concatenate([bins.T, jnp.zeros((slots, LANES - SUB), F32)], axis=1)


def slot_wave(params, lane):
    rows = params.shape[0]
    amp, phase, slope, curve, start = (col(params, i, rows) for i in range(5))
    high = jnp.floor(start * np.float32(1.0 / LANES))
    low = start - high * np.float32(LANES)
    offset = lane - low
    wrapped = offset < 0.0
    j = jnp.where(wrapped, offset + np.float32(Q), offset)
    angle = phase + slope * j + curve * j * j
    c, s = cis_turns(turns(angle))
    y = (j + np.float32(0.5)) * np.float32(1.0 / Q) - np.float32(0.5)
    envelope = poly(y * y, COS1)
    scale = amp * (envelope * envelope)
    return scale * c, scale * s, wrapped, high


def wave_kernel(bins_ref, noise_ref, wave_ref, total_ref, rim_ref, cols_ref, power_ref):
    slots = bins_ref.shape[1]
    band_bins = noise_ref.shape[1]
    blocks = band_bins // LANES
    slot_columns(bins_ref[...], cols_ref)
    rows = 2 * SUB
    lane = lane_iota(rows).astype(F32)

    def block(step, _):
        at = pl.ds(pl.multiple_of(step * rows, rows), rows)
        re, im, wrapped, high = slot_wave(cols_ref[at, :], lane)
        home = jnp.where(wrapped, high + 1.0, high)
        re_half, im_half = re.astype(BF16), im.astype(BF16)
        re, im = re_half.astype(F32), im_half.astype(F32)
        noise = jnp.zeros((rows, LANES), F32)
        for k in range(blocks + 1):
            inside = home == np.float32(k)
            if k < blocks:
                noise = jnp.where(inside, noise_ref[0:1, k * LANES : (k + 1) * LANES], noise)
            start = k * LANES if k < blocks else 2 * band_bins
            wave_ref[at, start : start + LANES] = jnp.where(inside, re, 0.0).astype(BF16)
            start += band_bins if k < blocks else LANES
            wave_ref[at, start : start + LANES] = jnp.where(inside, im, 0.0).astype(BF16)
        squares = re * re + im * im
        power_ref[at, :] = squares * noise
        for i, piece in enumerate(pieces(jnp.where(home == np.float32(blocks), squares, 0.0))):
            rim_ref[at, i * LANES : (i + 1) * LANES] = piece.astype(BF16)
        return 0

    lax.fori_loop(0, slots // rows, block, 0, unroll=4)
    total_ref[...] = row_sums(power_ref[...])


def fit_rows(band, bands):
    width = -(-bands // LANES) * LANES
    place = lax.broadcasted_iota(jnp.int32, (NCOEF, width), 1)
    order = lax.broadcasted_iota(jnp.int32, (NCOEF, width), 0)
    x = (2 * place + 1).astype(F32) * np.float32(1.0 / bands) - np.float32(1.0)
    term, after = jnp.ones_like(x), x
    basis = jnp.zeros_like(x)
    for degree in range(NCOEF):
        basis = jnp.where(order == degree, term, basis)
        term, after = after, np.float32(2.0) * x * after - term
    basis = jnp.where(place < bands, basis, 0.0)
    row = lax.broadcasted_iota(jnp.int32, (NCOEF, LANES), 0)
    lane = lax.broadcasted_iota(jnp.int32, (NCOEF, LANES), 1)
    gram = jnp.zeros((NCOEF, LANES), F32)
    for j in range(NCOEF):
        gram = jnp.where(lane == j, jnp.sum(basis * basis[j : j + 1, :], axis=1, keepdims=True), gram)
    side = basis
    for i in range(NCOEF):
        scale = np.float32(1.0) / jnp.sqrt(gram[i : i + 1, i : i + 1])
        upper = gram[i : i + 1, :] * scale
        factor = gram[:, i : i + 1] * scale
        solved = side[i : i + 1, :] * scale
        below = row > i
        gram = jnp.where(below, gram - factor * upper, jnp.where(row == i, upper, gram))
        side = jnp.where(order > i, side - factor * solved, jnp.where(order == i, solved, side))
    for i in reversed(range(NCOEF)):
        solved = side[i : i + 1, :] / gram[i : i + 1, i : i + 1]
        side = jnp.where(order < i, side - gram[:, i : i + 1] * solved, jnp.where(order == i, solved, side))
    mine = jnp.sum(jnp.where(place == band, side, 0.0), axis=1, keepdims=True)
    return jnp.sum(basis * mine, axis=0, keepdims=True)


def row_sums(x):
    ones = jnp.ones((SUB, LANES), F32)
    return lax.dot_general(ones, x, OVER_LANES, precision=lax.Precision.HIGHEST, preferred_element_type=F32)


def accepted(corr, total):
    return jax.nn.sigmoid(corr - np.float32(0.5) * total)


def score_kernel(
    harmonics, blocks, weighted_ref, resid_ref, noise_ref, bins_ref, wave_ref, total_ref, rim_squares_ref, rec_ref, extra_ref,
    cross_ref, cross_extra_ref, accept_ref, new_ref, log_ref,
    prev_ref, prev_power_ref, stage_ref, values_ref, edge_ref, rim_ref,
):
    walkers, own = weighted_ref.shape
    slots = wave_ref.shape[0]
    band_bins = own // 2
    last = blocks - 1
    span = cross_ref.shape[1]
    sources, extra = extra_ref.shape
    place = lax.axis_index("shard")
    first, final = place == 0, place == sources - 1

    below_rec = jnp.where(first, cross_ref[...], rec_ref[:, :span])
    above_rec = jnp.where(final, cross_ref[...], rec_ref[:, span:])
    source = lax.rem(place + 1, sources)
    rows = -(-3 * LANES // cross_extra_ref.shape[1])
    crossed = jnp.concatenate([cross_extra_ref[i : i + 1, :] for i in range(rows)], axis=1)
    above = jnp.where(final, crossed[:, : 3 * LANES], extra_ref[pl.ds(source, 1), : 3 * LANES])
    source = lax.rem(place + sources - 1, sources)
    below = extra_ref[pl.ds(source, 1), :]
    rows = -(-below.shape[1] // cross_extra_ref.shape[1])
    crossed = jnp.concatenate([cross_extra_ref[i : i + 1, :] for i in range(rows)], axis=1)
    below = jnp.where(first, crossed[:, : below.shape[1]], below)

    bins = jnp.concatenate(
        [below[:, 3 * LANES + i * slots : 3 * LANES + (i + 1) * slots] for i in range(5)] + [jnp.zeros((3, slots), F32)],
        axis=0,
    )
    passes = (bins[4:5] > np.float32(band_bins - Q)) & (bins[0:1] != 0.0)
    flags = jnp.broadcast_to(jnp.where(passes, 1.0, 0.0), (2 * SUB, slots)).astype(BF16)
    row, column = (lax.broadcasted_iota(jnp.int32, (LANES, LANES), i) for i in range(2))
    upto = jnp.where(row <= column, 1.0, 0.0).astype(BF16)
    ranks = []
    for start in range(0, slots, LANES):
        rank = jnp.dot(flags[:, start : start + LANES], upto, preferred_element_type=F32)[0:1]
        ranks.append(rank + ranks[-1][:, LANES - 1 :] if ranks else rank)
    passing = jnp.max(ranks[-1]).astype(jnp.int32)
    rank = jnp.where(passes, jnp.concatenate(ranks, axis=1), 0.0)
    bin_pieces = jnp.concatenate(pieces(bins), axis=0).astype(BF16)

    below_noise, above_noise = below[:, 2 * LANES : 3 * LANES], above[:, 2 * LANES : 3 * LANES]
    group = 2 * SUB
    lane = lane_iota(group).astype(F32)
    first_noise = noise_ref[0:1, :LANES]
    chunk = prev_ref.shape[0]
    tail = []

    def chosen_slots(index):
        place = lax.broadcasted_iota(jnp.int32, (chunk, slots), 0) + (index * chunk + 1)
        chosen = jnp.where(rank == place.astype(F32), 1.0, 0.0).astype(BF16)
        cols = lax.dot_general(chosen, bin_pieces, OVER_LANES, preferred_element_type=F32)
        return cols[:, :SUB] + cols[:, SUB : 2 * SUB] + cols[:, 2 * SUB : 3 * SUB]

    def fill(cols, start):
        at = slice(start, start + group)
        re, im, wrapped, _ = slot_wave(cols[at, :], lane)
        re, im = re.astype(BF16).astype(F32), im.astype(BF16).astype(F32)
        power = (re * re + im * im) * jnp.where(wrapped, first_noise, below_noise)
        for i, piece in enumerate(pieces(power)):
            prev_power_ref[at, i * LANES : (i + 1) * LANES] = piece.astype(BF16)
        prev_ref[at, :LANES] = jnp.where(wrapped, 0.0, re).astype(BF16)
        prev_ref[at, LANES : 2 * LANES] = jnp.where(wrapped, 0.0, im).astype(BF16)
        prev_ref[at, 2 * LANES : 3 * LANES] = jnp.where(wrapped, re, 0.0).astype(BF16)
        prev_ref[at, 3 * LANES :] = jnp.where(wrapped, im, 0.0).astype(BF16)

    def spilled():
        corr = lax.dot_general(tail[0], prev_ref[...], OVER_LANES, preferred_element_type=F32)
        ones = jnp.ones((2 * SUB, prev_power_ref.shape[1]), BF16)
        total = lax.dot_general(ones, prev_power_ref[...], OVER_LANES, preferred_element_type=F32)
        half = accepted(corr, total[0:1, :]).astype(BF16)
        return jnp.dot(half, prev_ref[:, 2 * LANES :], preferred_element_type=F32)

    def spill(index, carried):
        cols = chosen_slots(index)
        for start in range(0, chunk, group):
            fill(cols, start)
        return carried + spilled()

    quantities = []
    for k, rec in ((last, below_rec), (0, above_rec)):
        amps, linear, reduced = coefficients(rec, harmonics * 2 * SUB, band_bins)
        quantities += [phase_terms(k, band_bins, linear, reduced), amp_terms(k, band_bins, amps)]
    evaluate = evaluator(quantities, stage_ref, values_ref)

    step = own // (walkers // SUB)
    corr = [jnp.zeros((walkers, slots), F32)]

    cols = chosen_slots(0)
    fills = list(range(0, chunk, group))

    def edge_block(q):
        lanes = slice(q * step, (q + 1) * step)
        corr[0] += lax.dot_general(weighted_ref[:, lanes], wave_ref[:, lanes], OVER_LANES, preferred_element_type=F32)
        halves = []
        for s in range(2):
            total = None
            for h in range(harmonics):
                at = pl.ds(q * LANES + (2 * h + s) * SUB, SUB)
                terms = []
                for i in range(2):
                    phase, a = (values_ref[at, (2 * i + j) * LANES : (2 * i + j + 1) * LANES] for j in range(2))
                    terms += [a * x for x in cis_turns(frac(phase))]
                total = terms if h == 0 else [x + y for x, y in zip(total, terms, strict=True)]
            halves.append(total)
        for i, template in enumerate(summed(halves)):
            part = (below, above)[i // 2][:, i % 2 * LANES : (i % 2 + 1) * LANES]
            edge_ref[q * SUB : (q + 1) * SUB, i * LANES : (i + 1) * LANES] = part - template
        for start in fills[q :: walkers // SUB]:
            fill(cols, start)

    by_walkers(walkers // SUB, evaluate, edge_block)
    noise = jnp.concatenate([below_noise, below_noise, above_noise, above_noise], axis=1)
    rim_ref[...] = (edge_ref[...] * noise).astype(BF16)
    mine = jnp.concatenate([weighted_ref[:, :LANES], weighted_ref[:, band_bins : band_bins + LANES]], axis=1)
    tail.append(jnp.concatenate([rim_ref[:, : 2 * LANES], mine], axis=1))

    corr = corr[0] + lax.dot_general(rim_ref[:, 2 * LANES :], wave_ref[:, own:], OVER_LANES, preferred_element_type=F32)
    noise = jnp.broadcast_to(jnp.concatenate([above_noise] * 3, axis=1), (2 * SUB, 3 * LANES)).astype(BF16)
    total = lax.dot_general(noise, rim_squares_ref[...], OVER_LANES, preferred_element_type=F32)
    accept = accepted(corr, total_ref[0:1, :] + total[0:1, :])
    accept = jnp.where(bins_ref[5:6, :] > 0.0, accept, 0.0)
    accept_ref[...] = accept
    half = accept.astype(BF16)

    squares = [jnp.zeros((walkers, LANES), F32)]
    width = 2 * LANES

    def update(start, carried=None):
        lanes = slice(start, start + width)
        new = resid_ref[:, lanes] - jnp.dot(half, wave_ref[:, lanes], preferred_element_type=F32)
        parts = [new[:, i : i + LANES] for i in range(0, width, LANES)]
        if carried is not None:
            part = start // band_bins
            parts[0] -= carried[:, part * LANES : (part + 1) * LANES]
        for i, piece in enumerate(parts):
            new_ref[:, start + i * LANES : start + (i + 1) * LANES] = piece
            squares[0] += piece * piece

    carried = spilled()
    for start in range(0, own, width):
        if start % band_bins:
            update(start)
    carried = lax.fori_loop(1, (passing + chunk - 1) // chunk, spill, carried)
    update(0, carried)
    update(band_bins, carried)
    squares = squares[0]
    total = jnp.sum(jnp.sum(squares, axis=0, keepdims=True), axis=1, keepdims=True)
    log_power = jnp.log(total * np.float32(1.0 / (walkers * own)) + np.float32(1e-6))
    log_ref[:, 0, :] = jnp.broadcast_to(log_power, (log_ref.shape[0], log_ref.shape[2]))


def output_kernel(bands, accept_ref, new_ref, prob_ref, out_ref, fit_ref):
    _, own = new_ref.shape
    half = own // 2
    prob_ref[...] = accept_ref[...]
    for part in range(2):
        out_ref[:, part, :] = new_ref[:, part * half : (part + 1) * half]
    fit = fit_rows(lax.axis_index(BOTH), bands)
    fit = jnp.broadcast_to(fit, (SUB, fit.shape[1])).T
    fit_ref[...] = jnp.broadcast_to(fit[:bands, 0:1], (bands, LANES))


def call(kernel, outs, args, scratch=(), smem=0, flops=0, name=None, hbm=False, unread=0, alias=None):
    vmem = pl.BlockSpec(memory_space=pltpu.VMEM)
    rest = vmem
    if hbm:
        rest = pl.BlockSpec(memory_space=pl.ANY)
        args = [pltpu.with_memory_space_constraint(x, pltpu.HBM) if x.dtype != jnp.int32 or x.ndim > 1 else x for x in args]
    specs = [pl.BlockSpec(memory_space=pltpu.SMEM)] * smem + [rest] * (len(args) - smem)
    if unread:
        specs[-unread:] = [pl.BlockSpec(memory_space=pl.ANY)] * unread
    return pl.pallas_call(
        kernel,
        out_shape=outs,
        in_specs=specs,
        out_specs=[vmem] * len(outs),
        scratch_shapes=scratch,
        compiler_params=pltpu.CompilerParams(vmem_limit_bytes=16 * 2**20),
        cost_estimate=pl.CostEstimate(flops=flops, bytes_accessed=2**20, transcendentals=0),
        name=name,
        input_output_aliases=alias or {},
    )(*args)


def shape(dims, dtype):
    return jax.ShapeDtypeStruct(dims, dtype)


def local(
    data,
    inv_noise,
    mbh_amp,
    mbh_phase,
    bin_amp,
    bin_phase,
    bin_slope,
    bin_curve,
    bin_start,
    bin_count,
):
    band_bins = data.shape[1]
    slots = bin_amp.shape[1]
    rows, harmonics, powers, peers = mbh_amp.shape
    groups = lax.axis_size("group")
    walkers = rows * peers // 2
    bands = lax.axis_size(BOTH)
    own = 2 * band_bins

    span = padded(2 * powers * harmonics * rows)
    extra = 3 * LANES + 5 * slots
    cross_rows = -(-extra // span // SUB) * SUB
    packed, bins, data, noise, own_rows = call(
        pack_kernel,
        [
            shape((peers, 1, 3 * span + extra), F32),
            shape((SUB, slots), F32),
            shape((2, band_bins), F32),
            shape((1, band_bins), F32),
            shape((peers, span), F32),
        ],
        [
            mbh_amp.transpose(1, 2, 3, 0), mbh_phase.transpose(1, 2, 3, 0), data, inv_noise.reshape(-1, LANES),
            bin_amp, bin_phase, bin_slope, bin_curve, bin_start, bin_count,
        ],
        scratch=[
            pltpu.VMEM((harmonics, powers, peers, rows), F32),
            pltpu.VMEM((harmonics, powers, peers, rows), F32),
            pltpu.VMEM((4, 1, slots), F32),
            pltpu.VMEM((1, slots), jnp.int32),
            pltpu.VMEM((band_bins // LANES, LANES), BF16),
            pltpu.SMEM((1,), jnp.int32),
            pltpu.SemaphoreType.DMA((10,)),
        ],
        hbm=True,
        name="pack",
    )
    received = lax.all_to_all(packed, "shard", split_axis=0, concat_axis=0, tiled=True)
    received = received.reshape(peers, -1)
    wave, slot_power, rim_squares = call(
        wave_kernel,
        [shape((slots, own + 2 * LANES), BF16), shape((SUB, slots), F32), shape((slots, 3 * LANES), BF16)],
        [bins, noise],
        scratch=[pltpu.VMEM((slots, LANES), F32), pltpu.VMEM((slots, LANES), F32)],
        flops=10**9,
        name="waves",
    )
    direct = rows == 2 * SUB
    before = [slot_power]
    scratch = [pltpu.VMEM((stage_rows(45), walkers // SUB, LANES), F32), pltpu.VMEM((walkers // SUB * LANES, 7 * LANES), F32)]
    if direct:
        (own_resid,) = call(
            functools.partial(own_kernel, harmonics),
            [shape((SUB, own), F32)],
            [own_rows, data],
            scratch=[pltpu.VMEM((stage_rows(45), 1, LANES), F32), pltpu.VMEM((LANES, 7 * LANES), F32)],
            flops=10**9,
            name="own_template",
        )
        before.append(own_resid)
    (to_cross,) = call(
        cross_kernel,
        [shape((peers + cross_rows, span), F32)],
        [received, *before],
        unread=len(before),
        name="cross",
    )
    pairs = [(g * peers, (g + 1) * peers) for g in range(groups - 1)]
    pairs += [(g * peers + peers - 1, (g - 1) * peers + peers - 1) for g in range(1, groups)]
    crossed = lax.ppermute(to_cross, BOTH, pairs)

    extras = received[:, 3 * span :]
    parts = [received[:, i * span : (i + 1) * span] for i in range(3)] + [crossed[:peers]]
    crossed_extra = crossed[peers:]
    if not direct:

        def by_eight(x):
            x = x[:, : 2 * powers * harmonics * rows].reshape(peers, 2 * powers, harmonics, rows)
            x = x.transpose(1, 2, 0, 3).reshape(2 * powers, harmonics, walkers // SUB, SUB, 2)
            x = x.transpose(2, 0, 1, 4, 3).reshape(walkers // SUB, 2 * powers * harmonics * 2 * SUB)
            return jnp.pad(x, ((0, 0), (0, padded(x.shape[1]) - x.shape[1])))

        parts = [by_eight(x) for x in parts]

    resid, weighted = call(
        functools.partial(template_kernel, harmonics, direct),
        [shape((walkers, own), F32), shape((walkers, own), BF16)],
        [parts[0], data, noise, *before[1:]],
        scratch=scratch,
        flops=10**9,
        name="template",
    )
    accept, updated, log_power = call(
        functools.partial(score_kernel, harmonics, band_bins // LANES),
        [shape((walkers, slots), F32), shape((walkers, own), F32), shape((bands, 1, LANES), F32)],
        [
            weighted, resid, noise, bins, wave, slot_power, rim_squares, jnp.concatenate(parts[1:3], axis=1), extras,
            parts[3], crossed_extra,
        ],
        scratch=[
            pltpu.VMEM((min(slots, LANES), 4 * LANES), BF16),
            pltpu.VMEM((min(slots, LANES), 3 * LANES), BF16),
            pltpu.VMEM((stage_rows(48), walkers // SUB, LANES), F32),
            pltpu.VMEM((walkers // SUB * LANES, 4 * LANES), F32),
            pltpu.VMEM((walkers, 4 * LANES), F32),
            pltpu.VMEM((walkers, 4 * LANES), BF16),
        ],
        name="scores",
    )
    log_powers = lax.all_to_all(log_power, BOTH, split_axis=0, concat_axis=0, tiled=True)
    accept_prob, residual_new, fit = call(
        functools.partial(output_kernel, bands),
        [shape((walkers, slots), F32), shape((walkers, 2, band_bins), F32), shape((bands, LANES), F32)],
        [accept, updated],
        name="outputs",
    )
    noise_fit = jnp.sum(fit * log_powers[:, 0, :], axis=0)[:1]
    return (accept_prob, residual_new, noise_fit)


def solution(mesh):
    in_specs = (
        P(None, BOTH),
        P(BOTH),
        P("shard", None, None, "group"),
        P("shard", None, None, "group"),
        P(BOTH, None),
        P(BOTH, None),
        P(BOTH, None),
        P(BOTH, None),
        P(BOTH, None),
        P(BOTH),
    )
    out_specs = (P(None, BOTH), P(None, None, BOTH), P(BOTH))
    return jax.shard_map(local, mesh=mesh, in_specs=in_specs, out_specs=out_specs, check_vma=False)
```

```python
import functools
import math

import jax
import jax.numpy as jnp
import numpy as np
from jax import lax
from jax.experimental import pallas as pl
from jax.experimental.pallas import tpu as pltpu
from jax.sharding import PartitionSpec as P

Q = 128
NCOEF = 8
LANES = 128
SUB = 8
F32 = jnp.float32
BF16 = jnp.bfloat16
BOTH = ("group", "shard")
OVER_LANES = (((1,), (1,)), ((), ()))

INV_TAU = np.float32(1.0 / (2.0 * math.pi))
TAU_A = np.float32(round(2.0 * math.pi * 512) / 512)
TAU_B = np.float32(round((2.0 * math.pi - float(TAU_A)) * 2**22) / 2**22)
TAU_C = np.float32(2.0 * math.pi - float(TAU_A) - float(TAU_B))
SIN2 = (6.283185160089475, -10.33541375785372, 5.100062754574036, -1.1960903483123309, 0.15444025802555503)
COS1 = (0.9999999534666666, -4.934792858675247, 4.058411914166824, -1.3318801612473732, 0.2196967986012024)
SIN_ROOT2 = tuple(c / math.sqrt(2.0) for c in SIN2)
COS_ROOT2 = tuple(c * math.sqrt(2.0) for c in COS1)


def nearest(x):
    return jnp.round(x)


def padded(count):
    return -(-count // LANES) * LANES


def poly(y, coefs):
    total = np.float32(coefs[-1])
    for c in coefs[-2::-1]:
        total = total * y + np.float32(c)
    return total


def cis_turns(r):
    y = r * r
    s2 = poly(y, SIN_ROOT2) * r
    c1 = poly(y, COS_ROOT2)
    return np.float32(1.0) - s2 * s2, s2 * c1


def turns(angle):
    n = nearest(angle * INV_TAU)
    return (((angle - n * TAU_A) - n * TAU_B) - n * TAU_C) * INV_TAU


def frac(t):
    return t - nearest(t)


def col(x, lane, rows=SUB):
    return jnp.broadcast_to(x[:, lane : lane + 1], (rows, LANES))


def lane_iota(rows=SUB):
    return lax.broadcasted_iota(jnp.int32, (rows, LANES), 1)


def pack_kernel(
    amp_hbm, phase_hbm, data_hbm, noise_hbm, bin_amp_hbm, bin_phase_hbm, bin_slope_hbm, bin_curve_hbm,
    bin_start_hbm, count_hbm, packed_ref, bins_ref, data_ref, noise_ref, own_ref,
    amp_ref, phase_ref, rows_ref, start_ref, raw_noise_ref, count_ref, sems,
):
    copies = [
        pltpu.make_async_copy(source, target, sems.at[i])
        for i, (source, target) in enumerate(
            [
                (amp_hbm, amp_ref),
                (phase_hbm, phase_ref),
                (count_hbm, count_ref),
                (bin_amp_hbm, rows_ref.at[0]),
                (bin_phase_hbm, rows_ref.at[1]),
                (bin_slope_hbm, rows_ref.at[2]),
                (bin_curve_hbm, rows_ref.at[3]),
                (bin_start_hbm, start_ref),
                (data_hbm, data_ref),
                (noise_hbm, raw_noise_ref),
            ]
        )
    ]
    for copy in copies:
        copy.start()
    harmonics, powers, peers, rows = amp_ref.shape
    span = padded(2 * powers * harmonics * rows)
    slots = bins_ref.shape[1]
    band_bins = data_ref.shape[1]
    for copy in copies[2:]:
        copy.wait()
    live = lax.broadcasted_iota(jnp.int32, (1, slots), 1) < count_ref[0]
    amp = jnp.where(live, rows_ref[0], 0.0)
    slot_rows = [amp, rows_ref[1], rows_ref[2], rows_ref[3], start_ref[...].astype(F32)]
    bins_ref[...] = jnp.concatenate([*slot_rows, live.astype(F32), jnp.zeros((2, slots), F32)], axis=0)
    raw_noise = raw_noise_ref[...].astype(F32)
    noise = jnp.concatenate([raw_noise[i : i + 1] for i in range(raw_noise.shape[0])], axis=1)
    noise_ref[...] = noise
    start = 3 * span
    before = lax.rem(lax.axis_index("shard") + peers - 1, peers)
    for i, row in enumerate((data_ref[0:1, :], data_ref[1:2, :], noise)):
        packed_ref[:, 0, start : start + LANES] = jnp.broadcast_to(row[:, band_bins - LANES :], (peers, LANES))
        packed_ref[pl.ds(before, 1), 0, start : start + LANES] = row[:, :LANES]
        start += LANES
    for row in slot_rows:
        packed_ref[:, 0, start : start + slots] = jnp.broadcast_to(row, (peers, slots))
        start += slots
    for copy in copies[:2]:
        copy.wait()
    parts = [ref[h, power] for ref in (amp_ref, phase_ref) for power in range(powers) for h in range(harmonics)]
    if span > 2 * powers * harmonics * rows:
        parts.append(jnp.zeros((peers, span - 2 * powers * harmonics * rows), F32))
    packed = jnp.concatenate(parts, axis=1)
    if rows == 2 * SUB:
        lane = lax.broadcasted_iota(jnp.int32, (peers, LANES), 1)
        order = lane - lane % (2 * SUB) + lane % SUB * 2 + lane % (2 * SUB) // SUB
        blocks = [packed[:, i : i + LANES] for i in range(0, span, LANES)]
        blocks = [jnp.take_along_axis(x, order, axis=1, mode="promise_in_bounds") for x in blocks]
        packed = jnp.concatenate(blocks, axis=1)
    own_ref[...] = packed
    packed_ref[:, 0, :span] = packed
    packed_ref[:, 0, span : 2 * span] = jnp.concatenate([packed[-1:], packed[:-1]], axis=0)
    packed_ref[:, 0, 2 * span : 3 * span] = jnp.concatenate([packed[1:], packed[:1]], axis=0)


def cross_kernel(rec_ref, *refs):
    out_ref = refs[-1]
    peers = rec_ref.shape[0]
    span = out_ref.shape[1]
    first = lax.axis_index("shard") == 0
    out_ref[:peers, :] = jnp.where(first, rec_ref[:, span : 2 * span], rec_ref[:, 2 * span : 3 * span])
    row = rec_ref[peers - 1 : peers, 3 * span :]
    rim = rec_ref[0:1, 3 * span : 3 * span + 3 * LANES]
    row = jnp.concatenate([jnp.where(first, row[:, : 3 * LANES], rim), row[:, 3 * LANES :]], axis=1)
    for i, at in enumerate(range(0, row.shape[1], span)):
        lanes = min(span, row.shape[1] - at)
        out_ref[peers + i : peers + i + 1, :lanes] = row[:, at : at + lanes]


def coefficients(rec, width, band_bins):
    share = LANES / band_bins
    fill = jnp.zeros((rec.shape[0], LANES - width), F32)
    terms = [jnp.concatenate([rec[:, k * width : (k + 1) * width], fill], axis=1) for k in range(6)]
    amps, (p0, p1, p2) = terms[:3], terms[3:]
    return amps, (p1, p2), (turns(p0), turns(p1 * np.float32(share)), turns(p2 * np.float32(share * share)))


def phase_terms(k, band_bins, linear, reduced):
    p1, p2 = linear
    f0, f1, f2 = reduced
    share = LANES / band_bins
    const = frac(f0 + np.float32(k) * f1 + np.float32(k * k) * f2)
    slope = (p1 + p2 * np.float32(2 * k * share)) * np.float32(1.0 / band_bins) * INV_TAU
    return [const, slope, p2 * np.float32(1.0 / band_bins**2) * INV_TAU]


def amp_terms(k, band_bins, amps):
    a0, a1, a2 = amps
    at = k * LANES / band_bins
    slope = (a1 + a2 * np.float32(2 * at)) * np.float32(1.0 / band_bins)
    return [a0 + (a1 + a2 * np.float32(at)) * np.float32(at), slope, a2 * np.float32(1.0 / band_bins**2)]


def pieces(x):
    high = x.astype(BF16).astype(F32)
    rest = x - high
    middle = rest.astype(BF16).astype(F32)
    return [high, middle, (rest - middle).astype(BF16).astype(F32)]


def piece_rows(terms):
    rows = []
    for kind, term in zip(((0,), (1,), (2, 3)), terms):
        parts = pieces(term)
        rows += [(part, power) for power in kind for part in parts]
    return rows


def evaluator(quantities, stage_ref, values_ref):
    lane = lax.broadcasted_iota(jnp.int32, (1, LANES), 1)
    low = lane * lane % LANES
    powers = [x.astype(F32) for x in (jnp.ones_like(lane), lane, lane * lane - low, low)]
    count = stage_ref.shape[0]
    table, spans = [], []
    for terms in quantities:
        start = len(table)
        for part, power in piece_rows(terms):
            stage_ref[len(table)] = part
            table.append(powers[power])
        spans.append((start, len(table)))
    for i in range(len(table), count):
        stage_ref[i] = jnp.zeros(stage_ref.shape[1:], F32)
        table.append(jnp.zeros((1, LANES), F32))
    table = jnp.concatenate(table, axis=0)
    row = lax.broadcasted_iota(jnp.int32, (count, LANES), 0)
    blocks = [jnp.where((row >= start) & (row < stop), table, 0.0) for start, stop in spans]
    table = jnp.concatenate(blocks, axis=1).astype(BF16)

    def evaluate(q):
        rows = stage_ref[:, q, :].T.astype(BF16)
        values_ref[q * LANES : (q + 1) * LANES, :] = jnp.dot(rows, table, preferred_element_type=F32)

    return evaluate


def stage_rows(count):
    return -(-count // (2 * SUB)) * 2 * SUB


def by_walkers(count, evaluate, block):
    evaluate(0)
    for q in range(count):
        if q + 1 < count:
            evaluate(q + 1)
        block(q)


def summed(halves):
    return [a.astype(BF16).astype(F32) + b.astype(BF16).astype(F32) for a, b in zip(*halves, strict=True)]


def template_blocks(harmonics, rec, rows, data_ref, stage_ref, values_ref, emit):
    band_bins = data_ref.shape[1]
    blocks = band_bins // LANES
    share = LANES / band_bins
    amps, linear, reduced = coefficients(rec, harmonics * 2 * SUB, band_bins)
    _, f1, f2 = reduced
    twist_re, twist_im = cis_turns(frac(np.float32(2.0) * f2))
    now, then = amp_terms(0, band_bins, amps), amp_terms(1, band_bins, amps)
    evaluate = evaluator(
        [
            phase_terms(0, band_bins, linear, reduced),
            now,
            [frac(f1 + f2), linear[1] * np.float32(2 * share / band_bins) * INV_TAU],
            [then[0] - now[0], amps[2] * np.float32(2 * share / band_bins)],
            [twist_re],
            [twist_im],
            [amps[2] * np.float32(2 * share * share)],
        ],
        stage_ref,
        values_ref,
    )

    def block(q):
        halves = []
        for s in range(2):
            total = [None] * (2 * blocks)
            for h in range(harmonics):
                at = pl.ds(q * LANES + (2 * h + s) * SUB, SUB)
                values = [values_ref[at, i * LANES : (i + 1) * LANES] for i in range(7)]
                phase, a, w_phase, da, twist_re, twist_im, dda = values
                z_re, z_im = cis_turns(frac(phase))
                w_re, w_im = cis_turns(frac(w_phase))
                for k in range(blocks):
                    terms = (a * z_re, a * z_im)
                    for i in range(2):
                        total[2 * k + i] = terms[i] if h == 0 else total[2 * k + i] + terms[i]
                    if k + 1 < blocks:
                        z_re, z_im = z_re * w_re - z_im * w_im, z_re * w_im + z_im * w_re
                        a = a + da
                    if k + 2 < blocks:
                        w_re, w_im = w_re * twist_re - w_im * twist_im, w_re * twist_im + w_im * twist_re
                        da = da + dda
            halves.append(total)
        for i, template in enumerate(summed(halves)):
            here = i // 2 * LANES
            there = i % 2 * band_bins + here
            emit(q, slice(there, there + LANES), data_ref[i % 2 : i % 2 + 1, here : here + LANES] - template)

    by_walkers(rows, evaluate, block)


def own_kernel(harmonics, rec_ref, data_ref, resid_ref, stage_ref, values_ref):
    def emit(_, lanes, residual):
        resid_ref[:, lanes] = residual

    rec = rec_ref[pl.ds(lax.axis_index("shard"), 1), :]
    template_blocks(harmonics, rec, 1, data_ref, stage_ref, values_ref, emit)


def template_kernel(harmonics, own_done, *refs):
    if own_done:
        rec_ref, data_ref, noise_ref, own_ref, resid_ref, weighted_ref, stage_ref, values_ref = refs
    else:
        rec_ref, data_ref, noise_ref, resid_ref, weighted_ref, stage_ref, values_ref = refs
    band_bins = data_ref.shape[1]
    count = rec_ref.shape[0]
    rec = rec_ref[...]
    skip = 0
    if own_done:
        place = lax.axis_index("shard")
        rec = pltpu.roll(rec, lax.rem(2 * count - 1 - place, count), 0)
        resid_ref[pl.ds(pl.multiple_of(place * SUB, SUB), SUB), :] = own_ref[...]
        skip = 1

    def emit(q, lanes, residual):
        row = q * SUB
        if own_done:
            row = pl.multiple_of(lax.rem(place + 1 + q, count) * SUB, SUB)
        resid_ref[pl.ds(row, SUB), lanes] = residual

    template_blocks(harmonics, rec, count - skip, data_ref, stage_ref, values_ref, emit)
    for part in range(2):
        lanes = slice(part * band_bins, (part + 1) * band_bins)
        weighted_ref[:, lanes] = (resid_ref[:, lanes] * noise_ref[0:1, :]).astype(BF16)


def slot_columns(bins, cols_ref):
    slots = bins.shape[1]
    cols_ref[...] = jnp.concatenate([bins.T, jnp.zeros((slots, LANES - SUB), F32)], axis=1)


def slot_wave(params, lane):
    rows = params.shape[0]
    amp, phase, slope, curve, start = (col(params, i, rows) for i in range(5))
    high = jnp.floor(start * np.float32(1.0 / LANES))
    low = start - high * np.float32(LANES)
    offset = lane - low
    wrapped = offset < 0.0
    j = jnp.where(wrapped, offset + np.float32(Q), offset)
    angle = phase + slope * j + curve * j * j
    c, s = cis_turns(turns(angle))
    y = (j + np.float32(0.5)) * np.float32(1.0 / Q) - np.float32(0.5)
    envelope = poly(y * y, COS1)
    scale = amp * (envelope * envelope)
    return scale * c, scale * s, wrapped, high


def wave_kernel(bins_ref, noise_ref, wave_ref, total_ref, rim_ref, cols_ref, power_ref):
    slots = bins_ref.shape[1]
    band_bins = noise_ref.shape[1]
    blocks = band_bins // LANES
    slot_columns(bins_ref[...], cols_ref)
    rows = 2 * SUB
    lane = lane_iota(rows).astype(F32)

    def block(step, _):
        at = pl.ds(pl.multiple_of(step * rows, rows), rows)
        re, im, wrapped, high = slot_wave(cols_ref[at, :], lane)
        home = jnp.where(wrapped, high + 1.0, high)
        re_half, im_half = re.astype(BF16), im.astype(BF16)
        re, im = re_half.astype(F32), im_half.astype(F32)
        noise = jnp.zeros((rows, LANES), F32)
        for k in range(blocks + 1):
            inside = home == np.float32(k)
            if k < blocks:
                noise = jnp.where(inside, noise_ref[0:1, k * LANES : (k + 1) * LANES], noise)
            start = k * LANES if k < blocks else 2 * band_bins
            wave_ref[at, start : start + LANES] = jnp.where(inside, re, 0.0).astype(BF16)
            start += band_bins if k < blocks else LANES
            wave_ref[at, start : start + LANES] = jnp.where(inside, im, 0.0).astype(BF16)
        squares = re * re + im * im
        power_ref[at, :] = squares * noise
        for i, piece in enumerate(pieces(jnp.where(home == np.float32(blocks), squares, 0.0))):
            rim_ref[at, i * LANES : (i + 1) * LANES] = piece.astype(BF16)
        return 0

    lax.fori_loop(0, slots // rows, block, 0, unroll=4)
    total_ref[...] = row_sums(power_ref[...])


def fit_rows(band, bands):
    width = -(-bands // LANES) * LANES
    place = lax.broadcasted_iota(jnp.int32, (NCOEF, width), 1)
    order = lax.broadcasted_iota(jnp.int32, (NCOEF, width), 0)
    x = (2 * place + 1).astype(F32) * np.float32(1.0 / bands) - np.float32(1.0)
    term, after = jnp.ones_like(x), x
    basis = jnp.zeros_like(x)
    for degree in range(NCOEF):
        basis = jnp.where(order == degree, term, basis)
        term, after = after, np.float32(2.0) * x * after - term
    basis = jnp.where(place < bands, basis, 0.0)
    row = lax.broadcasted_iota(jnp.int32, (NCOEF, LANES), 0)
    lane = lax.broadcasted_iota(jnp.int32, (NCOEF, LANES), 1)
    gram = jnp.zeros((NCOEF, LANES), F32)
    for j in range(NCOEF):
        gram = jnp.where(lane == j, jnp.sum(basis * basis[j : j + 1, :], axis=1, keepdims=True), gram)
    side = basis
    for i in range(NCOEF):
        scale = np.float32(1.0) / jnp.sqrt(gram[i : i + 1, i : i + 1])
        upper = gram[i : i + 1, :] * scale
        factor = gram[:, i : i + 1] * scale
        solved = side[i : i + 1, :] * scale
        below = row > i
        gram = jnp.where(below, gram - factor * upper, jnp.where(row == i, upper, gram))
        side = jnp.where(order > i, side - factor * solved, jnp.where(order == i, solved, side))
    for i in reversed(range(NCOEF)):
        solved = side[i : i + 1, :] / gram[i : i + 1, i : i + 1]
        side = jnp.where(order < i, side - gram[:, i : i + 1] * solved, jnp.where(order == i, solved, side))
    mine = jnp.sum(jnp.where(place == band, side, 0.0), axis=1, keepdims=True)
    return jnp.sum(basis * mine, axis=0, keepdims=True)


def row_sums(x):
    ones = jnp.ones((SUB, LANES), F32)
    return lax.dot_general(ones, x, OVER_LANES, precision=lax.Precision.HIGHEST, preferred_element_type=F32)


def accepted(corr, total):
    return jax.nn.sigmoid(corr - np.float32(0.5) * total)


def score_kernel(
    harmonics, blocks, weighted_ref, resid_ref, noise_ref, bins_ref, wave_ref, total_ref, rim_squares_ref, rec_ref, extra_ref,
    cross_ref, cross_extra_ref, accept_ref, new_ref, log_ref,
    prev_ref, prev_power_ref, stage_ref, values_ref, edge_ref, rim_ref,
):
    walkers, own = weighted_ref.shape
    slots = wave_ref.shape[0]
    band_bins = own // 2
    last = blocks - 1
    span = cross_ref.shape[1]
    sources, extra = extra_ref.shape
    place = lax.axis_index("shard")
    first, final = place == 0, place == sources - 1

    below_rec = jnp.where(first, cross_ref[...], rec_ref[:, :span])
    above_rec = jnp.where(final, cross_ref[...], rec_ref[:, span:])
    source = lax.rem(place + 1, sources)
    rows = -(-3 * LANES // cross_extra_ref.shape[1])
    crossed = jnp.concatenate([cross_extra_ref[i : i + 1, :] for i in range(rows)], axis=1)
    above = jnp.where(final, crossed[:, : 3 * LANES], extra_ref[pl.ds(source, 1), : 3 * LANES])
    source = lax.rem(place + sources - 1, sources)
    below = extra_ref[pl.ds(source, 1), :]
    rows = -(-below.shape[1] // cross_extra_ref.shape[1])
    crossed = jnp.concatenate([cross_extra_ref[i : i + 1, :] for i in range(rows)], axis=1)
    below = jnp.where(first, crossed[:, : below.shape[1]], below)

    bins = jnp.concatenate(
        [below[:, 3 * LANES + i * slots : 3 * LANES + (i + 1) * slots] for i in range(5)] + [jnp.zeros((3, slots), F32)],
        axis=0,
    )
    passes = (bins[4:5] > np.float32(band_bins - Q)) & (bins[0:1] != 0.0)
    flags = jnp.broadcast_to(jnp.where(passes, 1.0, 0.0), (2 * SUB, slots)).astype(BF16)
    row, column = (lax.broadcasted_iota(jnp.int32, (LANES, LANES), i) for i in range(2))
    upto = jnp.where(row <= column, 1.0, 0.0).astype(BF16)
    ranks = []
    for start in range(0, slots, LANES):
        rank = jnp.dot(flags[:, start : start + LANES], upto, preferred_element_type=F32)[0:1]
        ranks.append(rank + ranks[-1][:, LANES - 1 :] if ranks else rank)
    passing = jnp.max(ranks[-1]).astype(jnp.int32)
    rank = jnp.where(passes, jnp.concatenate(ranks, axis=1), 0.0)
    bin_pieces = jnp.concatenate(pieces(bins), axis=0).astype(BF16)

    below_noise, above_noise = below[:, 2 * LANES : 3 * LANES], above[:, 2 * LANES : 3 * LANES]
    group = 2 * SUB
    lane = lane_iota(group).astype(F32)
    first_noise = noise_ref[0:1, :LANES]
    chunk = prev_ref.shape[0]
    tail = []

    def chosen_slots(index):
        place = lax.broadcasted_iota(jnp.int32, (chunk, slots), 0) + (index * chunk + 1)
        chosen = jnp.where(rank == place.astype(F32), 1.0, 0.0).astype(BF16)
        cols = lax.dot_general(chosen, bin_pieces, OVER_LANES, preferred_element_type=F32)
        return cols[:, :SUB] + cols[:, SUB : 2 * SUB] + cols[:, 2 * SUB : 3 * SUB]

    def fill(cols, start):
        at = slice(start, start + group)
        re, im, wrapped, _ = slot_wave(cols[at, :], lane)
        re, im = re.astype(BF16).astype(F32), im.astype(BF16).astype(F32)
        power = (re * re + im * im) * jnp.where(wrapped, first_noise, below_noise)
        for i, piece in enumerate(pieces(power)):
            prev_power_ref[at, i * LANES : (i + 1) * LANES] = piece.astype(BF16)
        prev_ref[at, :LANES] = jnp.where(wrapped, 0.0, re).astype(BF16)
        prev_ref[at, LANES : 2 * LANES] = jnp.where(wrapped, 0.0, im).astype(BF16)
        prev_ref[at, 2 * LANES : 3 * LANES] = jnp.where(wrapped, re, 0.0).astype(BF16)
        prev_ref[at, 3 * LANES :] = jnp.where(wrapped, im, 0.0).astype(BF16)

    def spilled():
        corr = lax.dot_general(tail[0], prev_ref[...], OVER_LANES, preferred_element_type=F32)
        ones = jnp.ones((2 * SUB, prev_power_ref.shape[1]), BF16)
        total = lax.dot_general(ones, prev_power_ref[...], OVER_LANES, preferred_element_type=F32)
        half = accepted(corr, total[0:1, :]).astype(BF16)
        return jnp.dot(half, prev_ref[:, 2 * LANES :], preferred_element_type=F32)

    def spill(index, carried):
        cols = chosen_slots(index)
        for start in range(0, chunk, group):
            fill(cols, start)
        return carried + spilled()

    quantities = []
    for k, rec in ((last, below_rec), (0, above_rec)):
        amps, linear, reduced = coefficients(rec, harmonics * 2 * SUB, band_bins)
        quantities += [phase_terms(k, band_bins, linear, reduced), amp_terms(k, band_bins, amps)]
    evaluate = evaluator(quantities, stage_ref, values_ref)

    step = own // (walkers // SUB)
    corr = [jnp.zeros((walkers, slots), F32)]

    cols = chosen_slots(0)
    fills = list(range(0, chunk, group))

    def edge_block(q):
        lanes = slice(q * step, (q + 1) * step)
        corr[0] += lax.dot_general(weighted_ref[:, lanes], wave_ref[:, lanes], OVER_LANES, preferred_element_type=F32)
        halves = []
        for s in range(2):
            total = None
            for h in range(harmonics):
                at = pl.ds(q * LANES + (2 * h + s) * SUB, SUB)
                terms = []
                for i in range(2):
                    phase, a = (values_ref[at, (2 * i + j) * LANES : (2 * i + j + 1) * LANES] for j in range(2))
                    terms += [a * x for x in cis_turns(frac(phase))]
                total = terms if h == 0 else [x + y for x, y in zip(total, terms, strict=True)]
            halves.append(total)
        for i, template in enumerate(summed(halves)):
            part = (below, above)[i // 2][:, i % 2 * LANES : (i % 2 + 1) * LANES]
            edge_ref[q * SUB : (q + 1) * SUB, i * LANES : (i + 1) * LANES] = part - template
        for start in fills[q :: walkers // SUB]:
            fill(cols, start)

    by_walkers(walkers // SUB, evaluate, edge_block)
    noise = jnp.concatenate([below_noise, below_noise, above_noise, above_noise], axis=1)
    rim_ref[...] = (edge_ref[...] * noise).astype(BF16)
    mine = jnp.concatenate([weighted_ref[:, :LANES], weighted_ref[:, band_bins : band_bins + LANES]], axis=1)
    tail.append(jnp.concatenate([rim_ref[:, : 2 * LANES], mine], axis=1))

    corr = corr[0] + lax.dot_general(rim_ref[:, 2 * LANES :], wave_ref[:, own:], OVER_LANES, preferred_element_type=F32)
    noise = jnp.broadcast_to(jnp.concatenate([above_noise] * 3, axis=1), (2 * SUB, 3 * LANES)).astype(BF16)
    total = lax.dot_general(noise, rim_squares_ref[...], OVER_LANES, preferred_element_type=F32)
    accept = accepted(corr, total_ref[0:1, :] + total[0:1, :])
    accept = jnp.where(bins_ref[5:6, :] > 0.0, accept, 0.0)
    accept_ref[...] = accept
    half = accept.astype(BF16)

    squares = [jnp.zeros((walkers, LANES), F32)]
    width = 2 * LANES

    def update(start, carried=None):
        lanes = slice(start, start + width)
        new = resid_ref[:, lanes] - jnp.dot(half, wave_ref[:, lanes], preferred_element_type=F32)
        parts = [new[:, i : i + LANES] for i in range(0, width, LANES)]
        if carried is not None:
            part = start // band_bins
            parts[0] -= carried[:, part * LANES : (part + 1) * LANES]
        for i, piece in enumerate(parts):
            new_ref[:, start + i * LANES : start + (i + 1) * LANES] = piece
            squares[0] += piece * piece

    carried = spilled()
    for start in range(0, own, width):
        if start % band_bins:
            update(start)
    carried = lax.fori_loop(1, (passing + chunk - 1) // chunk, spill, carried)
    update(0, carried)
    update(band_bins, carried)
    squares = squares[0]
    total = jnp.sum(jnp.sum(squares, axis=0, keepdims=True), axis=1, keepdims=True)
    log_power = jnp.log(total * np.float32(1.0 / (walkers * own)) + np.float32(1e-6))
    log_ref[:, 0, :] = jnp.broadcast_to(log_power, (log_ref.shape[0], log_ref.shape[2]))


def output_kernel(bands, accept_ref, new_ref, prob_ref, out_ref, fit_ref):
    _, own = new_ref.shape
    half = own // 2
    prob_ref[...] = accept_ref[...]
    for part in range(2):
        out_ref[:, part, :] = new_ref[:, part * half : (part + 1) * half]
    fit = fit_rows(lax.axis_index(BOTH), bands)
    fit = jnp.broadcast_to(fit, (SUB, fit.shape[1])).T
    fit_ref[...] = jnp.broadcast_to(fit[:bands, 0:1], (bands, LANES))


def call(kernel, outs, args, scratch=(), smem=0, flops=0, name=None, hbm=False, unread=0, alias=None):
    vmem = pl.BlockSpec(memory_space=pltpu.VMEM)
    rest = vmem
    if hbm:
        rest = pl.BlockSpec(memory_space=pl.ANY)
        args = [pltpu.with_memory_space_constraint(x, pltpu.HBM) if x.dtype != jnp.int32 or x.ndim > 1 else x for x in args]
    specs = [pl.BlockSpec(memory_space=pltpu.SMEM)] * smem + [rest] * (len(args) - smem)
    if unread:
        specs[-unread:] = [pl.BlockSpec(memory_space=pl.ANY)] * unread
    return pl.pallas_call(
        kernel,
        out_shape=outs,
        in_specs=specs,
        out_specs=[vmem] * len(outs),
        scratch_shapes=scratch,
        compiler_params=pltpu.CompilerParams(vmem_limit_bytes=16 * 2**20),
        cost_estimate=pl.CostEstimate(flops=flops, bytes_accessed=2**20, transcendentals=0),
        name=name,
        input_output_aliases=alias or {},
    )(*args)


def shape(dims, dtype):
    return jax.ShapeDtypeStruct(dims, dtype)


def local(
    data,
    inv_noise,
    mbh_amp,
    mbh_phase,
    bin_amp,
    bin_phase,
    bin_slope,
    bin_curve,
    bin_start,
    bin_count,
):
    band_bins = data.shape[1]
    slots = bin_amp.shape[1]
    rows, harmonics, powers, peers = mbh_amp.shape
    groups = lax.axis_size("group")
    walkers = rows * peers // 2
    bands = lax.axis_size(BOTH)
    own = 2 * band_bins

    span = padded(2 * powers * harmonics * rows)
    extra = 3 * LANES + 5 * slots
    cross_rows = -(-extra // span // SUB) * SUB
    packed, bins, data, noise, own_rows = call(
        pack_kernel,
        [
            shape((peers, 1, 3 * span + extra), F32),
            shape((SUB, slots), F32),
            shape((2, band_bins), F32),
            shape((1, band_bins), F32),
            shape((peers, span), F32),
        ],
        [
            mbh_amp.transpose(1, 2, 3, 0), mbh_phase.transpose(1, 2, 3, 0), data, inv_noise.reshape(-1, LANES),
            bin_amp, bin_phase, bin_slope, bin_curve, bin_start, bin_count,
        ],
        scratch=[
            pltpu.VMEM((harmonics, powers, peers, rows), F32),
            pltpu.VMEM((harmonics, powers, peers, rows), F32),
            pltpu.VMEM((4, 1, slots), F32),
            pltpu.VMEM((1, slots), jnp.int32),
            pltpu.VMEM((band_bins // LANES, LANES), BF16),
            pltpu.SMEM((1,), jnp.int32),
            pltpu.SemaphoreType.DMA((10,)),
        ],
        hbm=True,
        name="pack",
    )
    received = lax.all_to_all(packed, "shard", split_axis=0, concat_axis=0, tiled=True)
    received = received.reshape(peers, -1)
    wave, slot_power, rim_squares = call(
        wave_kernel,
        [shape((slots, own + 2 * LANES), BF16), shape((SUB, slots), F32), shape((slots, 3 * LANES), BF16)],
        [bins, noise],
        scratch=[pltpu.VMEM((slots, LANES), F32), pltpu.VMEM((slots, LANES), F32)],
        flops=10**9,
        name="waves",
    )
    direct = rows == 2 * SUB
    before = [slot_power]
    scratch = [pltpu.VMEM((stage_rows(45), walkers // SUB, LANES), F32), pltpu.VMEM((walkers // SUB * LANES, 7 * LANES), F32)]
    if direct:
        (own_resid,) = call(
            functools.partial(own_kernel, harmonics),
            [shape((SUB, own), F32)],
            [own_rows, data],
            scratch=[pltpu.VMEM((stage_rows(45), 1, LANES), F32), pltpu.VMEM((LANES, 7 * LANES), F32)],
            flops=10**9,
            name="own_template",
        )
        before.append(own_resid)
    (to_cross,) = call(
        cross_kernel,
        [shape((peers + cross_rows, span), F32)],
        [received, *before],
        unread=len(before),
        name="cross",
    )
    pairs = [(g * peers, (g + 1) * peers) for g in range(groups - 1)]
    pairs += [(g * peers + peers - 1, (g - 1) * peers + peers - 1) for g in range(1, groups)]
    crossed = lax.ppermute(to_cross, BOTH, pairs)

    extras = received[:, 3 * span :]
    parts = [received[:, i * span : (i + 1) * span] for i in range(3)] + [crossed[:peers]]
    crossed_extra = crossed[peers:]
    if not direct:

        def by_eight(x):
            x = x[:, : 2 * powers * harmonics * rows].reshape(peers, 2 * powers, harmonics, rows)
            x = x.transpose(1, 2, 0, 3).reshape(2 * powers, harmonics, walkers // SUB, SUB, 2)
            x = x.transpose(2, 0, 1, 4, 3).reshape(walkers // SUB, 2 * powers * harmonics * 2 * SUB)
            return jnp.pad(x, ((0, 0), (0, padded(x.shape[1]) - x.shape[1])))

        parts = [by_eight(x) for x in parts]

    resid, weighted = call(
        functools.partial(template_kernel, harmonics, direct),
        [shape((walkers, own), F32), shape((walkers, own), BF16)],
        [parts[0], data, noise, *before[1:]],
        scratch=scratch,
        flops=10**9,
        name="template",
    )
    accept, updated, log_power = call(
        functools.partial(score_kernel, harmonics, band_bins // LANES),
        [shape((walkers, slots), F32), shape((walkers, own), F32), shape((bands, 1, LANES), F32)],
        [
            weighted, resid, noise, bins, wave, slot_power, rim_squares, jnp.concatenate(parts[1:3], axis=1), extras,
            parts[3], crossed_extra,
        ],
        scratch=[
            pltpu.VMEM((min(slots, 6 * 2 * SUB), 4 * LANES), BF16),
            pltpu.VMEM((min(slots, 6 * 2 * SUB), 3 * LANES), BF16),
            pltpu.VMEM((stage_rows(48), walkers // SUB, LANES), F32),
            pltpu.VMEM((walkers // SUB * LANES, 4 * LANES), F32),
            pltpu.VMEM((walkers, 4 * LANES), F32),
            pltpu.VMEM((walkers, 4 * LANES), BF16),
        ],
        name="scores",
    )
    log_powers = lax.all_to_all(log_power, BOTH, split_axis=0, concat_axis=0, tiled=True)
    accept_prob, residual_new, fit = call(
        functools.partial(output_kernel, bands),
        [shape((walkers, slots), F32), shape((walkers, 2, band_bins), F32), shape((bands, LANES), F32)],
        [accept, updated],
        name="outputs",
    )
    noise_fit = jnp.sum(fit * log_powers[:, 0, :], axis=0)[:1]
    return (accept_prob, residual_new, noise_fit)


def solution(mesh):
    in_specs = (
        P(None, BOTH),
        P(BOTH),
        P("shard", None, None, "group"),
        P("shard", None, None, "group"),
        P(BOTH, None),
        P(BOTH, None),
        P(BOTH, None),
        P(BOTH, None),
        P(BOTH, None),
        P(BOTH),
    )
    out_specs = (P(None, BOTH), P(None, None, BOTH), P(BOTH))
    return jax.shard_map(local, mesh=mesh, in_specs=in_specs, out_specs=out_specs, check_vma=False)
```
